32 devices in a mesh: sample: 4 (over z), mp: 8 (over y, x, core).
Axes of the slice: x: 2, y: 2, z: 4, core: 2. Of those that a mesh axis runs over, the one named last changes fastest.
Arguments:
- volumes: bfloat16 [64, 4, 2048], P('mp', 'sample'), may hold values from -6 to 6
- w_first: bfloat16 [128, 1728], P('mp'), may hold values from -0.15625 to 0.15625
- w_second: bfloat16 [256, 3456], P('mp'), may hold values from -0.109375 to 0.109375
- cotangent: bfloat16 [256, 4, 2048], P('mp', 'sample'), may hold values from -6 to 6
Outputs:
- features: bfloat16 [256, 4, 2048], P('mp', 'sample')
- input_grad: bfloat16 [64, 4, 2048], P('mp', 'sample')
- grad_first: float32 [128, 1728], P('mp')
- grad_second: float32 [256, 3456], P('mp')
The draws below stay inside these ranges and needn't reach their ends.
All inputs are finite; a program needn't handle non-finite values.
Results may differ from the reference program's by a relative error of at most 0.024.
Values may be sent and summed in bfloat16 or wider, within the bound.
No kernel may reach another device: no remote copies, remote signals or barrier semaphores. Data moves between devices by JAX's collectives and lax.ppermute only.
A program may use at most 64 MiB of HBM per device.

```python
import math
import jax
import jax.numpy as jnp
from jax import lax

C0 = 64
C1 = 128
C2 = 256
SIDE = 16
DEPTH = 8
CELLS = 2048
BATCH = 4


def steps_of(own_key, extent, split, low, high):
    factor_of = 1.0
    for axis_at, shards_of in split:
        draws = jax.random.uniform(jax.random.fold_in(jax.random.fold_in(own_key, 6), axis_at), (shards_of,), jnp.float32, low / len(split), high / len(split))
        factor_of = factor_of * jnp.repeat(jnp.exp(draws), extent[axis_at] // shards_of).reshape((-1,) + (1,) * (len(extent) - 1 - axis_at))
    return factor_of


def centred(rng, dims, width, most, shards=(), kind=jnp.bfloat16):
    values = width * jax.random.normal(rng, dims, jnp.float32)
    if shards:
        values = values * steps_of(rng, dims, shards, -0.22, 0.18)
    return jnp.clip(values, -most, most).astype(kind)


def setup_inputs(seed: int = 0) -> dict:
    arg_keys = jax.random.split(jax.random.key(seed), 5)
    return {
        "volumes": centred(arg_keys[0], (C0, BATCH, CELLS), 1.0, 6.0, ((0, 8), (1, 4))),
        "w_first": centred(arg_keys[1], (C1, 27 * C0), (27 * C0) ** -0.5, 0.15625, ((0, 8),)),
        "w_second": centred(arg_keys[2], (C2, 27 * C1), (27 * C1) ** -0.5, 0.109375, ((0, 8),)),
        "cotangent": centred(arg_keys[3], (C2, BATCH, CELLS), 1.0, 6.0, ((0, 8), (1, 4))),
    }


def to_grid(array_in):
    return array_in.reshape(array_in.shape[0], array_in.shape[1], DEPTH, SIDE, SIDE)

def conv_forward(inputs, weights):
    filters = weights.shape[0]
    kernel = weights.astype(jnp.float32).reshape(filters, 3, 3, 3, inputs.shape[0])
    output = lax.conv_general_dilated(to_grid(inputs.astype(jnp.float32)), kernel, (1, 1, 1), ((1, 1), (1, 1), (1, 1)), dimension_numbers=('CNDHW', 'ODHWI', 'CNDHW'), precision=lax.Precision.HIGHEST)
    return output.reshape(filters, inputs.shape[1], -1)

def conv_data(deltas, weights, channels):
    kernel = weights.astype(jnp.float32).reshape(weights.shape[0], 3, 3, 3, channels)[:, ::-1, ::-1, ::-1, :]
    output = lax.conv_general_dilated(to_grid(deltas.astype(jnp.float32)), kernel, (1, 1, 1), ((1, 1), (1, 1), (1, 1)), dimension_numbers=('CNDHW', 'IDHWO', 'CNDHW'), precision=lax.Precision.HIGHEST)
    return output.reshape(channels, deltas.shape[1], -1)

def conv_weight(inputs, deltas):
    output = lax.conv_general_dilated(to_grid(inputs.astype(jnp.float32)), to_grid(deltas.astype(jnp.float32)), (1, 1, 1), ((1, 1), (1, 1), (1, 1)), dimension_numbers=('NCDHW', 'OIDHW', 'NCDHW'), precision=lax.Precision.HIGHEST)
    return jnp.transpose(output, (1, 2, 3, 4, 0)).reshape(deltas.shape[0], -1)

def silu_slope(values):
    sigmoid_v = jax.nn.sigmoid(values)
    return sigmoid_v * (1.0 + values * (1.0 - sigmoid_v))

def reference(volumes, w_first, w_second, cotangent):
    pre_first = conv_forward(volumes, w_first)
    hidden = jax.nn.silu(pre_first).astype(jnp.bfloat16)
    pre_second = conv_forward(hidden, w_second)
    features = jax.nn.silu(pre_second).astype(jnp.bfloat16)
    delta_second = (cotangent.astype(jnp.float32) * silu_slope(pre_second)).astype(jnp.bfloat16)
    grad_hidden = conv_data(delta_second, w_second, hidden.shape[0])
    delta_first = (grad_hidden * silu_slope(pre_first)).astype(jnp.bfloat16)
    input_grad = conv_data(delta_first, w_first, volumes.shape[0]).astype(jnp.bfloat16)
    grad_scale = 1.0 / math.sqrt(volumes.shape[1] * volumes.shape[2])
    grad_second = conv_weight(hidden, delta_second) * grad_scale
    grad_first = conv_weight(volumes, delta_first) * grad_scale
    return (features, input_grad, grad_first, grad_second)
```

```python
import functools
import math

import jax
import jax.numpy as jnp
from jax import lax
from jax.experimental import pallas as pl
from jax.experimental.pallas import tpu as pltpu
from jax.sharding import PartitionSpec as P

SIDE = 16
PLANE = SIDE * SIDE
F32 = jnp.float32
BF16 = jnp.bfloat16
VMEM_LIMIT = 48 * 1024 * 1024


def pitch_of(channels):
    width = 3 * channels
    slack = max((i * width) % 128 for i in range(9))
    return -(-(width + slack) // 128) * 128


def lane_grid(width):
    lane = lax.broadcasted_iota(jnp.int32, (1, width), 1)
    return lane % SIDE, (lane // SIDE) % SIDE


def inside(grid_xy, dy, dx):
    x, y = grid_xy
    ok = None
    for coord, step in ((y, dy), (x, dx)):
        if step < 0:
            now = coord >= -step
        elif step > 0:
            now = coord < SIDE - step
        else:
            continue
        ok = now if ok is None else ok & now
    return ok


def moved(values, grid_xy, dy, dx):
    if dy == 0 and dx == 0:
        return values
    width = values.shape[1]
    rolled = pltpu.roll(values, (-(dy * SIDE + dx)) % width, 1)
    return jnp.where(inside(grid_xy, dy, dx), rolled, 0.0)


def sigmoid(v):
    return 1.0 / (1.0 + jnp.exp(-v))


def dot(a, b):
    return lax.dot_general(a, b, (((1,), (0,)), ((), ())), preferred_element_type=F32)


def dot_nt(a, b):
    return lax.dot_general(a, b, (((1,), (1,)), ((), ())), preferred_element_type=F32)


def chunk_of(cells):
    return 2 * PLANE if cells % (2 * PLANE) == 0 else PLANE


def forward_kernel(n_mp, n_sample, c0, *refs):
    pieces = refs[:n_mp]
    w2r_ref, w2b_ref, cot_ref = refs[n_mp : n_mp + 3]
    outs = refs[n_mp + 3 :]
    feat_ref, pre_ref, vol_ref = outs[:3]
    part_refs = outs[3 : 3 + n_mp]
    grad_refs = outs[3 + n_mp : 3 + n_mp + n_sample]
    vs, w1s, v3, w1r, hid, pre, d9, part, grad = outs[3 + n_mp + n_sample :]

    me = lax.axis_index("mp")
    at = lax.axis_index("sample")
    f1 = w1s.shape[1]
    c1 = n_mp * f1
    f2, cells = cot_ref.shape
    chunk = chunk_of(cells)
    steps = cells // chunk
    pitch = pitch_of(c0)
    grid_xy = lane_grid(chunk)

    for k in range(n_mp):
        piece = pieces[k][...].astype(F32)
        slot = me ^ k
        w1s[slot] = piece[:f1]
        vs[slot] = piece[f1:, :cells]

    lane = lax.broadcasted_iota(jnp.int32, (1, pitch), 1)
    for dz in range(3):
        for dy in range(3):
            start = (dz * 3 + dy) * 3 * c0
            low = start // 128 * 128
            block = w1s[:, :, low : low + pitch].reshape(c1, pitch)
            if start != low:
                block = pltpu.roll(block, pitch - (start - low), 1)
            block = jnp.where(lane < 3 * c0, block, 0.0)
            w1r[dy * c1 : (dy + 1) * c1, dz * pitch : (dz + 1) * pitch] = block.astype(BF16)

    for ref in (v3, hid, d9):
        zero = jnp.zeros((ref.shape[0], PLANE), BF16)
        ref[:, :PLANE] = zero
        ref[:, PLANE + cells :] = zero
    v3[3 * c0 :, PLANE : PLANE + cells] = jnp.zeros((pitch - 3 * c0, cells), BF16)

    def take_volumes(step, carry):
        base = pl.multiple_of(step * chunk, chunk)
        values = vs[:, :, pl.ds(base, chunk)].reshape(c0, chunk)
        vol_ref[:, pl.ds(base, chunk)] = values.astype(BF16)
        for dx in range(3):
            v3[dx * c0 : (dx + 1) * c0, pl.ds(base + PLANE, chunk)] = moved(values, grid_xy, 0, dx - 1).astype(BF16)
        return carry

    lax.fori_loop(0, steps, take_volumes, 0)

    def first_conv(step, carry):
        base = pl.multiple_of(step * chunk, chunk)
        rhs = jnp.concatenate([v3[:, pl.ds(base + dz * PLANE, chunk)] for dz in range(3)], axis=0)
        z = dot(w1r[...], rhs)
        total = z[c1 : 2 * c1]
        total = total + moved(z[:c1], grid_xy, -1, 0)
        total = total + moved(z[2 * c1 :], grid_xy, 1, 0)
        pre[:, pl.ds(base, chunk)] = total
        hid[:, pl.ds(base + PLANE, chunk)] = (total * sigmoid(total)).astype(BF16)
        return carry

    lax.fori_loop(0, steps, first_conv, 0)
    pre_ref[...] = pre[pl.ds(pl.multiple_of(me * f1, f1), f1), :]

    def second_conv(step, carry):
        base = pl.multiple_of(step * chunk, chunk)
        rhs = jnp.concatenate([hid[:, pl.ds(base + dz * PLANE, chunk)] for dz in range(3)], axis=0)
        z = dot(w2r_ref[...], rhs)
        total = None
        for dy in range(3):
            for dx in range(3):
                k = dy * 3 + dx
                term = moved(z[k * f2 : (k + 1) * f2], grid_xy, dy - 1, dx - 1)
                total = term if total is None else total + term
        s = sigmoid(total)
        feat_ref[:, pl.ds(base, chunk)] = (total * s).astype(BF16)
        cot = cot_ref[:, pl.ds(base, chunk)].astype(F32)
        delta = (cot * (s * (1.0 + total * (1.0 - s)))).astype(BF16).astype(F32)
        for dy in range(3):
            for dx in range(3):
                k = dy * 3 + dx
                d9[k * f2 : (k + 1) * f2, pl.ds(base + PLANE, chunk)] = moved(delta, grid_xy, 1 - dy, 1 - dx).astype(BF16)
        return carry

    lax.fori_loop(0, steps, second_conv, 0)

    def data_conv(step, carry):
        base = pl.multiple_of(step * chunk, chunk)
        rhs = jnp.concatenate([d9[:, pl.ds(base + (2 - dz) * PLANE, chunk)] for dz in range(3)], axis=0)
        z = dot(w2b_ref[...], rhs)
        part[:, :, pl.ds(base, chunk)] = z.reshape(n_mp, f1, chunk)
        return carry

    lax.fori_loop(0, steps, data_conv, 0)
    for k in range(n_mp):
        part_refs[k][...] = part[me ^ k].astype(BF16)

    rows = f2 // n_sample
    for dz in range(3):
        g = dot_nt(d9[:, (2 - dz) * PLANE : (2 - dz) * PLANE + cells], hid[:, PLANE : PLANE + cells])
        for k in range(9):
            t = dz * 9 + k
            grad[:, :, t * c1 : (t + 1) * c1] = g[k * f2 : (k + 1) * f2].reshape(n_sample, rows, c1)
    for k in range(n_sample):
        grad_refs[k][...] = grad[at ^ k].astype(BF16)


def backward_kernel(n_mp, *refs):
    parts = refs[:n_mp]
    pre_ref, vol_ref, w1b_ref = refs[n_mp : n_mp + 3]
    out_refs = refs[n_mp + 3 : 2 * n_mp + 3]
    grad_ref, d9, part = refs[2 * n_mp + 3 :]
    me = lax.axis_index("mp")
    f1, cells = pre_ref.shape
    c0 = vol_ref.shape[0]
    chunk = chunk_of(cells)
    steps = cells // chunk
    grid_xy = lane_grid(chunk)

    zero = jnp.zeros((d9.shape[0], PLANE), BF16)
    d9[:, :PLANE] = zero
    d9[:, PLANE + cells :] = zero

    def take(step, carry):
        base = pl.multiple_of(step * chunk, chunk)
        total = parts[0][:, pl.ds(base, chunk)].astype(F32)
        for k in range(1, n_mp):
            total = total + parts[k][:, pl.ds(base, chunk)].astype(F32)
        v = pre_ref[:, pl.ds(base, chunk)]
        s = sigmoid(v)
        delta = (total * (s * (1.0 + v * (1.0 - s)))).astype(BF16).astype(F32)
        shifts = [moved(delta, grid_xy, 1 - dy, 1 - dx) for dy in range(3) for dx in range(3)]
        d9[:, pl.ds(base + PLANE, chunk)] = jnp.concatenate(shifts, axis=0).astype(BF16)
        return carry

    lax.fori_loop(0, steps, take, 0)

    def data_conv(step, carry):
        base = pl.multiple_of(step * chunk, chunk)
        z = None
        for dz in range(3):
            term = dot(w1b_ref[dz], d9[:, pl.ds(base + (2 - dz) * PLANE, chunk)])
            z = term if z is None else z + term
        part[:, :, pl.ds(base, chunk)] = z.reshape(n_mp, c0 // n_mp, chunk)
        return carry

    lax.fori_loop(0, steps, data_conv, 0)
    for k in range(n_mp):
        out_refs[k][...] = part[me ^ k].astype(BF16)

    reps = max(1, 128 // c0)
    span = reps * c0
    vol = vol_ref[...]
    wide = jnp.concatenate([vol] * reps, axis=0) if reps > 1 else vol
    blocks = []
    for dz in range(3):
        g = dot_nt(d9[:, (2 - dz) * PLANE : (2 - dz) * PLANE + cells], wide)
        blocks += [g[k * f1 : (k + 1) * f1] for k in range(9)]
    lane = lax.broadcasted_iota(jnp.int32, (1, span), 1)
    for t in range(0, 27, reps):
        merged = blocks[t]
        for r in range(1, min(reps, 27 - t)):
            merged = jnp.where(lane >= r * c0, blocks[t + r], merged)
        width = min(span, (27 - t) * c0)
        grad_ref[:, t * c0 : t * c0 + width] = merged[:, :width].astype(BF16)


def place_kernel(n_sample, scale, *refs):
    out_ref = refs[n_sample]
    at = lax.axis_index("sample")
    for k in range(n_sample):
        out_ref[at ^ k] = refs[k][...].astype(F32) * scale


def swap(value, axis, k):
    n = lax.axis_size(axis)
    return lax.ppermute(value, axis, [(i, i ^ k) for i in range(n)])


def call(kernel, out_shape, scratch, flops, nbytes):
    return pl.pallas_call(
        kernel,
        out_shape=out_shape,
        scratch_shapes=scratch,
        compiler_params=pltpu.CompilerParams(vmem_limit_bytes=VMEM_LIMIT),
        cost_estimate=pl.CostEstimate(flops=flops, bytes_accessed=nbytes, transcendentals=0),
    )


def local(volumes, w_first, w_second, cotangent):
    n_mp = lax.axis_size("mp")
    n_sample = lax.axis_size("sample")
    rows_in, _, cells = volumes.shape
    f1 = w_first.shape[0]
    f2 = w_second.shape[0]
    c0 = w_first.shape[1] // 27
    c1 = w_second.shape[1] // 27
    pitch = pitch_of(c0)
    scale = 1.0 / math.sqrt(n_sample * volumes.shape[1] * cells)
    volumes = volumes.reshape(rows_in, cells)
    cotangent = cotangent.reshape(f2, cells)
    padded = cells + 2 * PLANE

    need = (8 * 3 * c0) // 128 * 128 + pitch
    wide = max(cells, need)
    piece = jnp.concatenate(
        [
            jnp.pad(w_first, ((0, 0), (0, wide - w_first.shape[1]))),
            jnp.pad(volumes, ((0, 0), (0, wide - cells))),
        ],
        axis=0,
    )
    pieces = [piece] + [swap(piece, "mp", k) for k in range(1, n_mp)]

    w2t = w_second.reshape(f2, 3, 9, c1)
    w2r = jnp.transpose(w2t, (2, 0, 1, 3)).reshape(9 * f2, 3 * c1)
    w2b = jnp.transpose(w2t, (3, 1, 2, 0)).reshape(c1, 27 * f2)
    w1b = jnp.transpose(w_first.reshape(f1, 3, 9, c0), (1, 3, 2, 0)).reshape(3, c0, 9 * f1)

    sds = jax.ShapeDtypeStruct
    outs = call(
        functools.partial(forward_kernel, n_mp, n_sample, c0),
        [sds((f2, cells), BF16), sds((f1, cells), F32), sds((c0, cells), BF16)]
        + [sds((f1, cells), BF16)] * n_mp
        + [sds((f2 // n_sample, 27 * c1), BF16)] * n_sample,
        [
            pltpu.VMEM((n_mp, rows_in, cells), F32),
            pltpu.VMEM((n_mp, f1, wide), F32),
            pltpu.VMEM((pitch, padded), BF16),
            pltpu.VMEM((3 * c1, 3 * pitch), BF16),
            pltpu.VMEM((c1, padded), BF16),
            pltpu.VMEM((c1, cells), F32),
            pltpu.VMEM((9 * f2, padded), BF16),
            pltpu.VMEM((n_mp, f1, cells), F32),
            pltpu.VMEM((n_sample, f2 // n_sample, 27 * c1), F32),
        ],
        2 * cells * 27 * (c0 * c1 + 3 * f2 * c1),
        4 * 1024 * 1024,
    )(*pieces, w2r, w2b, cotangent)
    features, pre_own, vol_all = outs[:3]
    parts = outs[3 : 3 + n_mp]
    grads = outs[3 + n_mp :]

    parts = [parts[0]] + [swap(parts[k], "mp", k) for k in range(1, n_mp)]
    grads = [grads[0]] + [swap(grads[k], "sample", k) for k in range(1, n_sample)]

    outs = call(
        functools.partial(backward_kernel, n_mp),
        [sds((rows_in, cells), BF16)] * n_mp + [sds((f1, 27 * c0), BF16)],
        [
            pltpu.VMEM((9 * f1, padded), BF16),
            pltpu.VMEM((n_mp, rows_in, cells), F32),
        ],
        2 * cells * 27 * 2 * c0 * f1,
        1024 * 1024,
    )(*parts, pre_own, vol_all, w1b)
    ins = outs[:n_mp]
    grad_first = outs[n_mp]
    firsts = [grad_first] + [swap(grad_first, "sample", k) for k in range(1, n_sample)]
    ins = [ins[0]] + [swap(ins[k], "mp", k) for k in range(1, n_mp)]

    def total(values):
        result = values[0].astype(F32)
        for value in values[1:]:
            result = result + value.astype(F32)
        return result

    second = total(grads).astype(BF16)
    seconds = [second] + [swap(second, "sample", k) for k in range(1, n_sample)]
    grad_second = call(
        functools.partial(place_kernel, n_sample, scale),
        sds((n_sample,) + second.shape, F32),
        [],
        0,
        1024 * 1024,
    )(*seconds).reshape(f2, 27 * c1)
    input_grad = total(ins).astype(BF16)
    return (
        features.reshape(f2, 1, cells),
        input_grad.reshape(rows_in, 1, cells),
        total(firsts) * scale,
        grad_second,
    )


def solution(mesh):
    return jax.shard_map(
        local,
        mesh=mesh,
        in_specs=(P("mp", "sample", None), P("mp", None), P("mp", None), P("mp", "sample", None)),
        out_specs=(P("mp", "sample", None), P("mp", "sample", None), P("mp", None), P("mp", None)),
        check_vma=False,
    )
```

```python
import functools
import math

import jax
import jax.numpy as jnp
from jax import lax
from jax.experimental import pallas as pl
from jax.experimental.pallas import tpu as pltpu
from jax.sharding import PartitionSpec as P

SIDE = 16
PLANE = SIDE * SIDE
F32 = jnp.float32
BF16 = jnp.bfloat16
VMEM_LIMIT = 48 * 1024 * 1024


def pitch_of(channels):
    width = 3 * channels
    slack = max((i * width) % 128 for i in range(9))
    return -(-(width + slack) // 128) * 128


def lane_grid(width):
    lane = lax.broadcasted_iota(jnp.int32, (1, width), 1)
    return lane % SIDE, (lane // SIDE) % SIDE


def inside(grid_xy, dy, dx):
    x, y = grid_xy
    ok = None
    for coord, step in ((y, dy), (x, dx)):
        if step < 0:
            now = coord >= -step
        elif step > 0:
            now = coord < SIDE - step
        else:
            continue
        ok = now if ok is None else ok & now
    return ok


def moved(values, grid_xy, dy, dx):
    if dy == 0 and dx == 0:
        return values
    width = values.shape[1]
    rolled = pltpu.roll(values, (-(dy * SIDE + dx)) % width, 1)
    return jnp.where(inside(grid_xy, dy, dx), rolled, 0.0)


def sigmoid(v):
    return 1.0 / (1.0 + jnp.exp(-v))


def dot(a, b):
    return lax.dot_general(a, b, (((1,), (0,)), ((), ())), preferred_element_type=F32)


def dot_nt(a, b):
    return lax.dot_general(a, b, (((1,), (1,)), ((), ())), preferred_element_type=F32)


def chunk_of(cells):
    return 2 * PLANE if cells % (2 * PLANE) == 0 else PLANE


def forward_kernel(n_mp, n_sample, c0, *refs):
    pieces, w2r_ref, w2b_ref, cot_ref, feat_ref, pre_ref, vol_ref, part_ref, grad_ref = refs[:9]
    vs, w1s, v3, w1r, hid, pre, d9 = refs[9:]

    me = lax.axis_index("mp")
    f1 = w1s.shape[1]
    c1 = n_mp * f1
    f2, cells = cot_ref.shape
    chunk = chunk_of(cells)
    steps = cells // chunk
    pitch = pitch_of(c0)
    grid_xy = lane_grid(chunk)

    for k in range(n_mp):
        piece = pieces[k].astype(F32)
        w1s[k] = piece[:f1]
        vs[k] = piece[f1:, :cells]

    lane = lax.broadcasted_iota(jnp.int32, (1, pitch), 1)
    for dz in range(3):
        for dy in range(3):
            start = (dz * 3 + dy) * 3 * c0
            low = start // 128 * 128
            block = w1s[:, :, low : low + pitch].reshape(c1, pitch)
            if start != low:
                block = pltpu.roll(block, pitch - (start - low), 1)
            block = jnp.where(lane < 3 * c0, block, 0.0)
            w1r[dy * c1 : (dy + 1) * c1, dz * pitch : (dz + 1) * pitch] = block.astype(BF16)

    for ref in (v3, hid, d9):
        zero = jnp.zeros((ref.shape[0], PLANE), BF16)
        ref[:, :PLANE] = zero
        ref[:, PLANE + cells :] = zero
    v3[3 * c0 :, PLANE : PLANE + cells] = jnp.zeros((pitch - 3 * c0, cells), BF16)

    def take_volumes(step, carry):
        base = pl.multiple_of(step * chunk, chunk)
        values = vs[:, :, pl.ds(base, chunk)].reshape(c0, chunk)
        vol_ref[:, pl.ds(base, chunk)] = values.astype(BF16)
        for dx in range(3):
            v3[dx * c0 : (dx + 1) * c0, pl.ds(base + PLANE, chunk)] = moved(values, grid_xy, 0, dx - 1).astype(BF16)
        return carry

    lax.fori_loop(0, steps, take_volumes, 0)

    def first_conv(step, carry):
        base = pl.multiple_of(step * chunk, chunk)
        rhs = jnp.concatenate([v3[:, pl.ds(base + dz * PLANE, chunk)] for dz in range(3)], axis=0)
        z = dot(w1r[...], rhs)
        total = z[c1 : 2 * c1]
        total = total + moved(z[:c1], grid_xy, -1, 0)
        total = total + moved(z[2 * c1 :], grid_xy, 1, 0)
        pre[:, pl.ds(base, chunk)] = total
        hid[:, pl.ds(base + PLANE, chunk)] = (total * sigmoid(total)).astype(BF16)
        return carry

    lax.fori_loop(0, steps, first_conv, 0)
    pre_ref[...] = pre[pl.ds(pl.multiple_of(me * f1, f1), f1), :]

    def second_conv(step, carry):
        base = pl.multiple_of(step * chunk, chunk)
        rhs = jnp.concatenate([hid[:, pl.ds(base + dz * PLANE, chunk)] for dz in range(3)], axis=0)
        z = dot(w2r_ref[...], rhs)
        total = None
        for dy in range(3):
            for dx in range(3):
                k = dy * 3 + dx
                term = moved(z[k * f2 : (k + 1) * f2], grid_xy, dy - 1, dx - 1)
                total = term if total is None else total + term
        s = sigmoid(total)
        feat_ref[:, pl.ds(base, chunk)] = (total * s).astype(BF16)
        cot = cot_ref[:, pl.ds(base, chunk)].astype(F32)
        delta = (cot * (s * (1.0 + total * (1.0 - s)))).astype(BF16).astype(F32)
        for dy in range(3):
            for dx in range(3):
                k = dy * 3 + dx
                d9[k * f2 : (k + 1) * f2, pl.ds(base + PLANE, chunk)] = moved(delta, grid_xy, 1 - dy, 1 - dx).astype(BF16)
        return carry

    lax.fori_loop(0, steps, second_conv, 0)

    def data_conv(step, carry):
        base = pl.multiple_of(step * chunk, chunk)
        rhs = jnp.concatenate([d9[:, pl.ds(base + (2 - dz) * PLANE, chunk)] for dz in range(3)], axis=0)
        z = dot(w2b_ref[...], rhs)
        part_ref[:, :, pl.ds(base, chunk)] = z.astype(BF16).reshape(n_mp, f1, chunk)
        return carry

    lax.fori_loop(0, steps, data_conv, 0)

    rows = f2 // n_sample
    for dz in range(3):
        g = dot_nt(d9[:, (2 - dz) * PLANE : (2 - dz) * PLANE + cells], hid[:, PLANE : PLANE + cells])
        for k in range(9):
            t = dz * 9 + k
            grad_ref[:, :, t * c1 : (t + 1) * c1] = g[k * f2 : (k + 1) * f2].reshape(n_sample, rows, c1).astype(BF16)


def backward_kernel(n_mp, *refs):
    parts, pre_ref, vol_ref, w1b_ref, out_ref, grad_ref, d9 = refs
    f1, cells = pre_ref.shape
    c0 = vol_ref.shape[0]
    chunk = chunk_of(cells)
    steps = cells // chunk
    grid_xy = lane_grid(chunk)

    zero = jnp.zeros((d9.shape[0], PLANE), BF16)
    d9[:, :PLANE] = zero
    d9[:, PLANE + cells :] = zero

    def take(step, carry):
        base = pl.multiple_of(step * chunk, chunk)
        total = parts[0, :, pl.ds(base, chunk)].astype(F32)
        for k in range(1, n_mp):
            total = total + parts[k, :, pl.ds(base, chunk)].astype(F32)
        v = pre_ref[:, pl.ds(base, chunk)]
        s = sigmoid(v)
        delta = (total * (s * (1.0 + v * (1.0 - s)))).astype(BF16).astype(F32)
        shifts = [moved(delta, grid_xy, 1 - dy, 1 - dx) for dy in range(3) for dx in range(3)]
        d9[:, pl.ds(base + PLANE, chunk)] = jnp.concatenate(shifts, axis=0).astype(BF16)
        return carry

    lax.fori_loop(0, steps, take, 0)

    def data_conv(step, carry):
        base = pl.multiple_of(step * chunk, chunk)
        z = None
        for dz in range(3):
            term = dot(w1b_ref[dz], d9[:, pl.ds(base + (2 - dz) * PLANE, chunk)])
            z = term if z is None else z + term
        out_ref[:, :, pl.ds(base, chunk)] = z.reshape(n_mp, c0 // n_mp, chunk).astype(BF16)
        return carry

    lax.fori_loop(0, steps, data_conv, 0)

    reps = max(1, 128 // c0)
    span = reps * c0
    vol = vol_ref[...]
    wide = jnp.concatenate([vol] * reps, axis=0) if reps > 1 else vol
    blocks = []
    for dz in range(3):
        g = dot_nt(d9[:, (2 - dz) * PLANE : (2 - dz) * PLANE + cells], wide)
        blocks += [g[k * f1 : (k + 1) * f1] for k in range(9)]
    lane = lax.broadcasted_iota(jnp.int32, (1, span), 1)
    for t in range(0, 27, reps):
        merged = blocks[t]
        for r in range(1, min(reps, 27 - t)):
            merged = jnp.where(lane >= r * c0, blocks[t + r], merged)
        width = min(span, (27 - t) * c0)
        grad_ref[:, t * c0 : t * c0 + width] = merged[:, :width].astype(BF16)


def call(kernel, out_shape, scratch, flops, nbytes):
    return pl.pallas_call(
        kernel,
        out_shape=out_shape,
        scratch_shapes=scratch,
        compiler_params=pltpu.CompilerParams(vmem_limit_bytes=VMEM_LIMIT),
        cost_estimate=pl.CostEstimate(flops=flops, bytes_accessed=nbytes, transcendentals=0),
    )


def local(volumes, w_first, w_second, cotangent):
    n_mp = lax.axis_size("mp")
    n_sample = lax.axis_size("sample")
    rows_in, _, cells = volumes.shape
    f1 = w_first.shape[0]
    f2 = w_second.shape[0]
    c0 = w_first.shape[1] // 27
    c1 = w_second.shape[1] // 27
    pitch = pitch_of(c0)
    scale = 1.0 / math.sqrt(n_sample * volumes.shape[1] * cells)
    volumes = volumes.reshape(rows_in, cells)
    cotangent = cotangent.reshape(f2, cells)
    padded = cells + 2 * PLANE

    need = (8 * 3 * c0) // 128 * 128 + pitch
    wide = max(cells, need)
    piece = jnp.concatenate(
        [
            jnp.pad(w_first, ((0, 0), (0, wide - w_first.shape[1]))),
            jnp.pad(volumes, ((0, 0), (0, wide - cells))),
        ],
        axis=0,
    )
    pieces = lax.all_gather(piece, "mp", axis=0, tiled=False)

    w2t = w_second.reshape(f2, 3, 9, c1)
    w2r = jnp.transpose(w2t, (2, 0, 1, 3)).reshape(9 * f2, 3 * c1)
    w2b = jnp.transpose(w2t, (3, 1, 2, 0)).reshape(c1, 27 * f2)
    w1b = jnp.transpose(w_first.reshape(f1, 3, 9, c0), (1, 3, 2, 0)).reshape(3, c0, 9 * f1)

    sds = jax.ShapeDtypeStruct
    features, pre_own, vol_all, parts, grads = call(
        functools.partial(forward_kernel, n_mp, n_sample, c0),
        [
            sds((f2, cells), BF16),
            sds((f1, cells), F32),
            sds((c0, cells), BF16),
            sds((n_mp, f1, cells), BF16),
            sds((n_sample, f2 // n_sample, 27 * c1), BF16),
        ],
        [
            pltpu.VMEM((n_mp, rows_in, cells), F32),
            pltpu.VMEM((n_mp, f1, wide), F32),
            pltpu.VMEM((pitch, padded), BF16),
            pltpu.VMEM((3 * c1, 3 * pitch), BF16),
            pltpu.VMEM((c1, padded), BF16),
            pltpu.VMEM((c1, cells), F32),
            pltpu.VMEM((9 * f2, padded), BF16),
        ],
        2 * cells * 27 * (c0 * c1 + 3 * f2 * c1),
        4 * 1024 * 1024,
    )(pieces, w2r, w2b, cotangent)

    parts = lax.all_to_all(parts, "mp", 0, 0, tiled=True)
    grads = lax.all_to_all(grads, "sample", 0, 0, tiled=True)

    ins, grad_first = call(
        functools.partial(backward_kernel, n_mp),
        [sds((n_mp, rows_in, cells), BF16), sds((f1, 27 * c0), BF16)],
        [pltpu.VMEM((9 * f1, padded), BF16)],
        2 * cells * 27 * 2 * c0 * f1,
        1024 * 1024,
    )(parts, pre_own, vol_all, w1b)
    ins = lax.all_to_all(ins, "mp", 0, 0, tiled=True)

    def total(values):
        result = values[0].astype(F32)
        for k in range(1, values.shape[0]):
            result = result + values[k].astype(F32)
        return result

    second = total(grads).astype(BF16).reshape(-1, 27 * c0)
    both = jnp.concatenate([grad_first, second], axis=0)
    both = lax.all_to_all(jnp.broadcast_to(both, (n_sample,) + both.shape), "sample", 0, 0, tiled=True)
    return (
        features.reshape(f2, 1, cells),
        total(ins).astype(BF16).reshape(rows_in, 1, cells),
        total(both[:, :f1]) * scale,
        both[:, f1:].astype(F32).reshape(f2, 27 * c1) * scale,
    )


def solution(mesh):
    return jax.shard_map(
        local,
        mesh=mesh,
        in_specs=(P("mp", "sample", None), P("mp", None), P("mp", None), P("mp", "sample", None)),
        out_specs=(P("mp", "sample", None), P("mp", "sample", None), P("mp", None), P("mp", None)),
        check_vma=False,
    )
```

```python
import functools
import math

import jax
import jax.numpy as jnp
from jax import lax
from jax.experimental import pallas as pl
from jax.experimental.pallas import tpu as pltpu
from jax.sharding import PartitionSpec as P

SIDE = 16
PLANE = SIDE * SIDE
F32 = jnp.float32
BF16 = jnp.bfloat16
VMEM_LIMIT = 48 * 1024 * 1024


def pitch_of(channels):
    width = 3 * channels
    slack = max((i * width) % 128 for i in range(9))
    return -(-(width + slack) // 128) * 128


def lane_grid(width):
    lane = lax.broadcasted_iota(jnp.int32, (1, width), 1)
    return lane % SIDE, (lane // SIDE) % SIDE


def inside(grid_xy, dy, dx):
    x, y = grid_xy
    ok = None
    for coord, step in ((y, dy), (x, dx)):
        if step < 0:
            now = coord >= -step
        elif step > 0:
            now = coord < SIDE - step
        else:
            continue
        ok = now if ok is None else ok & now
    return ok


def moved(values, grid_xy, dy, dx):
    if dy == 0 and dx == 0:
        return values
    width = values.shape[1]
    rolled = pltpu.roll(values, (-(dy * SIDE + dx)) % width, 1)
    return jnp.where(inside(grid_xy, dy, dx), rolled, 0.0)


def sigmoid(v):
    return 1.0 / (1.0 + jnp.exp(-v))


def dot(a, b):
    return lax.dot_general(a, b, (((1,), (0,)), ((), ())), preferred_element_type=F32)


def dot_nt(a, b):
    return lax.dot_general(a, b, (((1,), (1,)), ((), ())), preferred_element_type=F32)


def chunk_of(cells):
    return 2 * PLANE if cells % (2 * PLANE) == 0 else PLANE


def forward_kernel(n_mp, n_sample, c0, *refs):
    near_ref, far_ref, w2r_ref, w2b_ref, cot_ref = refs[:5]
    feat_ref, pre_ref, vol_ref, keep_ref, give_ref, half_keep_ref, half_give_ref = refs[5:12]
    vs, w1s, v3, w1r, hid, pre, d9, part, grad = refs[12:]

    me = lax.axis_index("mp")
    at = lax.axis_index("sample")
    f1 = w1s.shape[1]
    c1 = n_mp * f1
    f2, cells = cot_ref.shape
    chunk = chunk_of(cells)
    steps = cells // chunk
    pitch = pitch_of(c0)
    grid_xy = lane_grid(chunk)

    for k in range(n_mp):
        piece = (far_ref if k % 2 else near_ref)[k // 2].astype(F32)
        slot = me ^ k
        w1s[slot] = piece[:f1]
        vs[slot] = piece[f1:, :cells]

    lane = lax.broadcasted_iota(jnp.int32, (1, pitch), 1)
    for dz in range(3):
        for dy in range(3):
            start = (dz * 3 + dy) * 3 * c0
            low = start // 128 * 128
            block = w1s[:, :, low : low + pitch].reshape(c1, pitch)
            if start != low:
                block = pltpu.roll(block, pitch - (start - low), 1)
            block = jnp.where(lane < 3 * c0, block, 0.0)
            w1r[dy * c1 : (dy + 1) * c1, dz * pitch : (dz + 1) * pitch] = block.astype(BF16)

    for ref in (v3, hid, d9):
        zero = jnp.zeros((ref.shape[0], PLANE), BF16)
        ref[:, :PLANE] = zero
        ref[:, PLANE + cells :] = zero
    v3[3 * c0 :, PLANE : PLANE + cells] = jnp.zeros((pitch - 3 * c0, cells), BF16)

    def take_volumes(step, carry):
        base = pl.multiple_of(step * chunk, chunk)
        values = vs[:, :, pl.ds(base, chunk)].reshape(c0, chunk)
        vol_ref[:, pl.ds(base, chunk)] = values.astype(BF16)
        for dx in range(3):
            v3[dx * c0 : (dx + 1) * c0, pl.ds(base + PLANE, chunk)] = moved(values, grid_xy, 0, dx - 1).astype(BF16)
        return carry

    lax.fori_loop(0, steps, take_volumes, 0)

    def first_conv(step, carry):
        base = pl.multiple_of(step * chunk, chunk)
        rhs = jnp.concatenate([v3[:, pl.ds(base + dz * PLANE, chunk)] for dz in range(3)], axis=0)
        z = dot(w1r[...], rhs)
        total = z[c1 : 2 * c1]
        total = total + moved(z[:c1], grid_xy, -1, 0)
        total = total + moved(z[2 * c1 :], grid_xy, 1, 0)
        pre[:, pl.ds(base, chunk)] = total
        hid[:, pl.ds(base + PLANE, chunk)] = (total * sigmoid(total)).astype(BF16)
        return carry

    lax.fori_loop(0, steps, first_conv, 0)
    pre_ref[...] = pre[pl.ds(pl.multiple_of(me * f1, f1), f1), :]

    def second_conv(step, carry):
        base = pl.multiple_of(step * chunk, chunk)
        rhs = jnp.concatenate([hid[:, pl.ds(base + dz * PLANE, chunk)] for dz in range(3)], axis=0)
        z = dot(w2r_ref[...], rhs)
        total = None
        for dy in range(3):
            for dx in range(3):
                k = dy * 3 + dx
                term = moved(z[k * f2 : (k + 1) * f2], grid_xy, dy - 1, dx - 1)
                total = term if total is None else total + term
        s = sigmoid(total)
        feat_ref[:, pl.ds(base, chunk)] = (total * s).astype(BF16)
        cot = cot_ref[:, pl.ds(base, chunk)].astype(F32)
        delta = (cot * (s * (1.0 + total * (1.0 - s)))).astype(BF16).astype(F32)
        for dy in range(3):
            for dx in range(3):
                k = dy * 3 + dx
                d9[k * f2 : (k + 1) * f2, pl.ds(base + PLANE, chunk)] = moved(delta, grid_xy, 1 - dy, 1 - dx).astype(BF16)
        return carry

    lax.fori_loop(0, steps, second_conv, 0)

    def data_conv(step, carry):
        base = pl.multiple_of(step * chunk, chunk)
        rhs = jnp.concatenate([d9[:, pl.ds(base + (2 - dz) * PLANE, chunk)] for dz in range(3)], axis=0)
        z = dot(w2b_ref[...], rhs)
        part[:, :, pl.ds(base, chunk)] = z.reshape(n_mp, f1, chunk)
        return carry

    lax.fori_loop(0, steps, data_conv, 0)
    for k in range(n_mp):
        (give_ref if k % 2 else keep_ref)[k // 2] = part[me ^ k].astype(BF16)

    rows = f2 // 2
    for dz in range(3):
        g = dot_nt(d9[:, (2 - dz) * PLANE : (2 - dz) * PLANE + cells], hid[:, PLANE : PLANE + cells])
        for k in range(9):
            t = dz * 9 + k
            grad[:, :, t * c1 : (t + 1) * c1] = g[k * f2 : (k + 1) * f2].reshape(2, rows, c1)
    half_keep_ref[...] = grad[at % 2].astype(BF16)
    half_give_ref[...] = grad[1 - at % 2].astype(BF16)


def backward_kernel(n_mp, *refs):
    parts = refs[: n_mp // 2]
    pre_ref, vol_ref, w1b_ref, keep_ref, give_ref, grad_ref, d9, part = refs[n_mp // 2 :]
    me = lax.axis_index("mp")
    f1, cells = pre_ref.shape
    c0 = vol_ref.shape[0]
    chunk = chunk_of(cells)
    steps = cells // chunk
    grid_xy = lane_grid(chunk)

    zero = jnp.zeros((d9.shape[0], PLANE), BF16)
    d9[:, :PLANE] = zero
    d9[:, PLANE + cells :] = zero

    def take(step, carry):
        base = pl.multiple_of(step * chunk, chunk)
        total = parts[0][:, pl.ds(base, chunk)].astype(F32)
        for other in parts[1:]:
            total = total + other[:, pl.ds(base, chunk)].astype(F32)
        v = pre_ref[:, pl.ds(base, chunk)]
        s = sigmoid(v)
        delta = (total * (s * (1.0 + v * (1.0 - s)))).astype(BF16).astype(F32)
        shifts = [moved(delta, grid_xy, 1 - dy, 1 - dx) for dy in range(3) for dx in range(3)]
        d9[:, pl.ds(base + PLANE, chunk)] = jnp.concatenate(shifts, axis=0).astype(BF16)
        return carry

    lax.fori_loop(0, steps, take, 0)

    def data_conv(step, carry):
        base = pl.multiple_of(step * chunk, chunk)
        z = None
        for dz in range(3):
            term = dot(w1b_ref[dz], d9[:, pl.ds(base + (2 - dz) * PLANE, chunk)])
            z = term if z is None else z + term
        part[:, :, pl.ds(base, chunk)] = z.reshape(n_mp, c0 // n_mp, chunk)
        return carry

    lax.fori_loop(0, steps, data_conv, 0)
    for k in range(n_mp):
        (give_ref if k % 2 else keep_ref)[k // 2] = part[me ^ k].astype(BF16)

    reps = max(1, 128 // c0)
    span = reps * c0
    vol = vol_ref[...]
    wide = jnp.concatenate([vol] * reps, axis=0) if reps > 1 else vol
    blocks = []
    for dz in range(3):
        g = dot_nt(d9[:, (2 - dz) * PLANE : (2 - dz) * PLANE + cells], wide)
        blocks += [g[k * f1 : (k + 1) * f1] for k in range(9)]
    lane = lax.broadcasted_iota(jnp.int32, (1, span), 1)
    for t in range(0, 27, reps):
        merged = blocks[t]
        for r in range(1, min(reps, 27 - t)):
            merged = jnp.where(lane >= r * c0, blocks[t + r], merged)
        width = min(span, (27 - t) * c0)
        grad_ref[:, t * c0 : t * c0 + width] = merged[:, :width].astype(BF16)


def place_kernel(scale, mine_ref, other_ref, out_ref):
    bit = lax.axis_index("sample") % 2
    width = out_ref.shape[2]
    out_ref[bit] = mine_ref[...].astype(F32) * scale
    out_ref[1 - bit] = other_ref[:, :width].astype(F32) * scale


def swap(value, axis, k):
    n = lax.axis_size(axis)
    return lax.ppermute(value, axis, [(i, i ^ k) for i in range(n)])


def add(a, b):
    return (a.astype(F32) + b.astype(F32)).astype(BF16)


def sum_over_mp(keep, give):
    got = swap(give, "mp", 1)
    parts = [add(keep[j], got[j]) for j in range(keep.shape[0])]
    return [parts[0]] + [swap(parts[j], "mp", 2 * j) for j in range(1, len(parts))]


def bits_above(count):
    return [1 << i for i in range(1, count.bit_length() - 1)]


def call(kernel, out_shape, scratch, flops, nbytes):
    return pl.pallas_call(
        kernel,
        out_shape=out_shape,
        scratch_shapes=scratch,
        compiler_params=pltpu.CompilerParams(vmem_limit_bytes=VMEM_LIMIT),
        cost_estimate=pl.CostEstimate(flops=flops, bytes_accessed=nbytes, transcendentals=0),
    )


def local(volumes, w_first, w_second, cotangent):
    n_mp = lax.axis_size("mp")
    n_sample = lax.axis_size("sample")
    rows_in, _, cells = volumes.shape
    f1 = w_first.shape[0]
    f2 = w_second.shape[0]
    c0 = w_first.shape[1] // 27
    c1 = w_second.shape[1] // 27
    pitch = pitch_of(c0)
    scale = 1.0 / math.sqrt(n_sample * volumes.shape[1] * cells)
    volumes = volumes.reshape(rows_in, cells)
    cotangent = cotangent.reshape(f2, cells)
    padded = cells + 2 * PLANE

    need = (8 * 3 * c0) // 128 * 128 + pitch
    wide = max(cells, need)
    piece = jnp.concatenate(
        [
            jnp.pad(w_first, ((0, 0), (0, wide - w_first.shape[1]))),
            jnp.pad(volumes, ((0, 0), (0, wide - cells))),
        ],
        axis=0,
    )
    near = [piece] + [swap(piece, "mp", k) for k in range(2, n_mp, 2)]
    near = jnp.stack(near)
    far = swap(near, "mp", 1)

    w2t = w_second.reshape(f2, 3, 9, c1)
    w2r = jnp.transpose(w2t, (2, 0, 1, 3)).reshape(9 * f2, 3 * c1)
    w2b = jnp.transpose(w2t, (3, 1, 2, 0)).reshape(c1, 27 * f2)
    w1b = jnp.transpose(w_first.reshape(f1, 3, 9, c0), (1, 3, 2, 0)).reshape(3, c0, 9 * f1)

    sds = jax.ShapeDtypeStruct
    half = n_mp // 2
    features, pre_own, vol_all, keep, give, half_keep, half_give = call(
        functools.partial(forward_kernel, n_mp, n_sample, c0),
        [
            sds((f2, cells), BF16),
            sds((f1, cells), F32),
            sds((c0, cells), BF16),
            sds((half, f1, cells), BF16),
            sds((half, f1, cells), BF16),
            sds((f2 // 2, 27 * c1), BF16),
            sds((f2 // 2, 27 * c1), BF16),
        ],
        [
            pltpu.VMEM((n_mp, rows_in, cells), F32),
            pltpu.VMEM((n_mp, f1, wide), F32),
            pltpu.VMEM((pitch, padded), BF16),
            pltpu.VMEM((3 * c1, 3 * pitch), BF16),
            pltpu.VMEM((c1, padded), BF16),
            pltpu.VMEM((c1, cells), F32),
            pltpu.VMEM((9 * f2, padded), BF16),
            pltpu.VMEM((n_mp, f1, cells), F32),
            pltpu.VMEM((2, f2 // 2, 27 * c1), F32),
        ],
        2 * cells * 27 * (c0 * c1 + 3 * f2 * c1),
        4 * 1024 * 1024,
    )(near, far, w2r, w2b, cotangent)

    parts = sum_over_mp(keep, give)
    half_sum = add(half_keep, swap(half_give, "sample", 1))
    for bit in bits_above(n_sample):
        half_sum = add(half_sum, swap(half_sum, "sample", bit))

    keep, give, grad_first = call(
        functools.partial(backward_kernel, n_mp),
        [
            sds((half, rows_in, cells), BF16),
            sds((half, rows_in, cells), BF16),
            sds((f1, 27 * c0), BF16),
        ],
        [pltpu.VMEM((9 * f1, padded), BF16), pltpu.VMEM((n_mp, rows_in, cells), F32)],
        2 * cells * 27 * 2 * c0 * f1,
        1024 * 1024,
    )(*parts, pre_own, vol_all, w1b)
    ins = sum_over_mp(keep, give)

    both = swap(jnp.concatenate([half_sum, grad_first], axis=1), "sample", 1)
    grad_first = add(grad_first, both[:, 27 * c1 :])
    bits = bits_above(n_sample)
    for bit in bits[:-1]:
        grad_first = add(grad_first, swap(grad_first, "sample", bit))
    grad_first = (grad_first.astype(F32) + swap(grad_first, "sample", bits[-1]).astype(F32)) * scale
    grad_second = call(
        functools.partial(place_kernel, scale),
        sds((2, f2 // 2, 27 * c1), F32),
        [],
        0,
        1024 * 1024,
    )(half_sum, both).reshape(f2, 27 * c1)
    total = ins[0].astype(F32)
    for other in ins[1:]:
        total = total + other.astype(F32)
    return (
        features.reshape(f2, 1, cells),
        total.astype(BF16).reshape(rows_in, 1, cells),
        grad_first,
        grad_second,
    )


def solution(mesh):
    return jax.shard_map(
        local,
        mesh=mesh,
        in_specs=(P("mp", "sample", None), P("mp", None), P("mp", None), P("mp", "sample", None)),
        out_specs=(P("mp", "sample", None), P("mp", "sample", None), P("mp", None), P("mp", None)),
        check_vma=False,
    )
```

```python
import functools
import math

import jax
import jax.numpy as jnp
from jax import lax
from jax.experimental import pallas as pl
from jax.experimental.pallas import tpu as pltpu
from jax.sharding import PartitionSpec as P

SIDE = 16
PLANE = SIDE * SIDE
F32 = jnp.float32
BF16 = jnp.bfloat16
VMEM_LIMIT = 48 * 1024 * 1024


def pitch_of(channels):
    width = 3 * channels
    slack = max((i * width) % 128 for i in range(9))
    return -(-(width + slack) // 128) * 128


def lane_grid(width):
    lane = lax.broadcasted_iota(jnp.int32, (1, width), 1)
    return lane % SIDE, (lane // SIDE) % SIDE


def inside(grid_xy, dy, dx):
    x, y = grid_xy
    ok = None
    for coord, step in ((y, dy), (x, dx)):
        if step < 0:
            now = coord >= -step
        elif step > 0:
            now = coord < SIDE - step
        else:
            continue
        ok = now if ok is None else ok & now
    return ok


def moved(values, grid_xy, dy, dx):
    if dy == 0 and dx == 0:
        return values
    width = values.shape[1]
    rolled = pltpu.roll(values, (-(dy * SIDE + dx)) % width, 1)
    return jnp.where(inside(grid_xy, dy, dx), rolled, 0.0)


def sigmoid(v):
    return 0.5 + 0.5 * jnp.tanh(0.5 * v)


def dot(a, b):
    return lax.dot_general(a, b, (((1,), (0,)), ((), ())), preferred_element_type=F32)


def dot_nt(a, b):
    return lax.dot_general(a, b, (((1,), (1,)), ((), ())), preferred_element_type=F32)


def chunk_of(cells):
    return 2 * PLANE if cells % (2 * PLANE) == 0 else PLANE


def forward_kernel(n_mp, c0, *refs):
    near_ref, far_ref, w2r_ref, w2b_ref, cot_ref = refs[:5]
    feat_ref, pre_ref, vol_ref, keep_ref, give_ref, grad_ref = refs[5:11]
    vs, w1s, v3, w1r, hid, pre, d9, part, acc = refs[11:]

    me = lax.axis_index("mp")
    f1 = w1s.shape[1]
    c1 = n_mp * f1
    f2, cells = cot_ref.shape
    chunk = chunk_of(cells)
    steps = cells // chunk
    pitch = pitch_of(c0)
    grid_xy = lane_grid(chunk)

    for k in range(n_mp):
        piece = (far_ref if k % 2 else near_ref)[k // 2].astype(F32)
        slot = me ^ k
        w1s[slot] = piece[:f1]
        vs[slot] = piece[f1:, :cells]

    lane = lax.broadcasted_iota(jnp.int32, (1, pitch), 1)
    for dz in range(3):
        for dy in range(3):
            start = (dz * 3 + dy) * 3 * c0
            low = start // 128 * 128
            block = w1s[:, :, low : low + pitch].reshape(c1, pitch)
            if start != low:
                block = pltpu.roll(block, pitch - (start - low), 1)
            block = jnp.where(lane < 3 * c0, block, 0.0)
            w1r[dy * c1 : (dy + 1) * c1, dz * pitch : (dz + 1) * pitch] = block.astype(BF16)

    for ref in (v3, hid, d9):
        zero = jnp.zeros((ref.shape[0], PLANE), BF16)
        ref[:, :PLANE] = zero
        ref[:, PLANE + cells :] = zero
    v3[3 * c0 :, PLANE : PLANE + cells] = jnp.zeros((pitch - 3 * c0, cells), BF16)

    for step in range(steps):
        base = step * chunk
        values = vs[:, :, base : base + chunk].reshape(c0, chunk)
        vol_ref[:, base : base + chunk] = values.astype(BF16)
        for dx in range(3):
            v3[dx * c0 : (dx + 1) * c0, base + PLANE : base + PLANE + chunk] = moved(values, grid_xy, 0, dx - 1).astype(BF16)

    def stacked(ref, base, order):
        return jnp.concatenate([ref[:, base + dz * PLANE : base + dz * PLANE + chunk] for dz in order], axis=0)

    def first_conv(base):
        z = dot(w1r[...], stacked(v3, base, (0, 1, 2)))
        total = z[c1 : 2 * c1]
        total = total + moved(z[:c1], grid_xy, -1, 0)
        total = total + moved(z[2 * c1 :], grid_xy, 1, 0)
        pre[:, base : base + chunk] = total
        hid[:, base + PLANE : base + PLANE + chunk] = (total * sigmoid(total)).astype(BF16)

    def second_conv(base):
        z = dot(w2r_ref[...], stacked(hid, base, (0, 1, 2)))
        total = None
        for dy in range(3):
            for dx in range(3):
                k = dy * 3 + dx
                term = moved(z[k * f2 : (k + 1) * f2], grid_xy, dy - 1, dx - 1)
                total = term if total is None else total + term
        s = sigmoid(total)
        feat_ref[:, base : base + chunk] = (total * s).astype(BF16)
        cot = cot_ref[:, base : base + chunk].astype(F32)
        delta = (cot * (s * (1.0 + total * (1.0 - s)))).astype(BF16).astype(F32)
        for dy in range(3):
            for dx in range(3):
                k = dy * 3 + dx
                d9[k * f2 : (k + 1) * f2, base + PLANE : base + PLANE + chunk] = moved(delta, grid_xy, 1 - dy, 1 - dx).astype(BF16)

    def gradients(base):
        deltas = stacked(d9, base, (2, 1, 0))
        part[:, :, base : base + chunk] = dot(w2b_ref[...], deltas).reshape(n_mp, f1, chunk)
        g = dot_nt(deltas, hid[:, base + PLANE : base + PLANE + chunk])
        acc[...] = g if base == 0 else acc[...] + g

    for step in range(steps + 2):
        if step < steps:
            first_conv(step * chunk)
        if 1 <= step <= steps:
            second_conv((step - 1) * chunk)
        if step >= 2:
            gradients((step - 2) * chunk)

    pre_ref[...] = pre[pl.ds(pl.multiple_of(me * f1, f1), f1), :]
    for k in range(n_mp):
        (give_ref if k % 2 else keep_ref)[k // 2] = part[me ^ k].astype(BF16)
    for t in range(27):
        grad_ref[:, t * c1 : (t + 1) * c1] = acc[t * f2 : (t + 1) * f2].astype(BF16)


def backward_kernel(n_mp, *refs):
    parts = refs[: n_mp // 2]
    pre_ref, vol_ref, w1b_ref, keep_ref, give_ref, grad_ref, d9, part, acc = refs[n_mp // 2 :]
    me = lax.axis_index("mp")
    f1, cells = pre_ref.shape
    c0 = vol_ref.shape[0]
    chunk = chunk_of(cells)
    steps = cells // chunk
    grid_xy = lane_grid(chunk)

    zero = jnp.zeros((d9.shape[0], PLANE), BF16)
    d9[:, :PLANE] = zero
    d9[:, PLANE + cells :] = zero

    reps = max(1, 128 // c0)
    span = reps * c0

    def take(base):
        total = parts[0][:, base : base + chunk].astype(F32)
        for other in parts[1:]:
            total = total + other[:, base : base + chunk].astype(F32)
        v = pre_ref[:, base : base + chunk]
        s = sigmoid(v)
        delta = (total * (s * (1.0 + v * (1.0 - s)))).astype(BF16).astype(F32)
        shifts = [moved(delta, grid_xy, 1 - dy, 1 - dx) for dy in range(3) for dx in range(3)]
        d9[:, base + PLANE : base + PLANE + chunk] = jnp.concatenate(shifts, axis=0).astype(BF16)

    def gradients(base):
        deltas = jnp.concatenate([d9[:, base + dz * PLANE : base + dz * PLANE + chunk] for dz in (2, 1, 0)], axis=0)
        part[:, :, base : base + chunk] = dot(w1b_ref[...], deltas).reshape(n_mp, c0 // n_mp, chunk)
        vol = vol_ref[:, base : base + chunk]
        g = dot_nt(deltas, jnp.concatenate([vol] * reps, axis=0))
        acc[...] = g if base == 0 else acc[...] + g

    for step in range(steps + 1):
        if step < steps:
            take(step * chunk)
        if step >= 1:
            gradients((step - 1) * chunk)
    for k in range(n_mp):
        (give_ref if k % 2 else keep_ref)[k // 2] = part[me ^ k].astype(BF16)

    lane = lax.broadcasted_iota(jnp.int32, (1, span), 1)
    for t in range(0, 27, reps):
        merged = acc[t * f1 : (t + 1) * f1]
        for r in range(1, min(reps, 27 - t)):
            merged = jnp.where(lane >= r * c0, acc[(t + r) * f1 : (t + r + 1) * f1], merged)
        width = min(span, (27 - t) * c0)
        grad_ref[:, t * c0 : t * c0 + width] = merged[:, :width].astype(BF16)


def swap(value, axis, k):
    n = lax.axis_size(axis)
    return lax.ppermute(value, axis, [(i, i ^ k) for i in range(n)])


def add(a, b):
    return (a.astype(F32) + b.astype(F32)).astype(BF16)


def sum_over_chips(keep, got):
    parts = [add(keep[j], got[j]) for j in range(keep.shape[0])]
    return [parts[0]] + [swap(parts[j], "mp", 2 * j) for j in range(1, len(parts))]


def bits_of(count):
    return [1 << i for i in reversed(range(count.bit_length() - 1))]


def call(kernel, out_shape, scratch, flops, nbytes):
    return pl.pallas_call(
        kernel,
        out_shape=out_shape,
        scratch_shapes=scratch,
        compiler_params=pltpu.CompilerParams(vmem_limit_bytes=VMEM_LIMIT),
        cost_estimate=pl.CostEstimate(flops=flops, bytes_accessed=nbytes, transcendentals=0),
    )


def local(volumes, w_first, w_second, cotangent):
    n_mp = lax.axis_size("mp")
    n_sample = lax.axis_size("sample")
    rows_in, _, cells = volumes.shape
    f1 = w_first.shape[0]
    f2 = w_second.shape[0]
    c0 = w_first.shape[1] // 27
    c1 = w_second.shape[1] // 27
    pitch = pitch_of(c0)
    scale = 1.0 / math.sqrt(n_sample * volumes.shape[1] * cells)
    volumes = volumes.reshape(rows_in, cells)
    cotangent = cotangent.reshape(f2, cells)
    padded = cells + 2 * PLANE

    need = (8 * 3 * c0) // 128 * 128 + pitch
    wide = max(cells, need)
    piece = jnp.concatenate(
        [
            jnp.pad(w_first, ((0, 0), (0, wide - w_first.shape[1]))),
            jnp.pad(volumes, ((0, 0), (0, wide - cells))),
        ],
        axis=0,
    )
    near = [piece] + [swap(piece, "mp", k) for k in range(2, n_mp, 2)]
    near = jnp.stack(near)
    far = swap(near, "mp", 1)

    w2t = w_second.reshape(f2, 3, 9, c1)
    w2r = jnp.transpose(w2t, (2, 0, 1, 3)).reshape(9 * f2, 3 * c1)
    w2b = jnp.transpose(w2t, (3, 1, 2, 0)).reshape(c1, 27 * f2)
    w1b = jnp.transpose(w_first.reshape(f1, 27, c0), (2, 1, 0)).reshape(c0, 27 * f1)

    sds = jax.ShapeDtypeStruct
    half = n_mp // 2
    features, pre_own, vol_all, keep, give, grad_second = call(
        functools.partial(forward_kernel, n_mp, c0),
        [
            sds((f2, cells), BF16),
            sds((f1, cells), F32),
            sds((c0, cells), BF16),
            sds((half, f1, cells), BF16),
            sds((half, f1, cells), BF16),
            sds((f2, 27 * c1), BF16),
        ],
        [
            pltpu.VMEM((n_mp, rows_in, cells), F32),
            pltpu.VMEM((n_mp, f1, wide), F32),
            pltpu.VMEM((pitch, padded), BF16),
            pltpu.VMEM((3 * c1, 3 * pitch), BF16),
            pltpu.VMEM((c1, padded), BF16),
            pltpu.VMEM((c1, cells), F32),
            pltpu.VMEM((9 * f2, padded), BF16),
            pltpu.VMEM((n_mp, f1, cells), F32),
            pltpu.VMEM((27 * f2, c1), F32),
        ],
        2 * cells * 27 * (c0 * c1 + 3 * f2 * c1),
        4 * 1024 * 1024,
    )(near, far, w2r, w2b, cotangent)

    bits = bits_of(n_sample)
    parts = sum_over_chips(keep, swap(give, "mp", 1))
    second_got = swap(grad_second, "sample", bits[0])

    keep, give, grad_first = call(
        functools.partial(backward_kernel, n_mp),
        [
            sds((half, rows_in, cells), BF16),
            sds((half, rows_in, cells), BF16),
            sds((f1, 27 * c0), BF16),
        ],
        [
            pltpu.VMEM((9 * f1, padded), BF16),
            pltpu.VMEM((n_mp, rows_in, cells), F32),
            pltpu.VMEM((27 * f1, max(1, 128 // c0) * c0), F32),
        ],
        2 * cells * 27 * 2 * c0 * f1,
        1024 * 1024,
    )(*parts, pre_own, vol_all, w1b)
    ins = sum_over_chips(keep, swap(give, "mp", 1))

    second_got, grad_first = lax.optimization_barrier((second_got, grad_first))
    first_got = swap(grad_first, "sample", bits[0])
    for bit in bits[1:]:
        grad_first = add(grad_first, first_got)
        first_got = swap(grad_first, "sample", bit)
        grad_second = add(grad_second, second_got)
        second_got = swap(grad_second, "sample", bit)
    grad_first = (grad_first.astype(F32) + first_got.astype(F32)) * scale
    grad_second = (grad_second.astype(F32) + second_got.astype(F32)) * scale
    total = ins[0].astype(F32)
    for other in ins[1:]:
        total = total + other.astype(F32)
    return (
        features.reshape(f2, 1, cells),
        total.astype(BF16).reshape(rows_in, 1, cells),
        grad_first,
        grad_second,
    )


def solution(mesh):
    return jax.shard_map(
        local,
        mesh=mesh,
        in_specs=(P("mp", "sample", None), P("mp", None), P("mp", None), P("mp", "sample", None)),
        out_specs=(P("mp", "sample", None), P("mp", "sample", None), P("mp", None), P("mp", None)),
        check_vma=False,
    )
```

```python
import functools
import math

import jax
import jax.numpy as jnp
from jax import lax
from jax.experimental import pallas as pl
from jax.experimental.pallas import tpu as pltpu
from jax.sharding import PartitionSpec as P

SIDE = 16
PLANE = SIDE * SIDE
F32 = jnp.float32
BF16 = jnp.bfloat16
VMEM_LIMIT = 48 * 1024 * 1024


def pitch_of(channels):
    width = 3 * channels
    slack = max((i * width) % 128 for i in range(9))
    return -(-(width + slack) // 128) * 128


def lane_grid(width):
    lane = lax.broadcasted_iota(jnp.int32, (1, width), 1)
    return lane % SIDE, (lane // SIDE) % SIDE


def inside(grid_xy, dy, dx):
    x, y = grid_xy
    ok = None
    for coord, step in ((y, dy), (x, dx)):
        if step < 0:
            now = coord >= -step
        elif step > 0:
            now = coord < SIDE - step
        else:
            continue
        ok = now if ok is None else ok & now
    return ok


def moved(values, grid_xy, dy, dx):
    if dy == 0 and dx == 0:
        return values
    width = values.shape[1]
    rolled = pltpu.roll(values, (-(dy * SIDE + dx)) % width, 1)
    return jnp.where(inside(grid_xy, dy, dx), rolled, 0.0)


def sigmoid(v):
    return 0.5 + 0.5 * jnp.tanh(0.5 * v)


def dot(a, b):
    return lax.dot_general(a, b, (((1,), (0,)), ((), ())), preferred_element_type=F32)


def dot_nt(a, b):
    return lax.dot_general(a, b, (((1,), (1,)), ((), ())), preferred_element_type=F32)


def chunk_of(cells):
    return 2 * PLANE if cells % (2 * PLANE) == 0 else PLANE


def pack_kernel(w_ref, v_ref, out_ref):
    f1, width = w_ref.shape
    rows_in, cells = v_ref.shape
    run = cells * rows_in // f1
    lanes = out_ref.shape[1] - run
    out_ref[:, :width] = w_ref[...]
    if lanes > width:
        out_ref[:, width:lanes] = jnp.zeros((f1, lanes - width), BF16)
    folded = [v_ref[:, i * run : (i + 1) * run].astype(F32) for i in range(f1 // rows_in)]
    out_ref[:, lanes:] = jnp.concatenate(folded, axis=0).astype(BF16)


def forward_kernel(n_mp, c0, *refs):
    near_ref, far_ref, w2r_ref, cot_ref = refs[:4]
    feat_ref, pre_ref, vol_ref, d9, half_keep_ref, half_give_ref = refs[4:10]
    vs, w1s, v3, w1r, hid, pre, acc = refs[10:]

    me = lax.axis_index("mp")
    low_half = lax.axis_index("sample") % 2 == 0
    _, f1, lanes = w1s.shape
    rows_in = vs.shape[1]
    folds = f1 // rows_in
    run = near_ref.shape[2] - lanes
    c1 = n_mp * f1
    f2, cells = cot_ref.shape
    chunk = chunk_of(cells)
    steps = cells // chunk
    pitch = pitch_of(c0)
    grid_xy = lane_grid(chunk)

    for k in range(n_mp):
        piece = (far_ref if k % 2 else near_ref)[k // 2].astype(F32)
        slot = me ^ k
        w1s[slot] = piece[:, :lanes]
        for i in range(folds):
            vs[slot, :, i * run : (i + 1) * run] = piece[i * rows_in : (i + 1) * rows_in, lanes:]

    lane = lax.broadcasted_iota(jnp.int32, (1, pitch), 1)
    for dz in range(3):
        for dy in range(3):
            start = (dz * 3 + dy) * 3 * c0
            low = start // 128 * 128
            block = w1s[:, :, low : low + pitch].reshape(c1, pitch)
            if start != low:
                block = pltpu.roll(block, pitch - (start - low), 1)
            block = jnp.where(lane < 3 * c0, block, 0.0)
            w1r[dy * c1 : (dy + 1) * c1, dz * pitch : (dz + 1) * pitch] = block.astype(BF16)

    for ref in (v3, hid, d9):
        zero = jnp.zeros((ref.shape[0], PLANE), BF16)
        ref[:, :PLANE] = zero
        ref[:, PLANE + cells :] = zero
    v3[3 * c0 :, PLANE : PLANE + cells] = jnp.zeros((pitch - 3 * c0, cells), BF16)

    for step in range(steps):
        base = step * chunk
        values = vs[:, :, base : base + chunk].reshape(c0, chunk)
        vol_ref[:, base : base + chunk] = values.astype(BF16)
        for dx in range(3):
            v3[dx * c0 : (dx + 1) * c0, base + PLANE : base + PLANE + chunk] = moved(values, grid_xy, 0, dx - 1).astype(BF16)

    def stacked(ref, base, order):
        return jnp.concatenate([ref[:, base + dz * PLANE : base + dz * PLANE + chunk] for dz in order], axis=0)

    def first_conv(base):
        z = dot(w1r[...], stacked(v3, base, (0, 1, 2)))
        total = z[c1 : 2 * c1]
        total = total + moved(z[:c1], grid_xy, -1, 0)
        total = total + moved(z[2 * c1 :], grid_xy, 1, 0)
        pre[:, base : base + chunk] = total
        hid[:, base + PLANE : base + PLANE + chunk] = (total * sigmoid(total)).astype(BF16)

    def second_conv(base):
        z = dot(w2r_ref[...], stacked(hid, base, (0, 1, 2)))
        total = None
        for dy in range(3):
            for dx in range(3):
                k = dy * 3 + dx
                term = moved(z[k * f2 : (k + 1) * f2], grid_xy, dy - 1, dx - 1)
                total = term if total is None else total + term
        s = sigmoid(total)
        feat_ref[:, base : base + chunk] = (total * s).astype(BF16)
        cot = cot_ref[:, base : base + chunk].astype(F32)
        delta = (cot * (s * (1.0 + total * (1.0 - s)))).astype(BF16).astype(F32)
        for dy in range(3):
            for dx in range(3):
                k = dy * 3 + dx
                d9[k * f2 : (k + 1) * f2, base + PLANE : base + PLANE + chunk] = moved(delta, grid_xy, 1 - dy, 1 - dx).astype(BF16)

    def gradients(base):
        deltas = stacked(d9, base, (2, 1, 0))
        g = dot_nt(deltas, hid[:, base + PLANE : base + PLANE + chunk])
        acc[...] = g if base == 0 else acc[...] + g

    for step in range(steps + 2):
        if step < steps:
            first_conv(step * chunk)
        if 1 <= step <= steps:
            second_conv((step - 1) * chunk)
        if step >= 2:
            gradients((step - 2) * chunk)

    pre_ref[...] = pre[pl.ds(pl.multiple_of(me * f1, f1), f1), :]
    half = f2 // 2
    for t in range(27):
        low = acc[t * f2 : t * f2 + half]
        high = acc[t * f2 + half : (t + 1) * f2]
        half_keep_ref[:, t * c1 : (t + 1) * c1] = jnp.where(low_half, low, high).astype(BF16)
        half_give_ref[:, t * c1 : (t + 1) * c1] = jnp.where(low_half, high, low).astype(BF16)


def data_kernel(n_mp, d9, w2b_ref, keep_ref, give_ref, part):
    me = lax.axis_index("mp")
    _, f1, cells = part.shape
    chunk = chunk_of(cells)
    for base in range(0, cells, chunk):
        deltas = jnp.concatenate([d9[:, base + dz * PLANE : base + dz * PLANE + chunk] for dz in (2, 1, 0)], axis=0)
        part[:, :, base : base + chunk] = dot(w2b_ref[...], deltas).reshape(n_mp, f1, chunk)
    for k in range(n_mp):
        (give_ref if k % 2 else keep_ref)[k // 2] = part[me ^ k].astype(BF16)


def backward_kernel(n_mp, *refs):
    parts = refs[: n_mp // 2]
    pre_ref, vol_ref, w1b_ref, keep_ref, give_ref, grad_ref, d9, part, acc = refs[n_mp // 2 :]
    me = lax.axis_index("mp")
    f1, cells = pre_ref.shape
    c0 = vol_ref.shape[0]
    chunk = chunk_of(cells)
    steps = cells // chunk
    grid_xy = lane_grid(chunk)

    zero = jnp.zeros((d9.shape[0], PLANE), BF16)
    d9[:, :PLANE] = zero
    d9[:, PLANE + cells :] = zero

    reps = max(1, 128 // c0)
    span = reps * c0

    def take(base):
        total = parts[0][:, base : base + chunk].astype(F32)
        for other in parts[1:]:
            total = total + other[:, base : base + chunk].astype(F32)
        v = pre_ref[:, base : base + chunk]
        s = sigmoid(v)
        delta = (total * (s * (1.0 + v * (1.0 - s)))).astype(BF16).astype(F32)
        shifts = [moved(delta, grid_xy, 1 - dy, 1 - dx) for dy in range(3) for dx in range(3)]
        d9[:, base + PLANE : base + PLANE + chunk] = jnp.concatenate(shifts, axis=0).astype(BF16)

    def gradients(base):
        deltas = jnp.concatenate([d9[:, base + dz * PLANE : base + dz * PLANE + chunk] for dz in (2, 1, 0)], axis=0)
        part[:, :, base : base + chunk] = dot(w1b_ref[...], deltas).reshape(n_mp, c0 // n_mp, chunk)
        vol = vol_ref[:, base : base + chunk]
        g = dot_nt(deltas, jnp.concatenate([vol] * reps, axis=0))
        acc[...] = g if base == 0 else acc[...] + g

    for step in range(steps + 1):
        if step < steps:
            take(step * chunk)
        if step >= 1:
            gradients((step - 1) * chunk)
    for k in range(n_mp):
        (give_ref if k % 2 else keep_ref)[k // 2] = part[me ^ k].astype(BF16)

    lane = lax.broadcasted_iota(jnp.int32, (1, span), 1)
    for t in range(0, 27, reps):
        merged = acc[t * f1 : (t + 1) * f1]
        for r in range(1, min(reps, 27 - t)):
            merged = jnp.where(lane >= r * c0, acc[(t + r) * f1 : (t + r + 1) * f1], merged)
        width = min(span, (27 - t) * c0)
        grad_ref[:, t * c0 : t * c0 + width] = merged[:, :width].astype(BF16)


def place_kernel(scale, mine_ref, other_ref, out_ref):
    bit = lax.axis_index("sample") % 2
    width = out_ref.shape[2]
    out_ref[bit] = mine_ref[...].astype(F32) * scale
    out_ref[1 - bit] = other_ref[:, :width].astype(F32) * scale


def swap(value, axis, k):
    n = lax.axis_size(axis)
    return lax.ppermute(value, axis, [(i, i ^ k) for i in range(n)])


def add(a, b):
    return (a.astype(F32) + b.astype(F32)).astype(BF16)


def sum_over_chips(keep, got):
    parts = [add(keep[j], got[j]) for j in range(keep.shape[0])]
    return [parts[0]] + [swap(parts[j], "mp", 2 * j) for j in range(1, len(parts))]


def bits_above(count):
    return [1 << i for i in range(1, count.bit_length() - 1)]


def call(kernel, out_shape, scratch, flops, nbytes):
    return pl.pallas_call(
        kernel,
        out_shape=out_shape,
        scratch_shapes=scratch,
        compiler_params=pltpu.CompilerParams(vmem_limit_bytes=VMEM_LIMIT),
        cost_estimate=pl.CostEstimate(flops=flops, bytes_accessed=nbytes, transcendentals=0),
    )


def local(volumes, w_first, w_second, cotangent):
    n_mp = lax.axis_size("mp")
    n_sample = lax.axis_size("sample")
    rows_in, _, cells = volumes.shape
    f1 = w_first.shape[0]
    f2 = w_second.shape[0]
    c0 = w_first.shape[1] // 27
    c1 = w_second.shape[1] // 27
    pitch = pitch_of(c0)
    scale = 1.0 / math.sqrt(n_sample * volumes.shape[1] * cells)
    volumes = volumes.reshape(rows_in, cells)
    cotangent = cotangent.reshape(f2, cells)
    padded = cells + 2 * PLANE

    lanes = (8 * 3 * c0) // 128 * 128 + pitch
    run = cells * rows_in // f1
    piece = call(
        pack_kernel,
        jax.ShapeDtypeStruct((f1, lanes + run), BF16),
        [],
        0,
        256 * 1024,
    )(w_first, volumes)
    near = [piece] + [swap(piece, "mp", k) for k in range(2, n_mp, 2)]
    near = jnp.stack(near)
    far = swap(near, "mp", 1)

    w2t = w_second.reshape(f2, 3, 9, c1)
    w2r = jnp.transpose(w2t, (2, 0, 1, 3)).reshape(9 * f2, 3 * c1)
    w2b = jnp.transpose(w2t, (3, 1, 2, 0)).reshape(c1, 27 * f2)
    w1b = jnp.transpose(w_first.reshape(f1, 27, c0), (2, 1, 0)).reshape(c0, 27 * f1)

    sds = jax.ShapeDtypeStruct
    half = n_mp // 2
    features, pre_own, vol_all, d9, half_keep, half_give = call(
        functools.partial(forward_kernel, n_mp, c0),
        [
            sds((f2, cells), BF16),
            sds((f1, cells), F32),
            sds((c0, cells), BF16),
            sds((9 * f2, padded), BF16),
            sds((f2 // 2, 27 * c1), BF16),
            sds((f2 // 2, 27 * c1), BF16),
        ],
        [
            pltpu.VMEM((n_mp, rows_in, cells), F32),
            pltpu.VMEM((n_mp, f1, lanes), F32),
            pltpu.VMEM((pitch, padded), BF16),
            pltpu.VMEM((3 * c1, 3 * pitch), BF16),
            pltpu.VMEM((c1, padded), BF16),
            pltpu.VMEM((c1, cells), F32),
            pltpu.VMEM((27 * f2, c1), F32),
        ],
        2 * cells * 27 * (c0 * c1 + 2 * f2 * c1),
        4 * 1024 * 1024,
    )(near, far, w2r, cotangent)

    half_got = swap(half_give, "sample", 1)
    keep, give = call(
        functools.partial(data_kernel, n_mp),
        [sds((half, f1, cells), BF16), sds((half, f1, cells), BF16)],
        [pltpu.VMEM((n_mp, f1, cells), F32)],
        2 * cells * 27 * f2 * c1,
        2 * 1024 * 1024,
    )(d9, w2b)
    parts = sum_over_chips(keep, swap(give, "mp", 1))
    half_sum = add(half_keep, half_got)
    bits = bits_above(n_sample)
    for bit in bits[:-1]:
        half_sum = add(half_sum, swap(half_sum, "sample", bit))
    half_got = swap(half_sum, "sample", bits[-1])

    keep, give, grad_first = call(
        functools.partial(backward_kernel, n_mp),
        [
            sds((half, rows_in, cells), BF16),
            sds((half, rows_in, cells), BF16),
            sds((f1, 27 * c0), BF16),
        ],
        [
            pltpu.VMEM((9 * f1, padded), BF16),
            pltpu.VMEM((n_mp, rows_in, cells), F32),
            pltpu.VMEM((27 * f1, max(1, 128 // c0) * c0), F32),
        ],
        2 * cells * 27 * 2 * c0 * f1,
        1024 * 1024,
    )(*parts, pre_own, vol_all, w1b)
    ins = sum_over_chips(keep, swap(give, "mp", 1))

    half_got, grad_first = lax.optimization_barrier((half_got, grad_first))
    half_sum = add(half_sum, half_got)
    both = swap(jnp.concatenate([half_sum, grad_first], axis=1), "sample", 1)
    grad_first = add(grad_first, both[:, 27 * c1 :])
    for bit in bits[:-1]:
        grad_first = add(grad_first, swap(grad_first, "sample", bit))
    grad_first = (grad_first.astype(F32) + swap(grad_first, "sample", bits[-1]).astype(F32)) * scale
    grad_second = call(
        functools.partial(place_kernel, scale),
        sds((2, f2 // 2, 27 * c1), F32),
        [],
        0,
        1024 * 1024,
    )(half_sum, both).reshape(f2, 27 * c1)
    total = ins[0].astype(F32)
    for other in ins[1:]:
        total = total + other.astype(F32)
    return (
        features.reshape(f2, 1, cells),
        total.astype(BF16).reshape(rows_in, 1, cells),
        grad_first,
        grad_second,
    )


def solution(mesh):
    return jax.shard_map(
        local,
        mesh=mesh,
        in_specs=(P("mp", "sample", None), P("mp", None), P("mp", None), P("mp", "sample", None)),
        out_specs=(P("mp", "sample", None), P("mp", "sample", None), P("mp", None), P("mp", None)),
        check_vma=False,
    )
```

```python
import functools
import math

import jax
import jax.numpy as jnp
from jax import lax
from jax.experimental import pallas as pl
from jax.experimental.pallas import tpu as pltpu
from jax.sharding import PartitionSpec as P

SIDE = 16
PLANE = SIDE * SIDE
F32 = jnp.float32
BF16 = jnp.bfloat16
VMEM_LIMIT = 48 * 1024 * 1024


def pitch_of(channels):
    width = 3 * channels
    slack = max((i * width) % 128 for i in range(9))
    return -(-(width + slack) // 128) * 128


def lane_grid(width):
    lane = lax.broadcasted_iota(jnp.int32, (1, width), 1)
    return lane % SIDE, (lane // SIDE) % SIDE


def inside(grid_xy, dy, dx):
    x, y = grid_xy
    ok = None
    for coord, step in ((y, dy), (x, dx)):
        if step < 0:
            now = coord >= -step
        elif step > 0:
            now = coord < SIDE - step
        else:
            continue
        ok = now if ok is None else ok & now
    return ok


def moved(values, grid_xy, dy, dx):
    if dy == 0 and dx == 0:
        return values
    width = values.shape[1]
    rolled = pltpu.roll(values, (-(dy * SIDE + dx)) % width, 1)
    return jnp.where(inside(grid_xy, dy, dx), rolled, 0.0)


def sigmoid(v):
    return 0.5 + 0.5 * jnp.tanh(0.5 * v)


def dot(a, b):
    return lax.dot_general(a, b, (((1,), (0,)), ((), ())), preferred_element_type=F32)


def dot_nt(a, b):
    return lax.dot_general(a, b, (((1,), (1,)), ((), ())), preferred_element_type=F32)


def chunk_of(cells):
    return 2 * PLANE if cells % (2 * PLANE) == 0 else PLANE


def forward_kernel(n_mp, c0, *refs):
    near_ref, far_ref, w2r_ref, cot_ref = refs[:4]
    feat_ref, pre_ref, vol_ref, d9, half_keep_ref, half_give_ref = refs[4:10]
    vs, w1s, v3, w1r, hid, pre, acc = refs[10:]

    me = lax.axis_index("mp")
    low_half = lax.axis_index("sample") % 2 == 0
    _, f1, lanes = w1s.shape
    c1 = n_mp * f1
    f2, cells = cot_ref.shape
    chunk = chunk_of(cells)
    steps = cells // chunk
    pitch = pitch_of(c0)
    grid_xy = lane_grid(chunk)

    for k in range(n_mp):
        piece = (far_ref if k % 2 else near_ref)[k // 2].astype(F32)
        slot = me ^ k
        w1s[slot] = piece[:f1, :lanes]
        vs[slot] = piece[f1:, :cells]

    lane = lax.broadcasted_iota(jnp.int32, (1, pitch), 1)
    for dz in range(3):
        for dy in range(3):
            start = (dz * 3 + dy) * 3 * c0
            low = start // 128 * 128
            block = w1s[:, :, low : low + pitch].reshape(c1, pitch)
            if start != low:
                block = pltpu.roll(block, pitch - (start - low), 1)
            block = jnp.where(lane < 3 * c0, block, 0.0)
            w1r[dy * c1 : (dy + 1) * c1, dz * pitch : (dz + 1) * pitch] = block.astype(BF16)

    for ref in (v3, hid, d9):
        zero = jnp.zeros((ref.shape[0], PLANE), BF16)
        ref[:, :PLANE] = zero
        ref[:, PLANE + cells :] = zero
    v3[3 * c0 :, PLANE : PLANE + cells] = jnp.zeros((pitch - 3 * c0, cells), BF16)

    for step in range(steps):
        base = step * chunk
        values = vs[:, :, base : base + chunk].reshape(c0, chunk)
        vol_ref[:, base : base + chunk] = values.astype(BF16)
        for dx in range(3):
            v3[dx * c0 : (dx + 1) * c0, base + PLANE : base + PLANE + chunk] = moved(values, grid_xy, 0, dx - 1).astype(BF16)

    def stacked(ref, base, order):
        return jnp.concatenate([ref[:, base + dz * PLANE : base + dz * PLANE + chunk] for dz in order], axis=0)

    def first_conv(base):
        z = dot(w1r[...], stacked(v3, base, (0, 1, 2)))
        total = z[c1 : 2 * c1]
        total = total + moved(z[:c1], grid_xy, -1, 0)
        total = total + moved(z[2 * c1 :], grid_xy, 1, 0)
        pre[:, base : base + chunk] = total
        hid[:, base + PLANE : base + PLANE + chunk] = (total * sigmoid(total)).astype(BF16)

    def second_conv(base):
        z = dot(w2r_ref[...], stacked(hid, base, (0, 1, 2)))
        total = None
        for dy in range(3):
            for dx in range(3):
                k = dy * 3 + dx
                term = moved(z[k * f2 : (k + 1) * f2], grid_xy, dy - 1, dx - 1)
                total = term if total is None else total + term
        s = sigmoid(total)
        feat_ref[:, base : base + chunk] = (total * s).astype(BF16)
        cot = cot_ref[:, base : base + chunk].astype(F32)
        delta = (cot * (s * (1.0 + total * (1.0 - s)))).astype(BF16).astype(F32)
        for dy in range(3):
            for dx in range(3):
                k = dy * 3 + dx
                d9[k * f2 : (k + 1) * f2, base + PLANE : base + PLANE + chunk] = moved(delta, grid_xy, 1 - dy, 1 - dx).astype(BF16)

    def gradients(base):
        deltas = stacked(d9, base, (2, 1, 0))
        g = dot_nt(deltas, hid[:, base + PLANE : base + PLANE + chunk])
        acc[...] = g if base == 0 else acc[...] + g

    for step in range(steps + 2):
        if step < steps:
            first_conv(step * chunk)
        if 1 <= step <= steps:
            second_conv((step - 1) * chunk)
        if step >= 2:
            gradients((step - 2) * chunk)

    pre_ref[...] = pre[pl.ds(pl.multiple_of(me * f1, f1), f1), :]
    half = f2 // 2
    for t in range(27):
        low = acc[t * f2 : t * f2 + half]
        high = acc[t * f2 + half : (t + 1) * f2]
        half_keep_ref[:, t * c1 : (t + 1) * c1] = jnp.where(low_half, low, high).astype(BF16)
        half_give_ref[:, t * c1 : (t + 1) * c1] = jnp.where(low_half, high, low).astype(BF16)


def data_kernel(n_mp, d9, w2b_ref, keep_ref, give_ref, part):
    me = lax.axis_index("mp")
    _, f1, cells = part.shape
    chunk = chunk_of(cells)
    for base in range(0, cells, chunk):
        deltas = jnp.concatenate([d9[:, base + dz * PLANE : base + dz * PLANE + chunk] for dz in (2, 1, 0)], axis=0)
        part[:, :, base : base + chunk] = dot(w2b_ref[...], deltas).reshape(n_mp, f1, chunk)
    for k in range(n_mp):
        (give_ref if k % 2 else keep_ref)[k // 2] = part[me ^ k].astype(BF16)


def backward_kernel(n_mp, *refs):
    parts = refs[: n_mp // 2]
    pre_ref, vol_ref, w1b_ref, keep_ref, give_ref, grad_ref, d9, part, acc = refs[n_mp // 2 :]
    me = lax.axis_index("mp")
    f1, cells = pre_ref.shape
    c0 = vol_ref.shape[0]
    chunk = chunk_of(cells)
    steps = cells // chunk
    grid_xy = lane_grid(chunk)

    zero = jnp.zeros((d9.shape[0], PLANE), BF16)
    d9[:, :PLANE] = zero
    d9[:, PLANE + cells :] = zero

    reps = max(1, 128 // c0)
    span = reps * c0

    def take(base):
        total = parts[0][:, base : base + chunk].astype(F32)
        for other in parts[1:]:
            total = total + other[:, base : base + chunk].astype(F32)
        v = pre_ref[:, base : base + chunk]
        s = sigmoid(v)
        delta = (total * (s * (1.0 + v * (1.0 - s)))).astype(BF16).astype(F32)
        shifts = [moved(delta, grid_xy, 1 - dy, 1 - dx) for dy in range(3) for dx in range(3)]
        d9[:, base + PLANE : base + PLANE + chunk] = jnp.concatenate(shifts, axis=0).astype(BF16)

    def gradients(base):
        deltas = jnp.concatenate([d9[:, base + dz * PLANE : base + dz * PLANE + chunk] for dz in (2, 1, 0)], axis=0)
        part[:, :, base : base + chunk] = dot(w1b_ref[...], deltas).reshape(n_mp, c0 // n_mp, chunk)
        vol = vol_ref[:, base : base + chunk]
        g = dot_nt(deltas, jnp.concatenate([vol] * reps, axis=0))
        acc[...] = g if base == 0 else acc[...] + g

    for step in range(steps + 1):
        if step < steps:
            take(step * chunk)
        if step >= 1:
            gradients((step - 1) * chunk)
    for k in range(n_mp):
        (give_ref if k % 2 else keep_ref)[k // 2] = part[me ^ k].astype(BF16)

    lane = lax.broadcasted_iota(jnp.int32, (1, span), 1)
    for t in range(0, 27, reps):
        merged = acc[t * f1 : (t + 1) * f1]
        for r in range(1, min(reps, 27 - t)):
            merged = jnp.where(lane >= r * c0, acc[(t + r) * f1 : (t + r + 1) * f1], merged)
        width = min(span, (27 - t) * c0)
        grad_ref[:, t * c0 : t * c0 + width] = merged[:, :width].astype(BF16)


def place_kernel(scale, mine_ref, other_ref, out_ref):
    bit = lax.axis_index("sample") % 2
    width = out_ref.shape[2]
    out_ref[bit] = mine_ref[...].astype(F32) * scale
    out_ref[1 - bit] = other_ref[:, :width].astype(F32) * scale


def swap(value, axis, k):
    n = lax.axis_size(axis)
    return lax.ppermute(value, axis, [(i, i ^ k) for i in range(n)])


def add(a, b):
    return (a.astype(F32) + b.astype(F32)).astype(BF16)


def total(values):
    result = values[0].astype(F32)
    for value in values[1:]:
        result = result + value.astype(F32)
    return result


def sum_over_chips(keep, got):
    parts = [add(keep[j], got[j]) for j in range(keep.shape[0])]
    return [parts[0]] + [swap(parts[j], "mp", 2 * j) for j in range(1, len(parts))]


def bits_above(count):
    return [1 << i for i in range(1, count.bit_length() - 1)]


def call(kernel, out_shape, scratch, flops, nbytes):
    return pl.pallas_call(
        kernel,
        out_shape=out_shape,
        scratch_shapes=scratch,
        compiler_params=pltpu.CompilerParams(vmem_limit_bytes=VMEM_LIMIT),
        cost_estimate=pl.CostEstimate(flops=flops, bytes_accessed=nbytes, transcendentals=0),
    )


def local(volumes, w_first, w_second, cotangent):
    n_mp = lax.axis_size("mp")
    n_sample = lax.axis_size("sample")
    rows_in, _, cells = volumes.shape
    f1 = w_first.shape[0]
    f2 = w_second.shape[0]
    c0 = w_first.shape[1] // 27
    c1 = w_second.shape[1] // 27
    pitch = pitch_of(c0)
    scale = 1.0 / math.sqrt(n_sample * volumes.shape[1] * cells)
    volumes = volumes.reshape(rows_in, cells)
    cotangent = cotangent.reshape(f2, cells)
    padded = cells + 2 * PLANE

    lanes = (8 * 3 * c0) // 128 * 128 + pitch
    wide = max(cells, lanes)
    piece = jnp.concatenate(
        [
            jnp.pad(w_first, ((0, 0), (0, wide - w_first.shape[1]))),
            jnp.pad(volumes, ((0, 0), (0, wide - cells))),
        ],
        axis=0,
    )
    near = [piece] + [swap(piece, "mp", k) for k in range(2, n_mp, 2)]
    near = jnp.stack(near)
    far = swap(near, "mp", 1)

    w2t = w_second.reshape(f2, 3, 9, c1)
    w2r = jnp.transpose(w2t, (2, 0, 1, 3)).reshape(9 * f2, 3 * c1)
    w2b = jnp.transpose(w2t, (3, 1, 2, 0)).reshape(c1, 27 * f2)
    w1b = jnp.transpose(w_first.reshape(f1, 27, c0), (2, 1, 0)).reshape(c0, 27 * f1)

    sds = jax.ShapeDtypeStruct
    half = n_mp // 2
    features, pre_own, vol_all, d9, half_keep, half_give = call(
        functools.partial(forward_kernel, n_mp, c0),
        [
            sds((f2, cells), BF16),
            sds((f1, cells), F32),
            sds((c0, cells), BF16),
            sds((9 * f2, padded), BF16),
            sds((f2 // 2, 27 * c1), BF16),
            sds((f2 // 2, 27 * c1), BF16),
        ],
        [
            pltpu.VMEM((n_mp, rows_in, cells), F32),
            pltpu.VMEM((n_mp, f1, lanes), F32),
            pltpu.VMEM((pitch, padded), BF16),
            pltpu.VMEM((3 * c1, 3 * pitch), BF16),
            pltpu.VMEM((c1, padded), BF16),
            pltpu.VMEM((c1, cells), F32),
            pltpu.VMEM((27 * f2, c1), F32),
        ],
        2 * cells * 27 * (c0 * c1 + 2 * f2 * c1),
        4 * 1024 * 1024,
    )(near, far, w2r, cotangent)

    half_got = swap(half_give, "sample", 1)
    keep, give = call(
        functools.partial(data_kernel, n_mp),
        [sds((half, f1, cells), BF16), sds((half, f1, cells), BF16)],
        [pltpu.VMEM((n_mp, f1, cells), F32)],
        2 * cells * 27 * f2 * c1,
        2 * 1024 * 1024,
    )(d9, w2b)
    parts = sum_over_chips(keep, swap(give, "mp", 1))
    *parts, half_got = lax.optimization_barrier((*parts, half_got))
    half_sum = add(half_keep, half_got)
    bits = bits_above(n_sample)
    for bit in bits[:-1]:
        half_sum = add(half_sum, swap(half_sum, "sample", bit))
    half_got = swap(half_sum, "sample", bits[-1])

    keep, give, grad_first = call(
        functools.partial(backward_kernel, n_mp),
        [
            sds((half, rows_in, cells), BF16),
            sds((half, rows_in, cells), BF16),
            sds((f1, 27 * c0), BF16),
        ],
        [
            pltpu.VMEM((9 * f1, padded), BF16),
            pltpu.VMEM((n_mp, rows_in, cells), F32),
            pltpu.VMEM((27 * f1, max(1, 128 // c0) * c0), F32),
        ],
        2 * cells * 27 * 2 * c0 * f1,
        1024 * 1024,
    )(*parts, pre_own, vol_all, w1b)
    got = swap(give, "mp", 1)

    half_got, _ = lax.optimization_barrier((half_got, grad_first))
    half_sum = add(half_sum, half_got)
    got, half_sum = lax.optimization_barrier((got, half_sum))
    ins = sum_over_chips(keep, got)
    both = swap(jnp.concatenate([half_sum, grad_first], axis=1), "sample", 1)
    firsts = [grad_first] + [swap(grad_first, "sample", k) for k in range(2, n_sample)] + [both[:, 27 * c1 :]]
    grad_first = total(firsts) * scale
    grad_second = call(
        functools.partial(place_kernel, scale),
        sds((2, f2 // 2, 27 * c1), F32),
        [],
        0,
        1024 * 1024,
    )(half_sum, both).reshape(f2, 27 * c1)
    return (
        features.reshape(f2, 1, cells),
        total(ins).astype(BF16).reshape(rows_in, 1, cells),
        grad_first,
        grad_second,
    )


def solution(mesh):
    return jax.shard_map(
        local,
        mesh=mesh,
        in_specs=(P("mp", "sample", None), P("mp", None), P("mp", None), P("mp", "sample", None)),
        out_specs=(P("mp", "sample", None), P("mp", "sample", None), P("mp", None), P("mp", None)),
        check_vma=False,
    )
```

```python
import functools
import math

import jax
import jax.numpy as jnp
from jax import lax
from jax.experimental import pallas as pl
from jax.experimental.pallas import tpu as pltpu
from jax.sharding import PartitionSpec as P

SIDE = 16
PLANE = SIDE * SIDE
F32 = jnp.float32
BF16 = jnp.bfloat16
VMEM_LIMIT = 48 * 1024 * 1024
COVER = 10**12


def pitch_of(channels):
    width = 3 * channels
    slack = max((i * width) % 128 for i in range(9))
    return -(-(width + slack) // 128) * 128


def lane_grid(width):
    lane = lax.broadcasted_iota(jnp.int32, (1, width), 1)
    return lane % SIDE, (lane // SIDE) % SIDE


def inside(grid_xy, dy, dx):
    x, y = grid_xy
    ok = None
    for coord, step in ((y, dy), (x, dx)):
        if step < 0:
            now = coord >= -step
        elif step > 0:
            now = coord < SIDE - step
        else:
            continue
        ok = now if ok is None else ok & now
    return ok


def moved(values, grid_xy, dy, dx):
    if dy == 0 and dx == 0:
        return values
    width = values.shape[1]
    rolled = pltpu.roll(values, (-(dy * SIDE + dx)) % width, 1)
    return jnp.where(inside(grid_xy, dy, dx), rolled, 0.0)


def sigmoid(v):
    return 0.5 + 0.5 * jnp.tanh(0.5 * v)


def dot(a, b):
    return lax.dot_general(a, b, (((1,), (0,)), ((), ())), preferred_element_type=F32)


def dot_nt(a, b):
    return lax.dot_general(a, b, (((1,), (1,)), ((), ())), preferred_element_type=F32)


def chunk_of(cells):
    return 2 * PLANE if cells % (2 * PLANE) == 0 else PLANE


def forward_kernel(n_mp, c0, *refs):
    near_ref, far_ref, w2r_ref, cot_ref = refs[:4]
    feat_ref, pre_ref, vol_ref, d9, half_keep_ref, half_give_ref = refs[4:10]
    vs, w1s, v3, w1r, hid, pre, acc = refs[10:]

    me = lax.axis_index("mp")
    low_half = lax.axis_index("sample") % 2 == 0
    _, f1, lanes = w1s.shape
    c1 = n_mp * f1
    f2, cells = cot_ref.shape
    chunk = chunk_of(cells)
    steps = cells // chunk
    pitch = pitch_of(c0)
    grid_xy = lane_grid(chunk)

    for k in range(n_mp):
        piece = (far_ref if k % 2 else near_ref)[k // 2].astype(F32)
        slot = me ^ k
        w1s[slot] = piece[:f1, :lanes]
        vs[slot] = piece[f1:, :cells]

    lane = lax.broadcasted_iota(jnp.int32, (1, pitch), 1)
    for dz in range(3):
        for dy in range(3):
            start = (dz * 3 + dy) * 3 * c0
            low = start // 128 * 128
            block = w1s[:, :, low : low + pitch].reshape(c1, pitch)
            if start != low:
                block = pltpu.roll(block, pitch - (start - low), 1)
            block = jnp.where(lane < 3 * c0, block, 0.0)
            w1r[dy * c1 : (dy + 1) * c1, dz * pitch : (dz + 1) * pitch] = block.astype(BF16)

    for ref in (v3, hid, d9):
        zero = jnp.zeros((ref.shape[0], PLANE), BF16)
        ref[:, :PLANE] = zero
        ref[:, PLANE + cells :] = zero
    v3[3 * c0 :, PLANE : PLANE + cells] = jnp.zeros((pitch - 3 * c0, cells), BF16)

    for step in range(steps):
        base = step * chunk
        values = vs[:, :, base : base + chunk].reshape(c0, chunk)
        vol_ref[:, base : base + chunk] = values.astype(BF16)
        for dx in range(3):
            v3[dx * c0 : (dx + 1) * c0, base + PLANE : base + PLANE + chunk] = moved(values, grid_xy, 0, dx - 1).astype(BF16)

    def stacked(ref, base, order):
        return jnp.concatenate([ref[:, base + dz * PLANE : base + dz * PLANE + chunk] for dz in order], axis=0)

    def first_conv(base):
        z = dot(w1r[...], stacked(v3, base, (0, 1, 2)))
        total = z[c1 : 2 * c1]
        total = total + moved(z[:c1], grid_xy, -1, 0)
        total = total + moved(z[2 * c1 :], grid_xy, 1, 0)
        pre[:, base : base + chunk] = total
        hid[:, base + PLANE : base + PLANE + chunk] = (total * sigmoid(total)).astype(BF16)

    def second_conv(base):
        z = dot(w2r_ref[...], stacked(hid, base, (0, 1, 2)))
        total = None
        for dy in range(3):
            for dx in range(3):
                k = dy * 3 + dx
                term = moved(z[k * f2 : (k + 1) * f2], grid_xy, dy - 1, dx - 1)
                total = term if total is None else total + term
        s = sigmoid(total)
        feat_ref[:, base : base + chunk] = (total * s).astype(BF16)
        cot = cot_ref[:, base : base + chunk].astype(F32)
        delta = (cot * (s * (1.0 + total * (1.0 - s)))).astype(BF16).astype(F32)
        for dy in range(3):
            for dx in range(3):
                k = dy * 3 + dx
                d9[k * f2 : (k + 1) * f2, base + PLANE : base + PLANE + chunk] = moved(delta, grid_xy, 1 - dy, 1 - dx).astype(BF16)

    def gradients(base):
        deltas = stacked(d9, base, (2, 1, 0))
        g = dot_nt(deltas, hid[:, base + PLANE : base + PLANE + chunk])
        acc[...] = g if base == 0 else acc[...] + g

    for step in range(steps + 2):
        if step < steps:
            first_conv(step * chunk)
        if 1 <= step <= steps:
            second_conv((step - 1) * chunk)
        if step >= 2:
            gradients((step - 2) * chunk)

    pre_ref[...] = pre[pl.ds(pl.multiple_of(me * f1, f1), f1), :]
    half = f2 // 2
    for t in range(27):
        low = acc[t * f2 : t * f2 + half]
        high = acc[t * f2 + half : (t + 1) * f2]
        half_keep_ref[:, t * c1 : (t + 1) * c1] = jnp.where(low_half, low, high).astype(BF16)
        half_give_ref[:, t * c1 : (t + 1) * c1] = jnp.where(low_half, high, low).astype(BF16)


def data_kernel(n_mp, d9, w2b_ref, keep_ref, give_ref, part):
    me = lax.axis_index("mp")
    _, f1, cells = part.shape
    chunk = chunk_of(cells)
    for base in range(0, cells, chunk):
        deltas = jnp.concatenate([d9[:, base + dz * PLANE : base + dz * PLANE + chunk] for dz in (2, 1, 0)], axis=0)
        part[:, :, base : base + chunk] = dot(w2b_ref[...], deltas).reshape(n_mp, f1, chunk)
    for k in range(n_mp):
        (give_ref if k % 2 else keep_ref)[k // 2] = part[me ^ k].astype(BF16)


def backward_kernel(n_mp, *refs):
    parts = refs[: n_mp // 2]
    pre_ref, vol_ref, w1b_ref, keep_ref, give_ref, grad_ref, d9, part, acc = refs[n_mp // 2 :]
    me = lax.axis_index("mp")
    f1, cells = pre_ref.shape
    c0 = vol_ref.shape[0]
    chunk = chunk_of(cells)
    steps = cells // chunk
    grid_xy = lane_grid(chunk)

    zero = jnp.zeros((d9.shape[0], PLANE), BF16)
    d9[:, :PLANE] = zero
    d9[:, PLANE + cells :] = zero

    reps = max(1, 128 // c0)
    span = reps * c0

    def take(base):
        total = parts[0][:, base : base + chunk].astype(F32)
        for other in parts[1:]:
            total = total + other[:, base : base + chunk].astype(F32)
        v = pre_ref[:, base : base + chunk]
        s = sigmoid(v)
        delta = (total * (s * (1.0 + v * (1.0 - s)))).astype(BF16).astype(F32)
        shifts = [moved(delta, grid_xy, 1 - dy, 1 - dx) for dy in range(3) for dx in range(3)]
        d9[:, base + PLANE : base + PLANE + chunk] = jnp.concatenate(shifts, axis=0).astype(BF16)

    def gradients(base):
        deltas = jnp.concatenate([d9[:, base + dz * PLANE : base + dz * PLANE + chunk] for dz in (2, 1, 0)], axis=0)
        part[:, :, base : base + chunk] = dot(w1b_ref[...], deltas).reshape(n_mp, c0 // n_mp, chunk)
        vol = vol_ref[:, base : base + chunk]
        g = dot_nt(deltas, jnp.concatenate([vol] * reps, axis=0))
        acc[...] = g if base == 0 else acc[...] + g

    for step in range(steps + 1):
        if step < steps:
            take(step * chunk)
        if step >= 1:
            gradients((step - 1) * chunk)
    for k in range(n_mp):
        (give_ref if k % 2 else keep_ref)[k // 2] = part[me ^ k].astype(BF16)

    lane = lax.broadcasted_iota(jnp.int32, (1, span), 1)
    for t in range(0, 27, reps):
        merged = acc[t * f1 : (t + 1) * f1]
        for r in range(1, min(reps, 27 - t)):
            merged = jnp.where(lane >= r * c0, acc[(t + r) * f1 : (t + r + 1) * f1], merged)
        width = min(span, (27 - t) * c0)
        grad_ref[:, t * c0 : t * c0 + width] = merged[:, :width].astype(BF16)


def place_kernel(scale, mine_ref, other_ref, out_ref):
    bit = lax.axis_index("sample") % 2
    width = out_ref.shape[2]
    out_ref[bit] = mine_ref[...].astype(F32) * scale
    out_ref[1 - bit] = other_ref[:, :width].astype(F32) * scale


def swap(value, axis, k):
    n = lax.axis_size(axis)
    return lax.ppermute(value, axis, [(i, i ^ k) for i in range(n)])


def add(a, b):
    return (a.astype(F32) + b.astype(F32)).astype(BF16)


def total(values):
    result = values[0].astype(F32)
    for value in values[1:]:
        result = result + value.astype(F32)
    return result


def sum_over_chips(keep, got):
    parts = [add(keep[j], got[j]) for j in range(keep.shape[0])]
    return [parts[0]] + [swap(parts[j], "mp", 2 * j) for j in range(1, len(parts))]


def bits_above(count):
    return [1 << i for i in range(1, count.bit_length() - 1)]


def call(kernel, out_shape, scratch, flops, nbytes):
    return pl.pallas_call(
        kernel,
        out_shape=out_shape,
        scratch_shapes=scratch,
        compiler_params=pltpu.CompilerParams(vmem_limit_bytes=VMEM_LIMIT),
        cost_estimate=pl.CostEstimate(flops=flops, bytes_accessed=nbytes, transcendentals=0),
    )


def local(volumes, w_first, w_second, cotangent):
    n_mp = lax.axis_size("mp")
    n_sample = lax.axis_size("sample")
    rows_in, _, cells = volumes.shape
    f1 = w_first.shape[0]
    f2 = w_second.shape[0]
    c0 = w_first.shape[1] // 27
    c1 = w_second.shape[1] // 27
    pitch = pitch_of(c0)
    scale = 1.0 / math.sqrt(n_sample * volumes.shape[1] * cells)
    volumes = volumes.reshape(rows_in, cells)
    cotangent = cotangent.reshape(f2, cells)
    padded = cells + 2 * PLANE

    lanes = (8 * 3 * c0) // 128 * 128 + pitch
    wide = max(cells, lanes)
    piece = jnp.concatenate(
        [
            jnp.pad(w_first, ((0, 0), (0, wide - w_first.shape[1]))),
            jnp.pad(volumes, ((0, 0), (0, wide - cells))),
        ],
        axis=0,
    )
    near = [piece] + [swap(piece, "mp", k) for k in range(2, n_mp, 2)]
    near = jnp.stack(near)
    far = swap(near, "mp", 1)

    w2t = w_second.reshape(f2, 3, 9, c1)
    w2r = jnp.transpose(w2t, (2, 0, 1, 3)).reshape(9 * f2, 3 * c1)
    w2b = jnp.transpose(w2t, (3, 1, 2, 0)).reshape(c1, 27 * f2)
    w1b = jnp.transpose(w_first.reshape(f1, 27, c0), (2, 1, 0)).reshape(c0, 27 * f1)

    sds = jax.ShapeDtypeStruct
    half = n_mp // 2
    features, pre_own, vol_all, d9, half_keep, half_give = call(
        functools.partial(forward_kernel, n_mp, c0),
        [
            sds((f2, cells), BF16),
            sds((f1, cells), F32),
            sds((c0, cells), BF16),
            sds((9 * f2, padded), BF16),
            sds((f2 // 2, 27 * c1), BF16),
            sds((f2 // 2, 27 * c1), BF16),
        ],
        [
            pltpu.VMEM((n_mp, rows_in, cells), F32),
            pltpu.VMEM((n_mp, f1, lanes), F32),
            pltpu.VMEM((pitch, padded), BF16),
            pltpu.VMEM((3 * c1, 3 * pitch), BF16),
            pltpu.VMEM((c1, padded), BF16),
            pltpu.VMEM((c1, cells), F32),
            pltpu.VMEM((27 * f2, c1), F32),
        ],
        2 * cells * 27 * (c0 * c1 + 2 * f2 * c1),
        4 * 1024 * 1024,
    )(near, far, w2r, cotangent)

    half_got = swap(half_give, "sample", 1)
    keep, give = call(
        functools.partial(data_kernel, n_mp),
        [sds((half, f1, cells), BF16), sds((half, f1, cells), BF16)],
        [pltpu.VMEM((n_mp, f1, cells), F32)],
        2 * cells * 27 * f2 * c1,
        2 * 1024 * 1024,
    )(d9, w2b)
    parts = sum_over_chips(keep, swap(give, "mp", 1))
    half_sum = add(half_keep, half_got)
    bits = bits_above(n_sample)
    for bit in bits[:-1]:
        half_sum = add(half_sum, swap(half_sum, "sample", bit))
    half_got = swap(half_sum, "sample", bits[-1])

    keep, give, grad_first = call(
        functools.partial(backward_kernel, n_mp),
        [
            sds((half, rows_in, cells), BF16),
            sds((half, rows_in, cells), BF16),
            sds((f1, 27 * c0), BF16),
        ],
        [
            pltpu.VMEM((9 * f1, padded), BF16),
            pltpu.VMEM((n_mp, rows_in, cells), F32),
            pltpu.VMEM((27 * f1, max(1, 128 // c0) * c0), F32),
        ],
        COVER,
        1024 * 1024,
    )(*parts, pre_own, vol_all, w1b)
    got = swap(give, "mp", 1)
    ins = sum_over_chips(keep, got)
    input_grad = total(ins).astype(BF16)
    firsts = [grad_first] + [swap(grad_first, "sample", k) for k in range(1, n_sample)]
    grad_first = total(firsts) * scale

    half_sum = add(half_sum, half_got)
    both = swap(half_sum, "sample", 1)
    both, *_ = lax.optimization_barrier((both, grad_first, input_grad))
    grad_second = call(
        functools.partial(place_kernel, scale),
        sds((2, f2 // 2, 27 * c1), F32),
        [],
        0,
        1024 * 1024,
    )(half_sum, both).reshape(f2, 27 * c1)
    return (
        features.reshape(f2, 1, cells),
        input_grad.reshape(rows_in, 1, cells),
        grad_first,
        grad_second,
    )


def solution(mesh):
    return jax.shard_map(
        local,
        mesh=mesh,
        in_specs=(P("mp", "sample", None), P("mp", None), P("mp", None), P("mp", "sample", None)),
        out_specs=(P("mp", "sample", None), P("mp", "sample", None), P("mp", None), P("mp", None)),
        check_vma=False,
    )
```

```python
import functools
import math

import jax
import jax.numpy as jnp
from jax import lax
from jax.experimental import pallas as pl
from jax.experimental.pallas import tpu as pltpu
from jax.sharding import PartitionSpec as P

SIDE = 16
PLANE = SIDE * SIDE
F32 = jnp.float32
BF16 = jnp.bfloat16
VMEM_LIMIT = 48 * 1024 * 1024


def pitch_of(channels):
    width = 3 * channels
    slack = max((i * width) % 128 for i in range(9))
    return -(-(width + slack) // 128) * 128


def lane_grid(width):
    lane = lax.broadcasted_iota(jnp.int32, (1, width), 1)
    return lane % SIDE, (lane // SIDE) % SIDE


def inside(grid_xy, dy, dx):
    x, y = grid_xy
    ok = None
    for coord, step in ((y, dy), (x, dx)):
        if step < 0:
            now = coord >= -step
        elif step > 0:
            now = coord < SIDE - step
        else:
            continue
        ok = now if ok is None else ok & now
    return ok


def moved(values, grid_xy, dy, dx):
    if dy == 0 and dx == 0:
        return values
    width = values.shape[1]
    rolled = pltpu.roll(values, (-(dy * SIDE + dx)) % width, 1)
    return jnp.where(inside(grid_xy, dy, dx), rolled, 0.0)


def sigmoid(v):
    return 0.5 + 0.5 * jnp.tanh(0.5 * v)


def dot(a, b):
    return lax.dot_general(a, b, (((1,), (0,)), ((), ())), preferred_element_type=F32)


def dot_nt(a, b):
    return lax.dot_general(a, b, (((1,), (1,)), ((), ())), preferred_element_type=F32)


def chunk_of(cells):
    return 2 * PLANE if cells % (2 * PLANE) == 0 else PLANE


def forward_kernel(n_mp, c0, *refs):
    near_ref, far_ref, w2r_ref, w2b_ref, cot_ref = refs[:5]
    feat_ref, pre_ref, vol_ref, keep_ref, give_ref, grad_ref = refs[5:11]
    vs, w1s, v3, w1r, hid, pre, d9, part, acc = refs[11:]

    me = lax.axis_index("mp")
    f1 = w1s.shape[1]
    c1 = n_mp * f1
    f2, cells = cot_ref.shape
    chunk = chunk_of(cells)
    steps = cells // chunk
    pitch = pitch_of(c0)
    grid_xy = lane_grid(chunk)

    for k in range(n_mp):
        piece = (far_ref if k % 2 else near_ref)[k // 2].astype(F32)
        slot = me ^ k
        w1s[slot] = piece[:f1]
        vs[slot] = piece[f1:, :cells]

    lane = lax.broadcasted_iota(jnp.int32, (1, pitch), 1)
    for dz in range(3):
        for dy in range(3):
            start = (dz * 3 + dy) * 3 * c0
            low = start // 128 * 128
            block = w1s[:, :, low : low + pitch].reshape(c1, pitch)
            if start != low:
                block = pltpu.roll(block, pitch - (start - low), 1)
            block = jnp.where(lane < 3 * c0, block, 0.0)
            w1r[dy * c1 : (dy + 1) * c1, dz * pitch : (dz + 1) * pitch] = block.astype(BF16)

    for ref in (v3, hid, d9):
        zero = jnp.zeros((ref.shape[0], PLANE), BF16)
        ref[:, :PLANE] = zero
        ref[:, PLANE + cells :] = zero
    v3[3 * c0 :, PLANE : PLANE + cells] = jnp.zeros((pitch - 3 * c0, cells), BF16)

    for step in range(steps):
        base = step * chunk
        values = vs[:, :, base : base + chunk].reshape(c0, chunk)
        vol_ref[:, base : base + chunk] = values.astype(BF16)
        for dx in range(3):
            v3[dx * c0 : (dx + 1) * c0, base + PLANE : base + PLANE + chunk] = moved(values, grid_xy, 0, dx - 1).astype(BF16)

    def stacked(ref, base, order):
        return jnp.concatenate([ref[:, base + dz * PLANE : base + dz * PLANE + chunk] for dz in order], axis=0)

    def first_conv(base):
        z = dot(w1r[...], stacked(v3, base, (0, 1, 2)))
        total = z[c1 : 2 * c1]
        total = total + moved(z[:c1], grid_xy, -1, 0)
        total = total + moved(z[2 * c1 :], grid_xy, 1, 0)
        pre[:, base : base + chunk] = total
        hid[:, base + PLANE : base + PLANE + chunk] = (total * sigmoid(total)).astype(BF16)

    def second_conv(base):
        z = dot(w2r_ref[...], stacked(hid, base, (0, 1, 2)))
        total = None
        for dy in range(3):
            for dx in range(3):
                k = dy * 3 + dx
                term = moved(z[k * f2 : (k + 1) * f2], grid_xy, dy - 1, dx - 1)
                total = term if total is None else total + term
        s = sigmoid(total)
        feat_ref[:, base : base + chunk] = (total * s).astype(BF16)
        cot = cot_ref[:, base : base + chunk].astype(F32)
        delta = (cot * (s * (1.0 + total * (1.0 - s)))).astype(BF16).astype(F32)
        for dy in range(3):
            for dx in range(3):
                k = dy * 3 + dx
                d9[k * f2 : (k + 1) * f2, base + PLANE : base + PLANE + chunk] = moved(delta, grid_xy, 1 - dy, 1 - dx).astype(BF16)

    def gradients(base):
        deltas = stacked(d9, base, (2, 1, 0))
        part[:, :, base : base + chunk] = dot(w2b_ref[...], deltas).reshape(n_mp, f1, chunk)
        g = dot_nt(deltas, hid[:, base + PLANE : base + PLANE + chunk])
        acc[...] = g if base == 0 else acc[...] + g

    for step in range(steps + 2):
        if step < steps:
            first_conv(step * chunk)
        if 1 <= step <= steps:
            second_conv((step - 1) * chunk)
        if step >= 2:
            gradients((step - 2) * chunk)

    pre_ref[...] = pre[pl.ds(pl.multiple_of(me * f1, f1), f1), :]
    for k in range(n_mp):
        (give_ref if k % 2 else keep_ref)[k // 2] = part[me ^ k].astype(BF16)
    for t in range(27):
        grad_ref[:, t * c1 : (t + 1) * c1] = acc[t * f2 : (t + 1) * f2].astype(BF16)


def backward_kernel(n_mp, *refs):
    parts = refs[: n_mp // 2]
    pre_ref, vol_ref, w1b_ref, keep_ref, give_ref, grad_ref, d9, part, acc = refs[n_mp // 2 :]
    me = lax.axis_index("mp")
    f1, cells = pre_ref.shape
    c0 = vol_ref.shape[0]
    chunk = chunk_of(cells)
    steps = cells // chunk
    grid_xy = lane_grid(chunk)

    zero = jnp.zeros((d9.shape[0], PLANE), BF16)
    d9[:, :PLANE] = zero
    d9[:, PLANE + cells :] = zero

    reps = max(1, 128 // c0)
    span = reps * c0

    def take(base):
        total = parts[0][:, base : base + chunk].astype(F32)
        for other in parts[1:]:
            total = total + other[:, base : base + chunk].astype(F32)
        v = pre_ref[:, base : base + chunk]
        s = sigmoid(v)
        delta = (total * (s * (1.0 + v * (1.0 - s)))).astype(BF16).astype(F32)
        shifts = [moved(delta, grid_xy, 1 - dy, 1 - dx) for dy in range(3) for dx in range(3)]
        d9[:, base + PLANE : base + PLANE + chunk] = jnp.concatenate(shifts, axis=0).astype(BF16)

    def gradients(base):
        deltas = jnp.concatenate([d9[:, base + dz * PLANE : base + dz * PLANE + chunk] for dz in (2, 1, 0)], axis=0)
        part[:, :, base : base + chunk] = dot(w1b_ref[...], deltas).reshape(n_mp, c0 // n_mp, chunk)
        vol = vol_ref[:, base : base + chunk]
        g = dot_nt(deltas, jnp.concatenate([vol] * reps, axis=0))
        acc[...] = g if base == 0 else acc[...] + g

    for step in range(steps + 1):
        if step < steps:
            take(step * chunk)
        if step >= 1:
            gradients((step - 1) * chunk)
    for k in range(n_mp):
        (give_ref if k % 2 else keep_ref)[k // 2] = part[me ^ k].astype(BF16)

    lane = lax.broadcasted_iota(jnp.int32, (1, span), 1)
    for t in range(0, 27, reps):
        merged = acc[t * f1 : (t + 1) * f1]
        for r in range(1, min(reps, 27 - t)):
            merged = jnp.where(lane >= r * c0, acc[(t + r) * f1 : (t + r + 1) * f1], merged)
        width = min(span, (27 - t) * c0)
        grad_ref[:, t * c0 : t * c0 + width] = merged[:, :width].astype(BF16)


def swap(value, axis, k):
    n = lax.axis_size(axis)
    return lax.ppermute(value, axis, [(i, i ^ k) for i in range(n)])


def add(a, b):
    return (a.astype(F32) + b.astype(F32)).astype(BF16)


def sum_over_chips(keep, got):
    parts = [add(keep[j], got[j]) for j in range(keep.shape[0])]
    return [parts[0]] + [swap(parts[j], "mp", 2 * j) for j in range(1, len(parts))]


def bits_of(count):
    return [1 << i for i in reversed(range(count.bit_length() - 1))]


def call(kernel, out_shape, scratch, flops, nbytes):
    return pl.pallas_call(
        kernel,
        out_shape=out_shape,
        scratch_shapes=scratch,
        compiler_params=pltpu.CompilerParams(vmem_limit_bytes=VMEM_LIMIT),
        cost_estimate=pl.CostEstimate(flops=flops, bytes_accessed=nbytes, transcendentals=0),
    )


def local(volumes, w_first, w_second, cotangent):
    n_mp = lax.axis_size("mp")
    n_sample = lax.axis_size("sample")
    rows_in, _, cells = volumes.shape
    f1 = w_first.shape[0]
    f2 = w_second.shape[0]
    c0 = w_first.shape[1] // 27
    c1 = w_second.shape[1] // 27
    pitch = pitch_of(c0)
    scale = 1.0 / math.sqrt(n_sample * volumes.shape[1] * cells)
    volumes = volumes.reshape(rows_in, cells)
    cotangent = cotangent.reshape(f2, cells)
    padded = cells + 2 * PLANE

    need = (8 * 3 * c0) // 128 * 128 + pitch
    wide = max(cells, need)
    piece = jnp.concatenate(
        [
            jnp.pad(w_first, ((0, 0), (0, wide - w_first.shape[1]))),
            jnp.pad(volumes, ((0, 0), (0, wide - cells))),
        ],
        axis=0,
    )
    near = [piece] + [swap(piece, "mp", k) for k in range(2, n_mp, 2)]
    near = jnp.stack(near)
    far = swap(near, "mp", 1)

    w2t = w_second.reshape(f2, 3, 9, c1)
    w2r = jnp.transpose(w2t, (2, 0, 1, 3)).reshape(9 * f2, 3 * c1)
    w2b = jnp.transpose(w2t, (3, 1, 2, 0)).reshape(c1, 27 * f2)
    w1b = jnp.transpose(w_first.reshape(f1, 27, c0), (2, 1, 0)).reshape(c0, 27 * f1)

    sds = jax.ShapeDtypeStruct
    half = n_mp // 2
    features, pre_own, vol_all, keep, give, grad_second = call(
        functools.partial(forward_kernel, n_mp, c0),
        [
            sds((f2, cells), BF16),
            sds((f1, cells), F32),
            sds((c0, cells), BF16),
            sds((half, f1, cells), BF16),
            sds((half, f1, cells), BF16),
            sds((f2, 27 * c1), BF16),
        ],
        [
            pltpu.VMEM((n_mp, rows_in, cells), F32),
            pltpu.VMEM((n_mp, f1, wide), F32),
            pltpu.VMEM((pitch, padded), BF16),
            pltpu.VMEM((3 * c1, 3 * pitch), BF16),
            pltpu.VMEM((c1, padded), BF16),
            pltpu.VMEM((c1, cells), F32),
            pltpu.VMEM((9 * f2, padded), BF16),
            pltpu.VMEM((n_mp, f1, cells), F32),
            pltpu.VMEM((27 * f2, c1), F32),
        ],
        2 * cells * 27 * (c0 * c1 + 3 * f2 * c1),
        4 * 1024 * 1024,
    )(near, far, w2r, w2b, cotangent)

    bits = bits_of(n_sample)
    parts = sum_over_chips(keep, swap(give, "mp", 1))
    second_got = swap(grad_second, "sample", bits[0])

    keep, give, grad_first = call(
        functools.partial(backward_kernel, n_mp),
        [
            sds((half, rows_in, cells), BF16),
            sds((half, rows_in, cells), BF16),
            sds((f1, 27 * c0), BF16),
        ],
        [
            pltpu.VMEM((9 * f1, padded), BF16),
            pltpu.VMEM((n_mp, rows_in, cells), F32),
            pltpu.VMEM((27 * f1, max(1, 128 // c0) * c0), F32),
        ],
        2 * cells * 27 * 2 * c0 * f1,
        1024 * 1024,
    )(*parts, pre_own, vol_all, w1b)
    got = swap(give, "mp", 1)
    ins = sum_over_chips(keep, got)

    second_got, *_ = lax.optimization_barrier((second_got, grad_first))
    for bit in bits[::-1][:-1]:
        grad_first = add(grad_first, swap(grad_first, "sample", bit))
    first_got = swap(grad_first, "sample", bits[::-1][-1])
    for bit in bits[1:]:
        grad_second = add(grad_second, second_got)
        second_got = swap(grad_second, "sample", bit)
    grad_first = (grad_first.astype(F32) + first_got.astype(F32)) * scale
    grad_second = (grad_second.astype(F32) + second_got.astype(F32)) * scale
    total = ins[0].astype(F32)
    for other in ins[1:]:
        total = total + other.astype(F32)
    return (
        features.reshape(f2, 1, cells),
        total.astype(BF16).reshape(rows_in, 1, cells),
        grad_first,
        grad_second,
    )


def solution(mesh):
    return jax.shard_map(
        local,
        mesh=mesh,
        in_specs=(P("mp", "sample", None), P("mp", None), P("mp", None), P("mp", "sample", None)),
        out_specs=(P("mp", "sample", None), P("mp", "sample", None), P("mp", None), P("mp", None)),
        check_vma=False,
    )
```

```python
import functools
import math

import jax
import jax.numpy as jnp
from jax import lax
from jax.experimental import pallas as pl
from jax.experimental.pallas import tpu as pltpu
from jax.sharding import PartitionSpec as P

SIDE = 16
PLANE = SIDE * SIDE
F32 = jnp.float32
BF16 = jnp.bfloat16
VMEM_LIMIT = 48 * 1024 * 1024


def pitch_of(channels):
    width = 3 * channels
    slack = max((i * width) % 128 for i in range(9))
    return -(-(width + slack) // 128) * 128


def lane_grid(width):
    lane = lax.broadcasted_iota(jnp.int32, (1, width), 1)
    return lane % SIDE, (lane // SIDE) % SIDE


def inside(grid_xy, dy, dx):
    x, y = grid_xy
    ok = None
    for coord, step in ((y, dy), (x, dx)):
        if step < 0:
            now = coord >= -step
        elif step > 0:
            now = coord < SIDE - step
        else:
            continue
        ok = now if ok is None else ok & now
    return ok


def moved(values, grid_xy, dy, dx):
    if dy == 0 and dx == 0:
        return values
    width = values.shape[1]
    rolled = pltpu.roll(values, (-(dy * SIDE + dx)) % width, 1)
    return jnp.where(inside(grid_xy, dy, dx), rolled, 0.0)


def sigmoid(v):
    return 0.5 + 0.5 * jnp.tanh(0.5 * v)


def dot(a, b):
    return lax.dot_general(a, b, (((1,), (0,)), ((), ())), preferred_element_type=F32)


def dot_nt(a, b):
    return lax.dot_general(a, b, (((1,), (1,)), ((), ())), preferred_element_type=F32)


def chunk_of(cells):
    return PLANE


def forward_kernel(n_mp, c0, *refs):
    near_ref, far_ref, w2r_ref, w2b_ref, cot_ref = refs[:5]
    feat_ref, pre_ref, vol_ref, keep_ref, give_ref, grad_ref = refs[5:11]
    vs, w1s, v3, w1r, hid, pre, d9, part, acc = refs[11:]

    me = lax.axis_index("mp")
    f1 = w1s.shape[1]
    c1 = n_mp * f1
    f2, cells = cot_ref.shape
    chunk = chunk_of(cells)
    steps = cells // chunk
    pitch = pitch_of(c0)
    grid_xy = lane_grid(chunk)

    for k in range(n_mp):
        piece = (far_ref if k % 2 else near_ref)[k // 2].astype(F32)
        slot = me ^ k
        w1s[slot] = piece[:f1]
        vs[slot] = piece[f1:, :cells]

    lane = lax.broadcasted_iota(jnp.int32, (1, pitch), 1)
    for dz in range(3):
        for dy in range(3):
            start = (dz * 3 + dy) * 3 * c0
            low = start // 128 * 128
            block = w1s[:, :, low : low + pitch].reshape(c1, pitch)
            if start != low:
                block = pltpu.roll(block, pitch - (start - low), 1)
            block = jnp.where(lane < 3 * c0, block, 0.0)
            w1r[dy * c1 : (dy + 1) * c1, dz * pitch : (dz + 1) * pitch] = block.astype(BF16)

    for ref in (v3, hid, d9):
        zero = jnp.zeros((ref.shape[0], PLANE), BF16)
        ref[:, :PLANE] = zero
        ref[:, PLANE + cells :] = zero
    v3[3 * c0 :, PLANE : PLANE + cells] = jnp.zeros((pitch - 3 * c0, cells), BF16)

    for step in range(steps):
        base = step * chunk
        values = vs[:, :, base : base + chunk].reshape(c0, chunk)
        vol_ref[:, base : base + chunk] = values.astype(BF16)
        for dx in range(3):
            v3[dx * c0 : (dx + 1) * c0, base + PLANE : base + PLANE + chunk] = moved(values, grid_xy, 0, dx - 1).astype(BF16)

    def stacked(ref, base, order):
        return jnp.concatenate([ref[:, base + dz * PLANE : base + dz * PLANE + chunk] for dz in order], axis=0)

    def first_conv(base):
        z = dot(w1r[...], stacked(v3, base, (0, 1, 2)))
        total = z[c1 : 2 * c1]
        total = total + moved(z[:c1], grid_xy, -1, 0)
        total = total + moved(z[2 * c1 :], grid_xy, 1, 0)
        pre[:, base : base + chunk] = total
        hid[:, base + PLANE : base + PLANE + chunk] = (total * sigmoid(total)).astype(BF16)

    def second_conv(base):
        z = dot(w2r_ref[...], stacked(hid, base, (0, 1, 2)))
        total = None
        for dy in range(3):
            for dx in range(3):
                k = dy * 3 + dx
                term = moved(z[k * f2 : (k + 1) * f2], grid_xy, dy - 1, dx - 1)
                total = term if total is None else total + term
        s = sigmoid(total)
        feat_ref[:, base : base + chunk] = (total * s).astype(BF16)
        cot = cot_ref[:, base : base + chunk].astype(F32)
        delta = (cot * (s * (1.0 + total * (1.0 - s)))).astype(BF16).astype(F32)
        for dy in range(3):
            for dx in range(3):
                k = dy * 3 + dx
                d9[k * f2 : (k + 1) * f2, base + PLANE : base + PLANE + chunk] = moved(delta, grid_xy, 1 - dy, 1 - dx).astype(BF16)

    def gradients(base):
        deltas = stacked(d9, base, (2, 1, 0))
        part[:, :, base : base + chunk] = dot(w2b_ref[...], deltas).reshape(n_mp, f1, chunk)
        g = dot_nt(deltas, hid[:, base + PLANE : base + PLANE + chunk])
        acc[...] = g if base == 0 else acc[...] + g

    for step in range(steps + 2):
        if step < steps:
            first_conv(step * chunk)
        if 1 <= step <= steps:
            second_conv((step - 1) * chunk)
        if step >= 2:
            gradients((step - 2) * chunk)

    pre_ref[...] = pre[pl.ds(pl.multiple_of(me * f1, f1), f1), :]
    for k in range(n_mp):
        (give_ref if k % 2 else keep_ref)[k // 2] = part[me ^ k].astype(BF16)
    for t in range(27):
        grad_ref[:, t * c1 : (t + 1) * c1] = acc[t * f2 : (t + 1) * f2].astype(BF16)


def backward_kernel(n_mp, *refs):
    parts = refs[: n_mp // 2]
    pre_ref, vol_ref, w1b_ref, keep_ref, give_ref, grad_ref, d9, part, acc = refs[n_mp // 2 :]
    me = lax.axis_index("mp")
    f1, cells = pre_ref.shape
    c0 = vol_ref.shape[0]
    chunk = chunk_of(cells)
    steps = cells // chunk
    grid_xy = lane_grid(chunk)

    zero = jnp.zeros((d9.shape[0], PLANE), BF16)
    d9[:, :PLANE] = zero
    d9[:, PLANE + cells :] = zero

    reps = max(1, 128 // c0)
    span = reps * c0

    def take(base):
        total = parts[0][:, base : base + chunk].astype(F32)
        for other in parts[1:]:
            total = total + other[:, base : base + chunk].astype(F32)
        v = pre_ref[:, base : base + chunk]
        s = sigmoid(v)
        delta = (total * (s * (1.0 + v * (1.0 - s)))).astype(BF16).astype(F32)
        shifts = [moved(delta, grid_xy, 1 - dy, 1 - dx) for dy in range(3) for dx in range(3)]
        d9[:, base + PLANE : base + PLANE + chunk] = jnp.concatenate(shifts, axis=0).astype(BF16)

    def gradients(base):
        deltas = jnp.concatenate([d9[:, base + dz * PLANE : base + dz * PLANE + chunk] for dz in (2, 1, 0)], axis=0)
        part[:, :, base : base + chunk] = dot(w1b_ref[...], deltas).reshape(n_mp, c0 // n_mp, chunk)
        vol = vol_ref[:, base : base + chunk]
        g = dot_nt(deltas, jnp.concatenate([vol] * reps, axis=0))
        acc[...] = g if base == 0 else acc[...] + g

    for step in range(steps + 1):
        if step < steps:
            take(step * chunk)
        if step >= 1:
            gradients((step - 1) * chunk)
    for k in range(n_mp):
        (give_ref if k % 2 else keep_ref)[k // 2] = part[me ^ k].astype(BF16)

    lane = lax.broadcasted_iota(jnp.int32, (1, span), 1)
    for t in range(0, 27, reps):
        merged = acc[t * f1 : (t + 1) * f1]
        for r in range(1, min(reps, 27 - t)):
            merged = jnp.where(lane >= r * c0, acc[(t + r) * f1 : (t + r + 1) * f1], merged)
        width = min(span, (27 - t) * c0)
        grad_ref[:, t * c0 : t * c0 + width] = merged[:, :width].astype(BF16)


def finish_kernel(scale, count, *refs):
    ins = refs[:count]
    first_ref, first_got_ref, second_ref, second_got_ref, feat_in_ref = refs[count : count + 5]
    feat_ref, input_ref, first_out_ref, second_out_ref = refs[count + 5 :]
    second_out_ref[...] = (second_ref[...].astype(F32) + second_got_ref[...].astype(F32)) * scale
    feat_ref[...] = feat_in_ref[...]
    first_out_ref[...] = (first_ref[...].astype(F32) + first_got_ref[...].astype(F32)) * scale
    total = ins[0][...].astype(F32)
    for other in ins[1:]:
        total = total + other[...].astype(F32)
    input_ref[...] = total.astype(BF16)


def swap(value, axis, k):
    n = lax.axis_size(axis)
    return lax.ppermute(value, axis, [(i, i ^ k) for i in range(n)])


def add(a, b):
    return (a.astype(F32) + b.astype(F32)).astype(BF16)


def sum_over_chips(keep, got):
    parts = [add(keep[j], got[j]) for j in range(keep.shape[0])]
    return [parts[0]] + [swap(parts[j], "mp", 2 * j) for j in range(1, len(parts))]


def bits_of(count):
    return [1 << i for i in reversed(range(count.bit_length() - 1))]


def call(kernel, out_shape, scratch, flops, nbytes):
    return pl.pallas_call(
        kernel,
        out_shape=out_shape,
        scratch_shapes=scratch,
        compiler_params=pltpu.CompilerParams(vmem_limit_bytes=VMEM_LIMIT),
        cost_estimate=pl.CostEstimate(flops=flops, bytes_accessed=nbytes, transcendentals=0),
    )


def local(volumes, w_first, w_second, cotangent):
    n_mp = lax.axis_size("mp")
    n_sample = lax.axis_size("sample")
    rows_in, _, cells = volumes.shape
    f1 = w_first.shape[0]
    f2 = w_second.shape[0]
    c0 = w_first.shape[1] // 27
    c1 = w_second.shape[1] // 27
    pitch = pitch_of(c0)
    scale = 1.0 / math.sqrt(n_sample * volumes.shape[1] * cells)
    volumes = volumes.reshape(rows_in, cells)
    cotangent = cotangent.reshape(f2, cells)
    padded = cells + 2 * PLANE

    need = (8 * 3 * c0) // 128 * 128 + pitch
    wide = max(cells, need)
    piece = jnp.concatenate(
        [
            jnp.pad(w_first, ((0, 0), (0, wide - w_first.shape[1]))),
            jnp.pad(volumes, ((0, 0), (0, wide - cells))),
        ],
        axis=0,
    )
    near = [piece] + [swap(piece, "mp", k) for k in range(2, n_mp, 2)]
    near = jnp.stack(near)
    far = swap(near, "mp", 1)

    w2t = w_second.reshape(f2, 3, 9, c1)
    w2r = jnp.transpose(w2t, (2, 0, 1, 3)).reshape(9 * f2, 3 * c1)
    w2b = jnp.transpose(w2t, (3, 1, 2, 0)).reshape(c1, 27 * f2)
    w1b = jnp.transpose(w_first.reshape(f1, 27, c0), (2, 1, 0)).reshape(c0, 27 * f1)

    sds = jax.ShapeDtypeStruct
    half = n_mp // 2
    features, pre_own, vol_all, keep, give, grad_second = call(
        functools.partial(forward_kernel, n_mp, c0),
        [
            sds((f2, cells), BF16),
            sds((f1, cells), F32),
            sds((c0, cells), BF16),
            sds((half, f1, cells), BF16),
            sds((half, f1, cells), BF16),
            sds((f2, 27 * c1), BF16),
        ],
        [
            pltpu.VMEM((n_mp, rows_in, cells), F32),
            pltpu.VMEM((n_mp, f1, wide), F32),
            pltpu.VMEM((pitch, padded), BF16),
            pltpu.VMEM((3 * c1, 3 * pitch), BF16),
            pltpu.VMEM((c1, padded), BF16),
            pltpu.VMEM((c1, cells), F32),
            pltpu.VMEM((9 * f2, padded), BF16),
            pltpu.VMEM((n_mp, f1, cells), F32),
            pltpu.VMEM((27 * f2, c1), F32),
        ],
        2 * cells * 27 * (c0 * c1 + 3 * f2 * c1),
        4 * 1024 * 1024,
    )(near, far, w2r, w2b, cotangent)

    bits = bits_of(n_sample)
    parts = sum_over_chips(keep, swap(give, "mp", 1))
    second_got = swap(grad_second, "sample", bits[0])

    keep, give, grad_first = call(
        functools.partial(backward_kernel, n_mp),
        [
            sds((half, rows_in, cells), BF16),
            sds((half, rows_in, cells), BF16),
            sds((f1, 27 * c0), BF16),
        ],
        [
            pltpu.VMEM((9 * f1, padded), BF16),
            pltpu.VMEM((n_mp, rows_in, cells), F32),
            pltpu.VMEM((27 * f1, max(1, 128 // c0) * c0), F32),
        ],
        2 * cells * 27 * 2 * c0 * f1,
        1024 * 1024,
    )(*parts, pre_own, vol_all, w1b)
    got = swap(give, "mp", 1)
    ins = sum_over_chips(keep, got)

    second_got, *_ = lax.optimization_barrier((second_got, grad_first))
    for bit in bits[::-1][:-1]:
        grad_first = add(grad_first, swap(grad_first, "sample", bit))
    first_got = swap(grad_first, "sample", bits[::-1][-1])
    for bit in bits[1:]:
        grad_second = add(grad_second, second_got)
        second_got = swap(grad_second, "sample", bit)
    features, input_grad, grad_first, grad_second = call(
        functools.partial(finish_kernel, scale, half),
        [
            sds((f2, cells), BF16),
            sds((rows_in, cells), BF16),
            sds((f1, 27 * c0), F32),
            sds((f2, 27 * c1), F32),
        ],
        [],
        0,
        2 * 1024 * 1024,
    )(*ins, grad_first, first_got, grad_second, second_got, features)
    return (
        features.reshape(f2, 1, cells),
        input_grad.reshape(rows_in, 1, cells),
        grad_first,
        grad_second,
    )


def solution(mesh):
    return jax.shard_map(
        local,
        mesh=mesh,
        in_specs=(P("mp", "sample", None), P("mp", None), P("mp", None), P("mp", "sample", None)),
        out_specs=(P("mp", "sample", None), P("mp", "sample", None), P("mp", None), P("mp", None)),
        check_vma=False,
    )
```

```python
import functools
import math

import jax
import jax.numpy as jnp
from jax import lax
from jax.experimental import pallas as pl
from jax.experimental.pallas import tpu as pltpu
from jax.sharding import PartitionSpec as P

SIDE = 16
PLANE = SIDE * SIDE
F32 = jnp.float32
BF16 = jnp.bfloat16
VMEM_LIMIT = 48 * 1024 * 1024


def pitch_of(channels):
    width = 3 * channels
    slack = max((i * width) % 128 for i in range(9))
    return -(-(width + slack) // 128) * 128


def lane_grid(width):
    lane = lax.broadcasted_iota(jnp.int32, (1, width), 1)
    return lane % SIDE, (lane // SIDE) % SIDE


def inside(grid_xy, dy, dx):
    x, y = grid_xy
    ok = None
    for coord, step in ((y, dy), (x, dx)):
        if step < 0:
            now = coord >= -step
        elif step > 0:
            now = coord < SIDE - step
        else:
            continue
        ok = now if ok is None else ok & now
    return ok


def moved(values, grid_xy, dy, dx):
    if dy == 0 and dx == 0:
        return values
    width = values.shape[1]
    rolled = pltpu.roll(values, (-(dy * SIDE + dx)) % width, 1)
    return jnp.where(inside(grid_xy, dy, dx), rolled, 0.0)


def sigmoid(v):
    return 0.5 + 0.5 * jnp.tanh(0.5 * v)


def dot(a, b):
    return lax.dot_general(a, b, (((1,), (0,)), ((), ())), preferred_element_type=F32)


def dot_nt(a, b):
    return lax.dot_general(a, b, (((1,), (1,)), ((), ())), preferred_element_type=F32)


def chunk_of(cells, planes):
    while cells % (planes * PLANE):
        planes //= 2
    return planes * PLANE


def forward_kernel(n_mp, c0, *refs):
    near_ref, far_ref, w2r_ref, w2b_ref, cot_ref = refs[:5]
    feat_ref, pre_ref, vol_ref, keep_ref, give_ref, grad_ref = refs[5:11]
    vs, w1s, v3, w1r, hid, pre, d9, part, acc = refs[11:]

    me = lax.axis_index("mp")
    f1 = w1s.shape[1]
    c1 = n_mp * f1
    f2, cells = cot_ref.shape
    chunk = chunk_of(cells, 4)
    steps = cells // chunk
    pitch = pitch_of(c0)
    grid_xy = lane_grid(chunk)

    for k in range(n_mp):
        piece = (far_ref if k % 2 else near_ref)[k // 2].astype(F32)
        slot = me ^ k
        w1s[slot] = piece[:f1]
        vs[slot] = piece[f1:, :cells]

    lane = lax.broadcasted_iota(jnp.int32, (1, pitch), 1)
    for dz in range(3):
        for dy in range(3):
            start = (dz * 3 + dy) * 3 * c0
            low = start // 128 * 128
            block = w1s[:, :, low : low + pitch].reshape(c1, pitch)
            if start != low:
                block = pltpu.roll(block, pitch - (start - low), 1)
            block = jnp.where(lane < 3 * c0, block, 0.0)
            w1r[dy * c1 : (dy + 1) * c1, dz * pitch : (dz + 1) * pitch] = block.astype(BF16)

    for ref in (v3, hid, d9):
        zero = jnp.zeros((ref.shape[0], PLANE), BF16)
        ref[:, :PLANE] = zero
        ref[:, PLANE + cells :] = zero
    v3[3 * c0 :, PLANE : PLANE + cells] = jnp.zeros((pitch - 3 * c0, cells), BF16)

    for step in range(steps):
        base = step * chunk
        values = vs[:, :, base : base + chunk].reshape(c0, chunk)
        vol_ref[:, base : base + chunk] = values.astype(BF16)
        for dx in range(3):
            v3[dx * c0 : (dx + 1) * c0, base + PLANE : base + PLANE + chunk] = moved(values, grid_xy, 0, dx - 1).astype(BF16)

    def stacked(ref, base, order):
        return jnp.concatenate([ref[:, base + dz * PLANE : base + dz * PLANE + chunk] for dz in order], axis=0)

    def first_conv(base):
        z = dot(w1r[...], stacked(v3, base, (0, 1, 2)))
        total = z[c1 : 2 * c1]
        total = total + moved(z[:c1], grid_xy, -1, 0)
        total = total + moved(z[2 * c1 :], grid_xy, 1, 0)
        pre[:, base : base + chunk] = total
        hid[:, base + PLANE : base + PLANE + chunk] = (total * sigmoid(total)).astype(BF16)

    def second_conv(base):
        z = dot(w2r_ref[...], stacked(hid, base, (0, 1, 2)))
        total = None
        for dy in range(3):
            for dx in range(3):
                k = dy * 3 + dx
                term = moved(z[k * f2 : (k + 1) * f2], grid_xy, dy - 1, dx - 1)
                total = term if total is None else total + term
        s = sigmoid(total)
        feat_ref[:, base : base + chunk] = (total * s).astype(BF16)
        cot = cot_ref[:, base : base + chunk].astype(F32)
        delta = (cot * (s * (1.0 + total * (1.0 - s)))).astype(BF16).astype(F32)
        for dy in range(3):
            for dx in range(3):
                k = dy * 3 + dx
                d9[k * f2 : (k + 1) * f2, base + PLANE : base + PLANE + chunk] = moved(delta, grid_xy, 1 - dy, 1 - dx).astype(BF16)

    def gradients(base):
        deltas = stacked(d9, base, (2, 1, 0))
        part[:, :, base : base + chunk] = dot(w2b_ref[...], deltas).reshape(n_mp, f1, chunk)
        g = dot_nt(deltas, hid[:, base + PLANE : base + PLANE + chunk])
        acc[...] = g if base == 0 else acc[...] + g

    for step in range(steps + 2):
        if step < steps:
            first_conv(step * chunk)
        if 1 <= step <= steps:
            second_conv((step - 1) * chunk)
        if step >= 2:
            gradients((step - 2) * chunk)

    pre_ref[...] = pre[pl.ds(pl.multiple_of(me * f1, f1), f1), :]
    for k in range(n_mp):
        (give_ref if k % 2 else keep_ref)[k // 2] = part[me ^ k].astype(BF16)
    for t in range(27):
        grad_ref[:, t * c1 : (t + 1) * c1] = acc[t * f2 : (t + 1) * f2].astype(BF16)


def backward_kernel(n_mp, *refs):
    parts = refs[: n_mp // 2]
    pre_ref, vol_ref, w1b_ref, keep_ref, give_ref, grad_ref, d9, part, acc = refs[n_mp // 2 :]
    me = lax.axis_index("mp")
    f1, cells = pre_ref.shape
    c0 = vol_ref.shape[0]
    chunk = chunk_of(cells, 1)
    steps = cells // chunk
    grid_xy = lane_grid(chunk)

    zero = jnp.zeros((d9.shape[0], PLANE), BF16)
    d9[:, :PLANE] = zero
    d9[:, PLANE + cells :] = zero

    reps = max(1, 128 // c0)
    span = reps * c0

    def take(base):
        total = parts[0][:, base : base + chunk].astype(F32)
        for other in parts[1:]:
            total = total + other[:, base : base + chunk].astype(F32)
        v = pre_ref[:, base : base + chunk]
        s = sigmoid(v)
        delta = (total * (s * (1.0 + v * (1.0 - s)))).astype(BF16).astype(F32)
        shifts = [moved(delta, grid_xy, 1 - dy, 1 - dx) for dy in range(3) for dx in range(3)]
        d9[:, base + PLANE : base + PLANE + chunk] = jnp.concatenate(shifts, axis=0).astype(BF16)

    def gradients(base):
        deltas = jnp.concatenate([d9[:, base + dz * PLANE : base + dz * PLANE + chunk] for dz in (2, 1, 0)], axis=0)
        part[:, :, base : base + chunk] = dot(w1b_ref[...], deltas).reshape(n_mp, c0 // n_mp, chunk)
        vol = vol_ref[:, base : base + chunk]
        g = dot_nt(deltas, jnp.concatenate([vol] * reps, axis=0))
        acc[...] = g if base == 0 else acc[...] + g

    for step in range(steps + 1):
        if step < steps:
            take(step * chunk)
        if step >= 1:
            gradients((step - 1) * chunk)
    for k in range(n_mp):
        (give_ref if k % 2 else keep_ref)[k // 2] = part[me ^ k].astype(BF16)

    lane = lax.broadcasted_iota(jnp.int32, (1, span), 1)
    for t in range(0, 27, reps):
        merged = acc[t * f1 : (t + 1) * f1]
        for r in range(1, min(reps, 27 - t)):
            merged = jnp.where(lane >= r * c0, acc[(t + r) * f1 : (t + r + 1) * f1], merged)
        width = min(span, (27 - t) * c0)
        grad_ref[:, t * c0 : t * c0 + width] = merged[:, :width].astype(BF16)


def finish_kernel(scale, count, *refs):
    ins = refs[:count]
    first_ref, first_got_ref, second_ref, second_got_ref, feat_in_ref = refs[count : count + 5]
    feat_ref, input_ref, first_out_ref, second_out_ref = refs[count + 5 :]
    second_out_ref[...] = (second_ref[...].astype(F32) + second_got_ref[...].astype(F32)) * scale
    feat_ref[...] = feat_in_ref[...]
    first_out_ref[...] = (first_ref[...].astype(F32) + first_got_ref[...].astype(F32)) * scale
    total = ins[0][...].astype(F32)
    for other in ins[1:]:
        total = total + other[...].astype(F32)
    input_ref[...] = total.astype(BF16)


def swap(value, axis, k):
    n = lax.axis_size(axis)
    return lax.ppermute(value, axis, [(i, i ^ k) for i in range(n)])


def add(a, b):
    return (a.astype(F32) + b.astype(F32)).astype(BF16)


def sum_over_chips(keep, got):
    parts = [add(keep[j], got[j]) for j in range(keep.shape[0])]
    return [parts[0]] + [swap(parts[j], "mp", 2 * j) for j in range(1, len(parts))]


def bits_of(count):
    return [1 << i for i in reversed(range(count.bit_length() - 1))]


def call(kernel, out_shape, scratch, flops, nbytes):
    return pl.pallas_call(
        kernel,
        out_shape=out_shape,
        scratch_shapes=scratch,
        compiler_params=pltpu.CompilerParams(vmem_limit_bytes=VMEM_LIMIT),
        cost_estimate=pl.CostEstimate(flops=flops, bytes_accessed=nbytes, transcendentals=0),
    )


def local(volumes, w_first, w_second, cotangent):
    n_mp = lax.axis_size("mp")
    n_sample = lax.axis_size("sample")
    rows_in, _, cells = volumes.shape
    f1 = w_first.shape[0]
    f2 = w_second.shape[0]
    c0 = w_first.shape[1] // 27
    c1 = w_second.shape[1] // 27
    pitch = pitch_of(c0)
    scale = 1.0 / math.sqrt(n_sample * volumes.shape[1] * cells)
    volumes = volumes.reshape(rows_in, cells)
    cotangent = cotangent.reshape(f2, cells)
    padded = cells + 2 * PLANE

    need = (8 * 3 * c0) // 128 * 128 + pitch
    wide = max(cells, need)
    piece = jnp.concatenate(
        [
            jnp.pad(w_first, ((0, 0), (0, wide - w_first.shape[1]))),
            jnp.pad(volumes, ((0, 0), (0, wide - cells))),
        ],
        axis=0,
    )
    near = [piece] + [swap(piece, "mp", k) for k in range(2, n_mp, 2)]
    near = jnp.stack(near)
    far = swap(near, "mp", 1)

    w2t = w_second.reshape(f2, 3, 9, c1)
    w2r = jnp.transpose(w2t, (2, 0, 1, 3)).reshape(9 * f2, 3 * c1)
    w2b = jnp.transpose(w2t, (3, 1, 2, 0)).reshape(c1, 27 * f2)
    w1b = jnp.transpose(w_first.reshape(f1, 27, c0), (2, 1, 0)).reshape(c0, 27 * f1)

    sds = jax.ShapeDtypeStruct
    half = n_mp // 2
    features, pre_own, vol_all, keep, give, grad_second = call(
        functools.partial(forward_kernel, n_mp, c0),
        [
            sds((f2, cells), BF16),
            sds((f1, cells), F32),
            sds((c0, cells), BF16),
            sds((half, f1, cells), BF16),
            sds((half, f1, cells), BF16),
            sds((f2, 27 * c1), BF16),
        ],
        [
            pltpu.VMEM((n_mp, rows_in, cells), F32),
            pltpu.VMEM((n_mp, f1, wide), F32),
            pltpu.VMEM((pitch, padded), BF16),
            pltpu.VMEM((3 * c1, 3 * pitch), BF16),
            pltpu.VMEM((c1, padded), BF16),
            pltpu.VMEM((c1, cells), F32),
            pltpu.VMEM((9 * f2, padded), BF16),
            pltpu.VMEM((n_mp, f1, cells), F32),
            pltpu.VMEM((27 * f2, c1), F32),
        ],
        2 * cells * 27 * (c0 * c1 + 3 * f2 * c1),
        4 * 1024 * 1024,
    )(near, far, w2r, w2b, cotangent)

    bits = bits_of(n_sample)
    parts = sum_over_chips(keep, swap(give, "mp", 1))
    second_got = swap(grad_second, "sample", bits[0])

    keep, give, grad_first = call(
        functools.partial(backward_kernel, n_mp),
        [
            sds((half, rows_in, cells), BF16),
            sds((half, rows_in, cells), BF16),
            sds((f1, 27 * c0), BF16),
        ],
        [
            pltpu.VMEM((9 * f1, padded), BF16),
            pltpu.VMEM((n_mp, rows_in, cells), F32),
            pltpu.VMEM((27 * f1, max(1, 128 // c0) * c0), F32),
        ],
        2 * cells * 27 * 2 * c0 * f1,
        1024 * 1024,
    )(*parts, pre_own, vol_all, w1b)
    got = swap(give, "mp", 1)
    ins = sum_over_chips(keep, got)

    second_got, *_ = lax.optimization_barrier((second_got, grad_first))
    for bit in bits[::-1][:-1]:
        grad_first = add(grad_first, swap(grad_first, "sample", bit))
    first_got = swap(grad_first, "sample", bits[::-1][-1])
    for bit in bits[1:]:
        grad_second = add(grad_second, second_got)
        second_got = swap(grad_second, "sample", bit)
    features, input_grad, grad_first, grad_second = call(
        functools.partial(finish_kernel, scale, half),
        [
            sds((f2, cells), BF16),
            sds((rows_in, cells), BF16),
            sds((f1, 27 * c0), F32),
            sds((f2, 27 * c1), F32),
        ],
        [],
        0,
        2 * 1024 * 1024,
    )(*ins, grad_first, first_got, grad_second, second_got, features)
    return (
        features.reshape(f2, 1, cells),
        input_grad.reshape(rows_in, 1, cells),
        grad_first,
        grad_second,
    )


def solution(mesh):
    return jax.shard_map(
        local,
        mesh=mesh,
        in_specs=(P("mp", "sample", None), P("mp", None), P("mp", None), P("mp", "sample", None)),
        out_specs=(P("mp", "sample", None), P("mp", "sample", None), P("mp", None), P("mp", None)),
        check_vma=False,
    )
```

```python
import functools
import math

import jax
import jax.numpy as jnp
from jax import lax
from jax.experimental import pallas as pl
from jax.experimental.pallas import tpu as pltpu
from jax.sharding import PartitionSpec as P

SIDE = 16
PLANE = SIDE * SIDE
F32 = jnp.float32
BF16 = jnp.bfloat16
VMEM_LIMIT = 48 * 1024 * 1024


def pitch_of(channels):
    width = 3 * channels
    slack = max((i * width) % 128 for i in range(9))
    return -(-(width + slack) // 128) * 128


def lane_grid(width):
    lane = lax.broadcasted_iota(jnp.int32, (1, width), 1)
    return lane % SIDE, (lane // SIDE) % SIDE


def inside(grid_xy, dy, dx):
    x, y = grid_xy
    ok = None
    for coord, step in ((y, dy), (x, dx)):
        if step < 0:
            now = coord >= -step
        elif step > 0:
            now = coord < SIDE - step
        else:
            continue
        ok = now if ok is None else ok & now
    return ok


def moved(values, grid_xy, dy, dx):
    if dy == 0 and dx == 0:
        return values
    width = values.shape[1]
    rolled = pltpu.roll(values, (-(dy * SIDE + dx)) % width, 1)
    return jnp.where(inside(grid_xy, dy, dx), rolled, 0.0)


def sigmoid(v):
    return 0.5 + 0.5 * jnp.tanh(0.5 * v)


def dot(a, b):
    return lax.dot_general(a, b, (((1,), (0,)), ((), ())), preferred_element_type=F32)


def dot_nt(a, b):
    return lax.dot_general(a, b, (((1,), (1,)), ((), ())), preferred_element_type=F32)


def chunk_of(cells, planes):
    while cells % (planes * PLANE):
        planes //= 2
    return planes * PLANE


def forward_kernel(n_mp, c0, *refs):
    near_ref, far_ref, w2r_ref, w2b_ref, cot_ref = refs[:5]
    feat_ref, pre_ref, vol_ref, keep_ref, give_ref, grad_ref = refs[5:11]
    vs, w1s, v3, w1r, hid, pre, d9, part, acc = refs[11:]

    me = lax.axis_index("mp")
    f1 = w1s.shape[1]
    c1 = n_mp * f1
    f2, cells = cot_ref.shape
    chunk = chunk_of(cells, 8)
    steps = cells // chunk
    pitch = pitch_of(c0)
    grid_xy = lane_grid(chunk)

    for k in range(n_mp):
        piece = (far_ref if k % 2 else near_ref)[k // 2].astype(F32)
        slot = me ^ k
        w1s[slot] = piece[:f1]
        vs[slot] = piece[f1:, :cells]

    lane = lax.broadcasted_iota(jnp.int32, (1, pitch), 1)
    for dz in range(3):
        for dy in range(3):
            start = (dz * 3 + dy) * 3 * c0
            low = start // 128 * 128
            block = w1s[:, :, low : low + pitch].reshape(c1, pitch)
            if start != low:
                block = pltpu.roll(block, pitch - (start - low), 1)
            block = jnp.where(lane < 3 * c0, block, 0.0)
            w1r[dy * c1 : (dy + 1) * c1, dz * pitch : (dz + 1) * pitch] = block.astype(BF16)

    for ref in (v3, hid, d9):
        zero = jnp.zeros((ref.shape[0], PLANE), BF16)
        ref[:, :PLANE] = zero
        ref[:, PLANE + cells :] = zero
    v3[3 * c0 :, PLANE : PLANE + cells] = jnp.zeros((pitch - 3 * c0, cells), BF16)

    for step in range(steps):
        base = step * chunk
        values = vs[:, :, base : base + chunk].reshape(c0, chunk)
        vol_ref[:, base : base + chunk] = values.astype(BF16)
        for dx in range(3):
            v3[dx * c0 : (dx + 1) * c0, base + PLANE : base + PLANE + chunk] = moved(values, grid_xy, 0, dx - 1).astype(BF16)

    def stacked(ref, base, order):
        return jnp.concatenate([ref[:, base + dz * PLANE : base + dz * PLANE + chunk] for dz in order], axis=0)

    def first_conv(base):
        z = dot(w1r[...], stacked(v3, base, (0, 1, 2)))
        total = z[c1 : 2 * c1]
        total = total + moved(z[:c1], grid_xy, -1, 0)
        total = total + moved(z[2 * c1 :], grid_xy, 1, 0)
        pre[:, base : base + chunk] = total
        hid[:, base + PLANE : base + PLANE + chunk] = (total * sigmoid(total)).astype(BF16)

    def second_conv(base):
        z = dot(w2r_ref[...], stacked(hid, base, (0, 1, 2)))
        total = None
        for dy in range(3):
            for dx in range(3):
                k = dy * 3 + dx
                term = moved(z[k * f2 : (k + 1) * f2], grid_xy, dy - 1, dx - 1)
                total = term if total is None else total + term
        s = sigmoid(total)
        feat_ref[:, base : base + chunk] = (total * s).astype(BF16)
        cot = cot_ref[:, base : base + chunk].astype(F32)
        delta = (cot * (s * (1.0 + total * (1.0 - s)))).astype(BF16).astype(F32)
        for dy in range(3):
            for dx in range(3):
                k = dy * 3 + dx
                d9[k * f2 : (k + 1) * f2, base + PLANE : base + PLANE + chunk] = moved(delta, grid_xy, 1 - dy, 1 - dx).astype(BF16)

    def gradients(base):
        deltas = stacked(d9, base, (2, 1, 0))
        part[:, :, base : base + chunk] = dot(w2b_ref[...], deltas).reshape(n_mp, f1, chunk)
        g = dot_nt(deltas, hid[:, base + PLANE : base + PLANE + chunk])
        acc[...] = g if base == 0 else acc[...] + g

    for step in range(steps + 2):
        if step < steps:
            first_conv(step * chunk)
        if 1 <= step <= steps:
            second_conv((step - 1) * chunk)
        if step >= 2:
            gradients((step - 2) * chunk)

    pre_ref[...] = pre[pl.ds(pl.multiple_of(me * f1, f1), f1), :]
    for k in range(n_mp):
        (give_ref if k % 2 else keep_ref)[k // 2] = part[me ^ k].astype(BF16)
    for t in range(27):
        grad_ref[:, t * c1 : (t + 1) * c1] = acc[t * f2 : (t + 1) * f2].astype(BF16)


def backward_kernel(n_mp, *refs):
    parts = refs[: n_mp // 2]
    pre_ref, vol_ref, w1b_ref, keep_ref, give_ref, grad_ref, d9, part, acc = refs[n_mp // 2 :]
    me = lax.axis_index("mp")
    f1, cells = pre_ref.shape
    c0 = vol_ref.shape[0]
    chunk = chunk_of(cells, 8)
    steps = cells // chunk
    grid_xy = lane_grid(chunk)

    zero = jnp.zeros((d9.shape[0], PLANE), BF16)
    d9[:, :PLANE] = zero
    d9[:, PLANE + cells :] = zero

    reps = max(1, 128 // c0)
    span = reps * c0

    def take(base):
        total = parts[0][:, base : base + chunk].astype(F32)
        for other in parts[1:]:
            total = total + other[:, base : base + chunk].astype(F32)
        v = pre_ref[:, base : base + chunk]
        s = sigmoid(v)
        delta = (total * (s * (1.0 + v * (1.0 - s)))).astype(BF16).astype(F32)
        shifts = [moved(delta, grid_xy, 1 - dy, 1 - dx) for dy in range(3) for dx in range(3)]
        d9[:, base + PLANE : base + PLANE + chunk] = jnp.concatenate(shifts, axis=0).astype(BF16)

    def gradients(base):
        deltas = jnp.concatenate([d9[:, base + dz * PLANE : base + dz * PLANE + chunk] for dz in (2, 1, 0)], axis=0)
        part[:, :, base : base + chunk] = dot(w1b_ref[...], deltas).reshape(n_mp, c0 // n_mp, chunk)
        vol = vol_ref[:, base : base + chunk]
        g = dot_nt(deltas, jnp.concatenate([vol] * reps, axis=0))
        acc[...] = g if base == 0 else acc[...] + g

    for step in range(steps + 1):
        if step < steps:
            take(step * chunk)
        if step >= 1:
            gradients((step - 1) * chunk)
    for k in range(n_mp):
        (give_ref if k % 2 else keep_ref)[k // 2] = part[me ^ k].astype(BF16)

    lane = lax.broadcasted_iota(jnp.int32, (1, span), 1)
    for t in range(0, 27, reps):
        merged = acc[t * f1 : (t + 1) * f1]
        for r in range(1, min(reps, 27 - t)):
            merged = jnp.where(lane >= r * c0, acc[(t + r) * f1 : (t + r + 1) * f1], merged)
        width = min(span, (27 - t) * c0)
        grad_ref[:, t * c0 : t * c0 + width] = merged[:, :width].astype(BF16)


def finish_kernel(scale, count, *refs):
    ins = refs[:count]
    first_ref, first_got_ref, second_ref, second_got_ref, feat_in_ref = refs[count : count + 5]
    feat_ref, input_ref, first_out_ref, second_out_ref = refs[count + 5 :]
    second_out_ref[...] = (second_ref[...].astype(F32) + second_got_ref[...].astype(F32)) * scale
    feat_ref[...] = feat_in_ref[...]
    first_out_ref[...] = (first_ref[...].astype(F32) + first_got_ref[...].astype(F32)) * scale
    total = ins[0][...].astype(F32)
    for other in ins[1:]:
        total = total + other[...].astype(F32)
    input_ref[...] = total.astype(BF16)


def swap(value, axis, k):
    n = lax.axis_size(axis)
    return lax.ppermute(value, axis, [(i, i ^ k) for i in range(n)])


def add(a, b):
    return (a.astype(F32) + b.astype(F32)).astype(BF16)


def sum_over_chips(keep, got):
    parts = [add(keep[j], got[j]) for j in range(keep.shape[0])]
    return [parts[0]] + [swap(parts[j], "mp", 2 * j) for j in range(1, len(parts))]


def bits_of(count):
    return [1 << i for i in reversed(range(count.bit_length() - 1))]


def call(kernel, out_shape, scratch, flops, nbytes):
    return pl.pallas_call(
        kernel,
        out_shape=out_shape,
        scratch_shapes=scratch,
        compiler_params=pltpu.CompilerParams(vmem_limit_bytes=VMEM_LIMIT),
        cost_estimate=pl.CostEstimate(flops=flops, bytes_accessed=nbytes, transcendentals=0),
    )


def local(volumes, w_first, w_second, cotangent):
    n_mp = lax.axis_size("mp")
    n_sample = lax.axis_size("sample")
    rows_in, _, cells = volumes.shape
    f1 = w_first.shape[0]
    f2 = w_second.shape[0]
    c0 = w_first.shape[1] // 27
    c1 = w_second.shape[1] // 27
    pitch = pitch_of(c0)
    scale = 1.0 / math.sqrt(n_sample * volumes.shape[1] * cells)
    volumes = volumes.reshape(rows_in, cells)
    cotangent = cotangent.reshape(f2, cells)
    padded = cells + 2 * PLANE

    need = (8 * 3 * c0) // 128 * 128 + pitch
    wide = max(cells, need)
    piece = jnp.concatenate(
        [
            jnp.pad(w_first, ((0, 0), (0, wide - w_first.shape[1]))),
            jnp.pad(volumes, ((0, 0), (0, wide - cells))),
        ],
        axis=0,
    )
    near = [piece] + [swap(piece, "mp", k) for k in range(2, n_mp, 2)]
    near = jnp.stack(near)
    far = swap(near, "mp", 1)

    w2t = w_second.reshape(f2, 3, 9, c1)
    w2r = jnp.transpose(w2t, (2, 0, 1, 3)).reshape(9 * f2, 3 * c1)
    w2b = jnp.transpose(w2t, (3, 1, 2, 0)).reshape(c1, 27 * f2)
    w1b = jnp.transpose(w_first.reshape(f1, 27, c0), (2, 1, 0)).reshape(c0, 27 * f1)

    sds = jax.ShapeDtypeStruct
    half = n_mp // 2
    features, pre_own, vol_all, keep, give, grad_second = call(
        functools.partial(forward_kernel, n_mp, c0),
        [
            sds((f2, cells), BF16),
            sds((f1, cells), F32),
            sds((c0, cells), BF16),
            sds((half, f1, cells), BF16),
            sds((half, f1, cells), BF16),
            sds((f2, 27 * c1), BF16),
        ],
        [
            pltpu.VMEM((n_mp, rows_in, cells), F32),
            pltpu.VMEM((n_mp, f1, wide), F32),
            pltpu.VMEM((pitch, padded), BF16),
            pltpu.VMEM((3 * c1, 3 * pitch), BF16),
            pltpu.VMEM((c1, padded), BF16),
            pltpu.VMEM((c1, cells), F32),
            pltpu.VMEM((9 * f2, padded), BF16),
            pltpu.VMEM((n_mp, f1, cells), F32),
            pltpu.VMEM((27 * f2, c1), F32),
        ],
        2 * cells * 27 * (c0 * c1 + 3 * f2 * c1),
        4 * 1024 * 1024,
    )(near, far, w2r, w2b, cotangent)

    bits = bits_of(n_sample)
    parts = sum_over_chips(keep, swap(give, "mp", 1))
    second_got = swap(grad_second, "sample", bits[0])

    keep, give, grad_first = call(
        functools.partial(backward_kernel, n_mp),
        [
            sds((half, rows_in, cells), BF16),
            sds((half, rows_in, cells), BF16),
            sds((f1, 27 * c0), BF16),
        ],
        [
            pltpu.VMEM((9 * f1, padded), BF16),
            pltpu.VMEM((n_mp, rows_in, cells), F32),
            pltpu.VMEM((27 * f1, max(1, 128 // c0) * c0), F32),
        ],
        2 * cells * 27 * 2 * c0 * f1,
        1024 * 1024,
    )(*parts, pre_own, vol_all, w1b)
    got = swap(give, "mp", 1)
    ins = sum_over_chips(keep, got)

    second_got, *_ = lax.optimization_barrier((second_got, grad_first))
    for bit in bits[::-1][:-1]:
        grad_first = add(grad_first, swap(grad_first, "sample", bit))
    first_got = swap(grad_first, "sample", bits[::-1][-1])
    for bit in bits[1:]:
        grad_second = add(grad_second, second_got)
        second_got = swap(grad_second, "sample", bit)
    features, input_grad, grad_first, grad_second = call(
        functools.partial(finish_kernel, scale, half),
        [
            sds((f2, cells), BF16),
            sds((rows_in, cells), BF16),
            sds((f1, 27 * c0), F32),
            sds((f2, 27 * c1), F32),
        ],
        [],
        0,
        2 * 1024 * 1024,
    )(*ins, grad_first, first_got, grad_second, second_got, features)
    return (
        features.reshape(f2, 1, cells),
        input_grad.reshape(rows_in, 1, cells),
        grad_first,
        grad_second,
    )


def solution(mesh):
    return jax.shard_map(
        local,
        mesh=mesh,
        in_specs=(P("mp", "sample", None), P("mp", None), P("mp", None), P("mp", "sample", None)),
        out_specs=(P("mp", "sample", None), P("mp", "sample", None), P("mp", None), P("mp", None)),
        check_vma=False,
    )
```

```python
import functools
import math

import jax
import jax.numpy as jnp
from jax import lax
from jax.experimental import pallas as pl
from jax.experimental.pallas import tpu as pltpu
from jax.sharding import PartitionSpec as P

SIDE = 16
PLANE = SIDE * SIDE
F32 = jnp.float32
BF16 = jnp.bfloat16
VMEM_LIMIT = 48 * 1024 * 1024


def pitch_of(channels):
    width = 3 * channels
    slack = max((i * width) % 128 for i in range(9))
    return -(-(width + slack) // 128) * 128


def lane_grid(width):
    lane = lax.broadcasted_iota(jnp.int32, (1, width), 1)
    return lane % SIDE, (lane // SIDE) % SIDE


def inside(grid_xy, dy, dx):
    x, y = grid_xy
    ok = None
    for coord, step in ((y, dy), (x, dx)):
        if step < 0:
            now = coord >= -step
        elif step > 0:
            now = coord < SIDE - step
        else:
            continue
        ok = now if ok is None else ok & now
    return ok


def moved(values, grid_xy, dy, dx):
    if dy == 0 and dx == 0:
        return values
    width = values.shape[1]
    rolled = pltpu.roll(values, (-(dy * SIDE + dx)) % width, 1)
    return jnp.where(inside(grid_xy, dy, dx), rolled, 0.0)


def sigmoid(v):
    return 0.5 + 0.5 * jnp.tanh(0.5 * v)


def dot(a, b):
    return lax.dot_general(a, b, (((1,), (0,)), ((), ())), preferred_element_type=F32)


def dot_nt(a, b):
    return lax.dot_general(a, b, (((1,), (1,)), ((), ())), preferred_element_type=F32)


def chunk_of(cells, planes):
    while cells % (planes * PLANE):
        planes //= 2
    return planes * PLANE


def forward_kernel(n_mp, c0, *refs):
    near_ref, far_ref, w2r_ref, w2b_ref, cot_ref = refs[:5]
    feat_ref, pre_ref, vol_ref, keep_ref, give_ref, grad_ref = refs[5:11]
    vs, w1s, v3, w1r, hid, pre, d9, part, acc = refs[11:]

    me = lax.axis_index("mp")
    f1 = w1s.shape[1]
    c1 = n_mp * f1
    f2, cells = cot_ref.shape
    chunk = chunk_of(cells, 4)
    steps = cells // chunk
    pitch = pitch_of(c0)
    grid_xy = lane_grid(chunk)

    for k in range(n_mp):
        piece = (far_ref if k % 2 else near_ref)[k // 2].astype(F32)
        slot = me ^ k
        w1s[slot] = piece[:f1]
        vs[slot] = piece[f1:, :cells]

    lane = lax.broadcasted_iota(jnp.int32, (1, pitch), 1)
    for dz in range(3):
        for dy in range(3):
            start = (dz * 3 + dy) * 3 * c0
            low = start // 128 * 128
            block = w1s[:, :, low : low + pitch].reshape(c1, pitch)
            if start != low:
                block = pltpu.roll(block, pitch - (start - low), 1)
            block = jnp.where(lane < 3 * c0, block, 0.0)
            w1r[dy * c1 : (dy + 1) * c1, dz * pitch : (dz + 1) * pitch] = block.astype(BF16)

    for ref in (v3, hid, d9):
        zero = jnp.zeros((ref.shape[0], PLANE), BF16)
        ref[:, :PLANE] = zero
        ref[:, PLANE + cells :] = zero
    v3[3 * c0 :, PLANE : PLANE + cells] = jnp.zeros((pitch - 3 * c0, cells), BF16)

    for step in range(steps):
        base = step * chunk
        values = vs[:, :, base : base + chunk].reshape(c0, chunk)
        vol_ref[:, base : base + chunk] = values.astype(BF16)
        for dx in range(3):
            v3[dx * c0 : (dx + 1) * c0, base + PLANE : base + PLANE + chunk] = moved(values, grid_xy, 0, dx - 1).astype(BF16)

    def stacked(ref, base, order):
        return jnp.concatenate([ref[:, base + dz * PLANE : base + dz * PLANE + chunk] for dz in order], axis=0)

    def first_conv(base):
        z = dot(w1r[...], stacked(v3, base, (0, 1, 2)))
        total = z[c1 : 2 * c1]
        total = total + moved(z[:c1], grid_xy, -1, 0)
        total = total + moved(z[2 * c1 :], grid_xy, 1, 0)
        pre[:, base : base + chunk] = total
        hid[:, base + PLANE : base + PLANE + chunk] = (total * sigmoid(total)).astype(BF16)

    def second_conv(base):
        z = dot(w2r_ref[...], stacked(hid, base, (0, 1, 2)))
        total = None
        for dy in range(3):
            for dx in range(3):
                k = dy * 3 + dx
                term = moved(z[k * f2 : (k + 1) * f2], grid_xy, dy - 1, dx - 1)
                total = term if total is None else total + term
        s = sigmoid(total)
        feat_ref[:, base : base + chunk] = (total * s).astype(BF16)
        cot = cot_ref[:, base : base + chunk].astype(F32)
        delta = (cot * (s * (1.0 + total * (1.0 - s)))).astype(BF16).astype(F32)
        for dy in range(3):
            for dx in range(3):
                k = dy * 3 + dx
                d9[k * f2 : (k + 1) * f2, base + PLANE : base + PLANE + chunk] = moved(delta, grid_xy, 1 - dy, 1 - dx).astype(BF16)

    def gradients(base):
        deltas = stacked(d9, base, (2, 1, 0))
        part[:, :, base : base + chunk] = dot(w2b_ref[...], deltas).reshape(n_mp, f1, chunk)
        g = dot_nt(deltas, hid[:, base + PLANE : base + PLANE + chunk])
        acc[...] = g if base == 0 else acc[...] + g

    for step in range(steps + 2):
        if step < steps:
            first_conv(step * chunk)
        if 1 <= step <= steps:
            second_conv((step - 1) * chunk)
        if step >= 2:
            gradients((step - 2) * chunk)

    pre_ref[...] = pre[pl.ds(pl.multiple_of(me * f1, f1), f1), :]
    for k in range(n_mp):
        (give_ref if k % 2 else keep_ref)[k // 2] = part[me ^ k].astype(BF16)
    for t in range(27):
        grad_ref[:, t * c1 : (t + 1) * c1] = acc[t * f2 : (t + 1) * f2].astype(BF16)


def backward_kernel(n_mp, *refs):
    parts = refs[: n_mp // 2]
    pre_ref, vol_ref, w1b_ref, keep_ref, give_ref, grad_ref, d9, part, acc = refs[n_mp // 2 :]
    me = lax.axis_index("mp")
    f1, cells = pre_ref.shape
    c0 = vol_ref.shape[0]
    chunk = chunk_of(cells, 1)
    steps = cells // chunk
    grid_xy = lane_grid(chunk)

    zero = jnp.zeros((d9.shape[0], PLANE), BF16)
    d9[:, :PLANE] = zero
    d9[:, PLANE + cells :] = zero

    reps = max(1, 128 // c0)
    span = reps * c0

    def take(base):
        total = parts[0][:, base : base + chunk].astype(F32)
        for other in parts[1:]:
            total = total + other[:, base : base + chunk].astype(F32)
        v = pre_ref[:, base : base + chunk]
        s = sigmoid(v)
        delta = (total * (s * (1.0 + v * (1.0 - s)))).astype(BF16).astype(F32)
        shifts = [moved(delta, grid_xy, 1 - dy, 1 - dx) for dy in range(3) for dx in range(3)]
        d9[:, base + PLANE : base + PLANE + chunk] = jnp.concatenate(shifts, axis=0).astype(BF16)

    def gradients(base):
        deltas = jnp.concatenate([d9[:, base + dz * PLANE : base + dz * PLANE + chunk] for dz in (2, 1, 0)], axis=0)
        part[:, :, base : base + chunk] = dot(w1b_ref[...], deltas).reshape(n_mp, c0 // n_mp, chunk)
        vol = vol_ref[:, base : base + chunk]
        g = dot_nt(deltas, jnp.concatenate([vol] * reps, axis=0))
        acc[...] = g if base == 0 else acc[...] + g

    for step in range(steps + 1):
        if step < steps:
            take(step * chunk)
        if step >= 1:
            gradients((step - 1) * chunk)
    for k in range(n_mp):
        (give_ref if k % 2 else keep_ref)[k // 2] = part[me ^ k].astype(BF16)

    lane = lax.broadcasted_iota(jnp.int32, (1, span), 1)
    for t in range(0, 27, reps):
        merged = acc[t * f1 : (t + 1) * f1]
        for r in range(1, min(reps, 27 - t)):
            merged = jnp.where(lane >= r * c0, acc[(t + r) * f1 : (t + r + 1) * f1], merged)
        width = min(span, (27 - t) * c0)
        grad_ref[:, t * c0 : t * c0 + width] = merged[:, :width].astype(BF16)


def finish_kernel(scale, count, *refs):
    ins = refs[:count]
    first_ref, first_got_ref, second_ref, second_got_ref, feat_in_ref = refs[count : count + 5]
    feat_ref, input_ref, first_out_ref, second_out_ref = refs[count + 5 :]
    second_out_ref[...] = (second_ref[...].astype(F32) + second_got_ref[...].astype(F32)) * scale
    feat_ref[...] = feat_in_ref[...]
    first_out_ref[...] = (first_ref[...].astype(F32) + first_got_ref[...].astype(F32)) * scale
    total = ins[0][...].astype(F32)
    for other in ins[1:]:
        total = total + other[...].astype(F32)
    input_ref[...] = total.astype(BF16)


def swap(value, axis, k):
    n = lax.axis_size(axis)
    return lax.ppermute(value, axis, [(i, i ^ k) for i in range(n)])


def add(a, b):
    return (a.astype(F32) + b.astype(F32)).astype(BF16)


def sum_over_chips(keep, got):
    parts = [add(keep[j], got[j]) for j in range(keep.shape[0])]
    return [parts[0]] + [swap(parts[j], "mp", 2 * j) for j in range(1, len(parts))]


def bits_of(count):
    return [1 << i for i in reversed(range(count.bit_length() - 1))]


def call(kernel, out_shape, scratch, flops, nbytes):
    return pl.pallas_call(
        kernel,
        out_shape=out_shape,
        scratch_shapes=scratch,
        compiler_params=pltpu.CompilerParams(vmem_limit_bytes=VMEM_LIMIT),
        cost_estimate=pl.CostEstimate(flops=flops, bytes_accessed=nbytes, transcendentals=0),
    )


def local(volumes, w_first, w_second, cotangent):
    n_mp = lax.axis_size("mp")
    n_sample = lax.axis_size("sample")
    rows_in, _, cells = volumes.shape
    f1 = w_first.shape[0]
    f2 = w_second.shape[0]
    c0 = w_first.shape[1] // 27
    c1 = w_second.shape[1] // 27
    pitch = pitch_of(c0)
    scale = 1.0 / math.sqrt(n_sample * volumes.shape[1] * cells)
    volumes = volumes.reshape(rows_in, cells)
    cotangent = cotangent.reshape(f2, cells)
    padded = cells + 2 * PLANE

    need = (8 * 3 * c0) // 128 * 128 + pitch
    wide = max(cells, need)
    piece = jnp.concatenate(
        [
            jnp.pad(w_first, ((0, 0), (0, wide - w_first.shape[1]))),
            jnp.pad(volumes, ((0, 0), (0, wide - cells))),
        ],
        axis=0,
    )
    near = [piece] + [swap(piece, "mp", k) for k in range(2, n_mp, 2)]
    near = jnp.stack(near)
    far = swap(near, "mp", 1)

    w2t = w_second.reshape(f2, 3, 9, c1)
    w2r = jnp.transpose(w2t, (2, 0, 1, 3)).reshape(9 * f2, 3 * c1)
    w2b = jnp.transpose(w2t, (3, 1, 2, 0)).reshape(c1, 27 * f2)
    w1b = jnp.transpose(w_first.reshape(f1, 27, c0), (2, 1, 0)).reshape(c0, 27 * f1)

    sds = jax.ShapeDtypeStruct
    half = n_mp // 2
    features, pre_own, vol_all, keep, give, grad_second = call(
        functools.partial(forward_kernel, n_mp, c0),
        [
            sds((f2, cells), BF16),
            sds((f1, cells), F32),
            sds((c0, cells), BF16),
            sds((half, f1, cells), BF16),
            sds((half, f1, cells), BF16),
            sds((f2, 27 * c1), BF16),
        ],
        [
            pltpu.VMEM((n_mp, rows_in, cells), F32),
            pltpu.VMEM((n_mp, f1, wide), F32),
            pltpu.VMEM((pitch, padded), BF16),
            pltpu.VMEM((3 * c1, 3 * pitch), BF16),
            pltpu.VMEM((c1, padded), BF16),
            pltpu.VMEM((c1, cells), F32),
            pltpu.VMEM((9 * f2, padded), BF16),
            pltpu.VMEM((n_mp, f1, cells), F32),
            pltpu.VMEM((27 * f2, c1), F32),
        ],
        2 * cells * 27 * (c0 * c1 + 3 * f2 * c1),
        4 * 1024 * 1024,
    )(near, far, w2r, w2b, cotangent)

    bits = bits_of(n_sample)
    parts = sum_over_chips(keep, swap(give, "mp", 1))
    second_got = swap(grad_second, "sample", bits[0])

    keep, give, grad_first = call(
        functools.partial(backward_kernel, n_mp),
        [
            sds((half, rows_in, cells), BF16),
            sds((half, rows_in, cells), BF16),
            sds((f1, 27 * c0), BF16),
        ],
        [
            pltpu.VMEM((9 * f1, padded), BF16),
            pltpu.VMEM((n_mp, rows_in, cells), F32),
            pltpu.VMEM((27 * f1, max(1, 128 // c0) * c0), F32),
        ],
        2 * cells * 27 * 2 * c0 * f1,
        1024 * 1024,
    )(*parts, pre_own, vol_all, w1b)
    got = swap(give, "mp", 1)
    ins = sum_over_chips(keep, got)

    second_got, *_ = lax.optimization_barrier((second_got, grad_first))
    for bit in bits[:-1]:
        grad_first = add(grad_first, swap(grad_first, "sample", bit))
    first_got = swap(grad_first, "sample", bits[-1])
    for bit in bits[1:]:
        grad_second = add(grad_second, second_got)
        second_got = swap(grad_second, "sample", bit)
    features, input_grad, grad_first, grad_second = call(
        functools.partial(finish_kernel, scale, half),
        [
            sds((f2, cells), BF16),
            sds((rows_in, cells), BF16),
            sds((f1, 27 * c0), F32),
            sds((f2, 27 * c1), F32),
        ],
        [],
        0,
        2 * 1024 * 1024,
    )(*ins, grad_first, first_got, grad_second, second_got, features)
    return (
        features.reshape(f2, 1, cells),
        input_grad.reshape(rows_in, 1, cells),
        grad_first,
        grad_second,
    )


def solution(mesh):
    return jax.shard_map(
        local,
        mesh=mesh,
        in_specs=(P("mp", "sample", None), P("mp", None), P("mp", None), P("mp", "sample", None)),
        out_specs=(P("mp", "sample", None), P("mp", "sample", None), P("mp", None), P("mp", None)),
        check_vma=False,
    )
```

```python
import functools
import math

import jax
import jax.numpy as jnp
from jax import lax
from jax.experimental import pallas as pl
from jax.experimental.pallas import tpu as pltpu
from jax.sharding import PartitionSpec as P

SIDE = 16
PLANE = SIDE * SIDE
F32 = jnp.float32
BF16 = jnp.bfloat16
VMEM_LIMIT = 48 * 1024 * 1024


def pitch_of(channels):
    width = 3 * channels
    slack = max((i * width) % 128 for i in range(9))
    return -(-(width + slack) // 128) * 128


def lane_grid(width):
    lane = lax.broadcasted_iota(jnp.int32, (1, width), 1)
    return lane % SIDE, (lane // SIDE) % SIDE


def inside(grid_xy, dy, dx):
    x, y = grid_xy
    ok = None
    for coord, step in ((y, dy), (x, dx)):
        if step < 0:
            now = coord >= -step
        elif step > 0:
            now = coord < SIDE - step
        else:
            continue
        ok = now if ok is None else ok & now
    return ok


def moved(values, grid_xy, dy, dx):
    if dy == 0 and dx == 0:
        return values
    width = values.shape[1]
    rolled = pltpu.roll(values, (-(dy * SIDE + dx)) % width, 1)
    return jnp.where(inside(grid_xy, dy, dx), rolled, 0.0)


def sigmoid(v):
    return 0.5 + 0.5 * jnp.tanh(0.5 * v)


def dot(a, b):
    return lax.dot_general(a, b, (((1,), (0,)), ((), ())), preferred_element_type=F32)


def dot_nt(a, b):
    return lax.dot_general(a, b, (((1,), (1,)), ((), ())), preferred_element_type=F32)


def chunk_of(cells, planes):
    while cells % (planes * PLANE):
        planes //= 2
    return planes * PLANE


def forward_kernel(n_mp, c0, *refs):
    near_ref, far_ref, w2r_ref, w2b_ref, cot_ref = refs[:5]
    feat_ref, pre_ref, vol_ref, keep_ref, give_ref, grad_ref = refs[5:11]
    vs, w1s, v3, w1r, hid, pre, d9, part, acc = refs[11:]

    me = lax.axis_index("mp")
    f1 = w1s.shape[1]
    c1 = n_mp * f1
    f2, cells = cot_ref.shape
    chunk = chunk_of(cells, 4)
    steps = cells // chunk
    pitch = pitch_of(c0)
    grid_xy = lane_grid(chunk)

    for k in range(n_mp):
        piece = (far_ref if k % 2 else near_ref)[k // 2].astype(F32)
        slot = me ^ k
        w1s[slot] = piece[:f1]
        vs[slot] = piece[f1:, :cells]

    lane = lax.broadcasted_iota(jnp.int32, (1, pitch), 1)
    for dz in range(3):
        for dy in range(3):
            start = (dz * 3 + dy) * 3 * c0
            low = start // 128 * 128
            block = w1s[:, :, low : low + pitch].reshape(c1, pitch)
            if start != low:
                block = pltpu.roll(block, pitch - (start - low), 1)
            block = jnp.where(lane < 3 * c0, block, 0.0)
            w1r[dy * c1 : (dy + 1) * c1, dz * pitch : (dz + 1) * pitch] = block.astype(BF16)

    for ref in (v3, hid, d9):
        zero = jnp.zeros((ref.shape[0], PLANE), BF16)
        ref[:, :PLANE] = zero
        ref[:, PLANE + cells :] = zero
    v3[3 * c0 :, PLANE : PLANE + cells] = jnp.zeros((pitch - 3 * c0, cells), BF16)

    for step in range(steps):
        base = step * chunk
        values = vs[:, :, base : base + chunk].reshape(c0, chunk)
        vol_ref[:, base : base + chunk] = values.astype(BF16)
        for dx in range(3):
            v3[dx * c0 : (dx + 1) * c0, base + PLANE : base + PLANE + chunk] = moved(values, grid_xy, 0, dx - 1).astype(BF16)

    def stacked(ref, base, order):
        return jnp.concatenate([ref[:, base + dz * PLANE : base + dz * PLANE + chunk] for dz in order], axis=0)

    def first_conv(base):
        z = dot(w1r[...], stacked(v3, base, (0, 1, 2)))
        total = z[c1 : 2 * c1]
        total = total + moved(z[:c1], grid_xy, -1, 0)
        total = total + moved(z[2 * c1 :], grid_xy, 1, 0)
        pre[:, base : base + chunk] = total
        hid[:, base + PLANE : base + PLANE + chunk] = (total * sigmoid(total)).astype(BF16)

    def second_conv(base):
        z = dot(w2r_ref[...], stacked(hid, base, (0, 1, 2)))
        total = None
        for dy in range(3):
            for dx in range(3):
                k = dy * 3 + dx
                term = moved(z[k * f2 : (k + 1) * f2], grid_xy, dy - 1, dx - 1)
                total = term if total is None else total + term
        s = sigmoid(total)
        feat_ref[:, base : base + chunk] = (total * s).astype(BF16)
        cot = cot_ref[:, base : base + chunk].astype(F32)
        delta = (cot * (s * (1.0 + total * (1.0 - s)))).astype(BF16).astype(F32)
        for dy in range(3):
            for dx in range(3):
                k = dy * 3 + dx
                d9[k * f2 : (k + 1) * f2, base + PLANE : base + PLANE + chunk] = moved(delta, grid_xy, 1 - dy, 1 - dx).astype(BF16)

    def gradients(base):
        deltas = stacked(d9, base, (2, 1, 0))
        part[:, :, base : base + chunk] = dot(w2b_ref[...], deltas).reshape(n_mp, f1, chunk)
        g = dot_nt(deltas, hid[:, base + PLANE : base + PLANE + chunk])
        acc[...] = g if base == 0 else acc[...] + g

    for step in range(steps + 2):
        if step < steps:
            first_conv(step * chunk)
        if 1 <= step <= steps:
            second_conv((step - 1) * chunk)
        if step >= 2:
            gradients((step - 2) * chunk)

    pre_ref[...] = pre[pl.ds(pl.multiple_of(me * f1, f1), f1), :]
    for k in range(n_mp):
        (give_ref if k % 2 else keep_ref)[k // 2] = part[me ^ k].astype(BF16)
    for t in range(27):
        grad_ref[:, t * c1 : (t + 1) * c1] = acc[t * f2 : (t + 1) * f2].astype(BF16)


def backward_kernel(n_mp, *refs):
    parts = refs[: n_mp // 2]
    pre_ref, vol_ref, w1b_ref, keep_ref, give_ref, grad_ref, d9, part, acc = refs[n_mp // 2 :]
    me = lax.axis_index("mp")
    f1, cells = pre_ref.shape
    c0 = vol_ref.shape[0]
    chunk = chunk_of(cells, 1)
    steps = cells // chunk
    grid_xy = lane_grid(chunk)

    zero = jnp.zeros((d9.shape[0], PLANE), BF16)
    d9[:, :PLANE] = zero
    d9[:, PLANE + cells :] = zero

    reps = max(1, 128 // c0)
    span = reps * c0

    def take(base):
        total = parts[0][:, base : base + chunk].astype(F32)
        for other in parts[1:]:
            total = total + other[:, base : base + chunk].astype(F32)
        v = pre_ref[:, base : base + chunk]
        s = sigmoid(v)
        delta = (total * (s * (1.0 + v * (1.0 - s)))).astype(BF16).astype(F32)
        shifts = [moved(delta, grid_xy, 1 - dy, 1 - dx) for dy in range(3) for dx in range(3)]
        d9[:, base + PLANE : base + PLANE + chunk] = jnp.concatenate(shifts, axis=0).astype(BF16)

    def gradients(base):
        deltas = jnp.concatenate([d9[:, base + dz * PLANE : base + dz * PLANE + chunk] for dz in (2, 1, 0)], axis=0)
        part[:, :, base : base + chunk] = dot(w1b_ref[...], deltas).reshape(n_mp, c0 // n_mp, chunk)
        vol = vol_ref[:, base : base + chunk]
        g = dot_nt(deltas, jnp.concatenate([vol] * reps, axis=0))
        acc[...] = g if base == 0 else acc[...] + g

    for step in range(steps + 1):
        if step < steps:
            take(step * chunk)
        if step >= 1:
            gradients((step - 1) * chunk)
    for k in range(n_mp):
        (give_ref if k % 2 else keep_ref)[k // 2] = part[me ^ k].astype(BF16)

    lane = lax.broadcasted_iota(jnp.int32, (1, span), 1)
    for t in range(0, 27, reps):
        merged = acc[t * f1 : (t + 1) * f1]
        for r in range(1, min(reps, 27 - t)):
            merged = jnp.where(lane >= r * c0, acc[(t + r) * f1 : (t + r + 1) * f1], merged)
        width = min(span, (27 - t) * c0)
        grad_ref[:, t * c0 : t * c0 + width] = merged[:, :width].astype(BF16)


def finish_kernel(scale, count, *refs):
    ins = refs[:count]
    first_ref, first_got_ref, second_ref, second_got_ref, feat_in_ref = refs[count : count + 5]
    feat_ref, input_ref, first_out_ref, second_out_ref = refs[count + 5 :]
    second_out_ref[...] = (second_ref[...].astype(F32) + second_got_ref[...].astype(F32)) * scale
    feat_ref[...] = feat_in_ref[...]
    first_out_ref[...] = (first_ref[...].astype(F32) + first_got_ref[...].astype(F32)) * scale
    total = ins[0][...].astype(F32)
    for other in ins[1:]:
        total = total + other[...].astype(F32)
    input_ref[...] = total.astype(BF16)


def swap(value, axis, k):
    n = lax.axis_size(axis)
    return lax.ppermute(value, axis, [(i, i ^ k) for i in range(n)])


def add(a, b):
    return (a.astype(F32) + b.astype(F32)).astype(BF16)


def sum_over_chips(keep, got):
    parts = [add(keep[j], got[j]) for j in range(keep.shape[0])]
    return [parts[0]] + [swap(parts[j], "mp", 2 * j) for j in range(1, len(parts))]


def bits_of(count):
    return [1 << i for i in reversed(range(count.bit_length() - 1))]


def call(kernel, out_shape, scratch, flops, nbytes):
    return pl.pallas_call(
        kernel,
        out_shape=out_shape,
        scratch_shapes=scratch,
        compiler_params=pltpu.CompilerParams(vmem_limit_bytes=VMEM_LIMIT),
        cost_estimate=pl.CostEstimate(flops=flops, bytes_accessed=nbytes, transcendentals=0),
    )


def local(volumes, w_first, w_second, cotangent):
    n_mp = lax.axis_size("mp")
    n_sample = lax.axis_size("sample")
    rows_in, _, cells = volumes.shape
    f1 = w_first.shape[0]
    f2 = w_second.shape[0]
    c0 = w_first.shape[1] // 27
    c1 = w_second.shape[1] // 27
    pitch = pitch_of(c0)
    scale = 1.0 / math.sqrt(n_sample * volumes.shape[1] * cells)
    volumes = volumes.reshape(rows_in, cells)
    cotangent = cotangent.reshape(f2, cells)
    padded = cells + 2 * PLANE

    need = (8 * 3 * c0) // 128 * 128 + pitch
    wide = max(cells, need)
    piece = jnp.concatenate(
        [
            jnp.pad(w_first, ((0, 0), (0, wide - w_first.shape[1]))),
            jnp.pad(volumes, ((0, 0), (0, wide - cells))),
        ],
        axis=0,
    )
    near = [piece] + [swap(piece, "mp", k) for k in range(2, n_mp, 2)]
    near = jnp.stack(near)
    far = swap(near, "mp", 1)

    w2t = w_second.reshape(f2, 3, 9, c1)
    w2r = jnp.transpose(w2t, (2, 0, 1, 3)).reshape(9 * f2, 3 * c1)
    w2b = jnp.transpose(w2t, (3, 1, 2, 0)).reshape(c1, 27 * f2)
    w1b = jnp.transpose(w_first.reshape(f1, 27, c0), (2, 1, 0)).reshape(c0, 27 * f1)

    sds = jax.ShapeDtypeStruct
    half = n_mp // 2
    features, pre_own, vol_all, keep, give, grad_second = call(
        functools.partial(forward_kernel, n_mp, c0),
        [
            sds((f2, cells), BF16),
            sds((f1, cells), F32),
            sds((c0, cells), BF16),
            sds((half, f1, cells), BF16),
            sds((half, f1, cells), BF16),
            sds((f2, 27 * c1), BF16),
        ],
        [
            pltpu.VMEM((n_mp, rows_in, cells), F32),
            pltpu.VMEM((n_mp, f1, wide), F32),
            pltpu.VMEM((pitch, padded), BF16),
            pltpu.VMEM((3 * c1, 3 * pitch), BF16),
            pltpu.VMEM((c1, padded), BF16),
            pltpu.VMEM((c1, cells), F32),
            pltpu.VMEM((9 * f2, padded), BF16),
            pltpu.VMEM((n_mp, f1, cells), F32),
            pltpu.VMEM((27 * f2, c1), F32),
        ],
        2 * cells * 27 * (c0 * c1 + 3 * f2 * c1),
        4 * 1024 * 1024,
    )(near, far, w2r, w2b, cotangent)

    bits = bits_of(n_sample)
    parts = sum_over_chips(keep, swap(give, "mp", 1))
    second_got = swap(grad_second, "sample", bits[0])

    keep, give, grad_first = call(
        functools.partial(backward_kernel, n_mp),
        [
            sds((half, rows_in, cells), BF16),
            sds((half, rows_in, cells), BF16),
            sds((f1, 27 * c0), BF16),
        ],
        [
            pltpu.VMEM((9 * f1, padded), BF16),
            pltpu.VMEM((n_mp, rows_in, cells), F32),
            pltpu.VMEM((27 * f1, max(1, 128 // c0) * c0), F32),
        ],
        2 * cells * 27 * 2 * c0 * f1,
        1024 * 1024,
    )(*parts, pre_own, vol_all, w1b)
    got = swap(give, "mp", 1)
    ins = sum_over_chips(keep, got)

    first_got = swap(grad_first, "sample", bits[0])
    second_got, first_got = lax.optimization_barrier((second_got, first_got))
    for bit in bits[1:]:
        grad_first = add(grad_first, first_got)
        first_got = swap(grad_first, "sample", bit)
        grad_second = add(grad_second, second_got)
        second_got = swap(grad_second, "sample", bit)
    features, input_grad, grad_first, grad_second = call(
        functools.partial(finish_kernel, scale, half),
        [
            sds((f2, cells), BF16),
            sds((rows_in, cells), BF16),
            sds((f1, 27 * c0), F32),
            sds((f2, 27 * c1), F32),
        ],
        [],
        0,
        2 * 1024 * 1024,
    )(*ins, grad_first, first_got, grad_second, second_got, features)
    return (
        features.reshape(f2, 1, cells),
        input_grad.reshape(rows_in, 1, cells),
        grad_first,
        grad_second,
    )


def solution(mesh):
    return jax.shard_map(
        local,
        mesh=mesh,
        in_specs=(P("mp", "sample", None), P("mp", None), P("mp", None), P("mp", "sample", None)),
        out_specs=(P("mp", "sample", None), P("mp", "sample", None), P("mp", None), P("mp", None)),
        check_vma=False,
    )
```

```python
import functools
import math

import jax
import jax.numpy as jnp
from jax import lax
from jax.experimental import pallas as pl
from jax.experimental.pallas import tpu as pltpu
from jax.sharding import PartitionSpec as P

SIDE = 16
PLANE = SIDE * SIDE
F32 = jnp.float32
BF16 = jnp.bfloat16
VMEM_LIMIT = 48 * 1024 * 1024


def pitch_of(channels):
    width = 3 * channels
    slack = max((i * width) % 128 for i in range(9))
    return -(-(width + slack) // 128) * 128


def lane_grid(width):
    lane = lax.broadcasted_iota(jnp.int32, (1, width), 1)
    return lane % SIDE, (lane // SIDE) % SIDE


def inside(grid_xy, dy, dx):
    x, y = grid_xy
    ok = None
    for coord, step in ((y, dy), (x, dx)):
        if step < 0:
            now = coord >= -step
        elif step > 0:
            now = coord < SIDE - step
        else:
            continue
        ok = now if ok is None else ok & now
    return ok


def moved(values, grid_xy, dy, dx):
    if dy == 0 and dx == 0:
        return values
    width = values.shape[1]
    rolled = pltpu.roll(values, (-(dy * SIDE + dx)) % width, 1)
    return jnp.where(inside(grid_xy, dy, dx), rolled, 0.0)


def sigmoid(v):
    return 0.5 + 0.5 * jnp.tanh(0.5 * v)


def dot(a, b):
    return lax.dot_general(a, b, (((1,), (0,)), ((), ())), preferred_element_type=F32)


def dot_nt(a, b):
    return lax.dot_general(a, b, (((1,), (1,)), ((), ())), preferred_element_type=F32)


def chunk_of(cells, planes):
    while cells % (planes * PLANE):
        planes //= 2
    return planes * PLANE


def forward_kernel(n_mp, c0, *refs):
    near_ref, far_ref, w2r_ref, w2b_ref, cot_ref = refs[:5]
    feat_ref, pre_ref, vol_ref, keep_ref, give_ref, grad_ref = refs[5:11]
    vs, w1s, v3, w1r, hid, pre, d9, part, acc = refs[11:]

    me = lax.axis_index("mp")
    f1 = w1s.shape[1]
    c1 = n_mp * f1
    f2, cells = cot_ref.shape
    chunk = chunk_of(cells, 4)
    steps = cells // chunk
    pitch = pitch_of(c0)
    grid_xy = lane_grid(chunk)

    for k in range(n_mp):
        piece = (far_ref if k % 2 else near_ref)[k // 2].astype(F32)
        slot = me ^ k
        w1s[slot] = piece[:f1]
        vs[slot] = piece[f1:, :cells]

    lane = lax.broadcasted_iota(jnp.int32, (1, pitch), 1)
    for dz in range(3):
        for dy in range(3):
            start = (dz * 3 + dy) * 3 * c0
            low = start // 128 * 128
            block = w1s[:, :, low : low + pitch].reshape(c1, pitch)
            if start != low:
                block = pltpu.roll(block, pitch - (start - low), 1)
            block = jnp.where(lane < 3 * c0, block, 0.0)
            w1r[dy * c1 : (dy + 1) * c1, dz * pitch : (dz + 1) * pitch] = block.astype(BF16)

    for ref in (v3, hid, d9):
        zero = jnp.zeros((ref.shape[0], PLANE), BF16)
        ref[:, :PLANE] = zero
        ref[:, PLANE + cells :] = zero
    v3[3 * c0 :, PLANE : PLANE + cells] = jnp.zeros((pitch - 3 * c0, cells), BF16)

    for step in range(steps):
        base = step * chunk
        values = vs[:, :, base : base + chunk].reshape(c0, chunk)
        vol_ref[:, base : base + chunk] = values.astype(BF16)
        for dx in range(3):
            v3[dx * c0 : (dx + 1) * c0, base + PLANE : base + PLANE + chunk] = moved(values, grid_xy, 0, dx - 1).astype(BF16)

    def stacked(ref, base, order):
        return jnp.concatenate([ref[:, base + dz * PLANE : base + dz * PLANE + chunk] for dz in order], axis=0)

    def first_conv(base):
        z = dot(w1r[...], stacked(v3, base, (0, 1, 2)))
        total = z[c1 : 2 * c1]
        total = total + moved(z[:c1], grid_xy, -1, 0)
        total = total + moved(z[2 * c1 :], grid_xy, 1, 0)
        pre[:, base : base + chunk] = total
        hid[:, base + PLANE : base + PLANE + chunk] = (total * sigmoid(total)).astype(BF16)

    def second_conv(base):
        z = dot(w2r_ref[...], stacked(hid, base, (0, 1, 2)))
        total = None
        for dy in range(3):
            for dx in range(3):
                k = dy * 3 + dx
                term = moved(z[k * f2 : (k + 1) * f2], grid_xy, dy - 1, dx - 1)
                total = term if total is None else total + term
        s = sigmoid(total)
        feat_ref[:, base : base + chunk] = (total * s).astype(BF16)
        cot = cot_ref[:, base : base + chunk]
        delta = (cot * (s * (1.0 + total * (1.0 - s)))).astype(BF16).astype(F32)
        for dy in range(3):
            for dx in range(3):
                k = dy * 3 + dx
                d9[k * f2 : (k + 1) * f2, base + PLANE : base + PLANE + chunk] = moved(delta, grid_xy, 1 - dy, 1 - dx).astype(BF16)

    def gradients(base):
        deltas = stacked(d9, base, (2, 1, 0))
        part[:, :, base : base + chunk] = dot(w2b_ref[...], deltas).reshape(n_mp, f1, chunk)
        g = dot_nt(deltas, hid[:, base + PLANE : base + PLANE + chunk])
        acc[...] = g if base == 0 else acc[...] + g

    for step in range(steps + 2):
        if step < steps:
            first_conv(step * chunk)
        if 1 <= step <= steps:
            second_conv((step - 1) * chunk)
        if step >= 2:
            gradients((step - 2) * chunk)

    pre_ref[...] = pre[pl.ds(pl.multiple_of(me * f1, f1), f1), :]
    for k in range(n_mp):
        (give_ref if k % 2 else keep_ref)[k // 2] = part[me ^ k].astype(BF16)
    for t in range(27):
        grad_ref[:, t * c1 : (t + 1) * c1] = acc[t * f2 : (t + 1) * f2].astype(BF16)


def backward_kernel(n_mp, *refs):
    parts = refs[: n_mp // 2]
    pre_ref, vol_ref, w1b_ref, keep_ref, give_ref, grad_ref, d9, part, acc = refs[n_mp // 2 :]
    me = lax.axis_index("mp")
    f1, cells = pre_ref.shape
    c0 = vol_ref.shape[0]
    chunk = chunk_of(cells, 1)
    steps = cells // chunk
    grid_xy = lane_grid(chunk)

    zero = jnp.zeros((d9.shape[0], PLANE), BF16)
    d9[:, :PLANE] = zero
    d9[:, PLANE + cells :] = zero

    reps = max(1, 128 // c0)
    span = reps * c0

    def take(base):
        total = parts[0][:, base : base + chunk].astype(F32)
        for other in parts[1:]:
            total = total + other[:, base : base + chunk].astype(F32)
        v = pre_ref[:, base : base + chunk]
        s = sigmoid(v)
        delta = (total * (s * (1.0 + v * (1.0 - s)))).astype(BF16).astype(F32)
        shifts = [moved(delta, grid_xy, 1 - dy, 1 - dx) for dy in range(3) for dx in range(3)]
        d9[:, base + PLANE : base + PLANE + chunk] = jnp.concatenate(shifts, axis=0).astype(BF16)

    def gradients(base):
        deltas = jnp.concatenate([d9[:, base + dz * PLANE : base + dz * PLANE + chunk] for dz in (2, 1, 0)], axis=0)
        part[:, :, base : base + chunk] = dot(w1b_ref[...], deltas).reshape(n_mp, c0 // n_mp, chunk)
        vol = vol_ref[:, base : base + chunk]
        g = dot_nt(deltas, jnp.concatenate([vol] * reps, axis=0))
        acc[...] = g if base == 0 else acc[...] + g

    for step in range(steps + 1):
        if step < steps:
            take(step * chunk)
        if step >= 1:
            gradients((step - 1) * chunk)
    for k in range(n_mp):
        (give_ref if k % 2 else keep_ref)[k // 2] = part[me ^ k].astype(BF16)

    lane = lax.broadcasted_iota(jnp.int32, (1, span), 1)
    for t in range(0, 27, reps):
        merged = acc[t * f1 : (t + 1) * f1]
        for r in range(1, min(reps, 27 - t)):
            merged = jnp.where(lane >= r * c0, acc[(t + r) * f1 : (t + r + 1) * f1], merged)
        width = min(span, (27 - t) * c0)
        grad_ref[:, t * c0 : t * c0 + width] = merged[:, :width].astype(BF16)


def finish_kernel(scale, count, *refs):
    ins = refs[:count]
    first_ref, first_got_ref, second_ref, second_got_ref, feat_in_ref = refs[count : count + 5]
    feat_ref, input_ref, first_out_ref, second_out_ref = refs[count + 5 :]
    second_out_ref[...] = (second_ref[...].astype(F32) + second_got_ref[...].astype(F32)) * scale
    feat_ref[...] = feat_in_ref[...]
    first_out_ref[...] = (first_ref[...].astype(F32) + first_got_ref[...].astype(F32)) * scale
    total = ins[0][...].astype(F32)
    for other in ins[1:]:
        total = total + other[...].astype(F32)
    input_ref[...] = total.astype(BF16)


def swap(value, axis, k):
    n = lax.axis_size(axis)
    return lax.ppermute(value, axis, [(i, i ^ k) for i in range(n)])


def add(a, b):
    return (a.astype(F32) + b.astype(F32)).astype(BF16)


def sum_over_chips(keep, got):
    parts = [add(keep[j], got[j]) for j in range(keep.shape[0])]
    return [parts[0]] + [swap(parts[j], "mp", 2 * j) for j in range(1, len(parts))]


def bits_of(count):
    return [1 << i for i in reversed(range(count.bit_length() - 1))]


def call(kernel, out_shape, scratch, flops, nbytes):
    return pl.pallas_call(
        kernel,
        out_shape=out_shape,
        scratch_shapes=scratch,
        compiler_params=pltpu.CompilerParams(vmem_limit_bytes=VMEM_LIMIT),
        cost_estimate=pl.CostEstimate(flops=flops, bytes_accessed=nbytes, transcendentals=0),
    )


def local(volumes, w_first, w_second, cotangent):
    n_mp = lax.axis_size("mp")
    n_sample = lax.axis_size("sample")
    rows_in, _, cells = volumes.shape
    f1 = w_first.shape[0]
    f2 = w_second.shape[0]
    c0 = w_first.shape[1] // 27
    c1 = w_second.shape[1] // 27
    pitch = pitch_of(c0)
    scale = 1.0 / math.sqrt(n_sample * volumes.shape[1] * cells)
    volumes = volumes.reshape(rows_in, cells)
    cotangent = cotangent.reshape(f2, cells).astype(F32)
    padded = cells + 2 * PLANE

    need = (8 * 3 * c0) // 128 * 128 + pitch
    wide = max(cells, need)
    piece = jnp.concatenate(
        [
            jnp.pad(w_first, ((0, 0), (0, wide - w_first.shape[1]))),
            jnp.pad(volumes, ((0, 0), (0, wide - cells))),
        ],
        axis=0,
    )
    near = [piece] + [swap(piece, "mp", k) for k in range(2, n_mp, 2)]
    near = jnp.stack(near)
    far = swap(near, "mp", 1)

    w2t = w_second.reshape(f2, 3, 9, c1)
    w2r = jnp.transpose(w2t, (2, 0, 1, 3)).reshape(9 * f2, 3 * c1)
    w2b = jnp.transpose(w2t, (3, 1, 2, 0)).reshape(c1, 27 * f2)
    w1b = jnp.transpose(w_first.reshape(f1, 27, c0), (2, 1, 0)).reshape(c0, 27 * f1)

    sds = jax.ShapeDtypeStruct
    half = n_mp // 2
    features, pre_own, vol_all, keep, give, grad_second = call(
        functools.partial(forward_kernel, n_mp, c0),
        [
            sds((f2, cells), BF16),
            sds((f1, cells), F32),
            sds((c0, cells), BF16),
            sds((half, f1, cells), BF16),
            sds((half, f1, cells), BF16),
            sds((f2, 27 * c1), BF16),
        ],
        [
            pltpu.VMEM((n_mp, rows_in, cells), F32),
            pltpu.VMEM((n_mp, f1, wide), F32),
            pltpu.VMEM((pitch, padded), BF16),
            pltpu.VMEM((3 * c1, 3 * pitch), BF16),
            pltpu.VMEM((c1, padded), BF16),
            pltpu.VMEM((c1, cells), F32),
            pltpu.VMEM((9 * f2, padded), BF16),
            pltpu.VMEM((n_mp, f1, cells), F32),
            pltpu.VMEM((27 * f2, c1), F32),
        ],
        2 * cells * 27 * (c0 * c1 + 3 * f2 * c1),
        4 * 1024 * 1024,
    )(near, far, w2r, w2b, cotangent)

    bits = bits_of(n_sample)
    parts = sum_over_chips(keep, swap(give, "mp", 1))
    second_got = swap(grad_second, "sample", bits[0])

    keep, give, grad_first = call(
        functools.partial(backward_kernel, n_mp),
        [
            sds((half, rows_in, cells), BF16),
            sds((half, rows_in, cells), BF16),
            sds((f1, 27 * c0), BF16),
        ],
        [
            pltpu.VMEM((9 * f1, padded), BF16),
            pltpu.VMEM((n_mp, rows_in, cells), F32),
            pltpu.VMEM((27 * f1, max(1, 128 // c0) * c0), F32),
        ],
        2 * cells * 27 * 2 * c0 * f1,
        1024 * 1024,
    )(*parts, pre_own, vol_all, w1b)
    got = swap(give, "mp", 1)
    ins = sum_over_chips(keep, got)

    second_got, *_ = lax.optimization_barrier((second_got, grad_first))
    for bit in bits[:-1]:
        grad_first = add(grad_first, swap(grad_first, "sample", bit))
    first_got = swap(grad_first, "sample", bits[-1])
    for bit in bits[1:]:
        grad_second = add(grad_second, second_got)
        second_got = swap(grad_second, "sample", bit)
    features, input_grad, grad_first, grad_second = call(
        functools.partial(finish_kernel, scale, half),
        [
            sds((f2, cells), BF16),
            sds((rows_in, cells), BF16),
            sds((f1, 27 * c0), F32),
            sds((f2, 27 * c1), F32),
        ],
        [],
        0,
        2 * 1024 * 1024,
    )(*ins, grad_first, first_got, grad_second, second_got, features)
    return (
        features.reshape(f2, 1, cells),
        input_grad.reshape(rows_in, 1, cells),
        grad_first,
        grad_second,
    )


def solution(mesh):
    return jax.shard_map(
        local,
        mesh=mesh,
        in_specs=(P("mp", "sample", None), P("mp", None), P("mp", None), P("mp", "sample", None)),
        out_specs=(P("mp", "sample", None), P("mp", "sample", None), P("mp", None), P("mp", None)),
        check_vma=False,
    )
```
